32 devices in a mesh: groups: 2 (over y), seq: 4 (over z), chan: 2 (over x), sub: 2 (over core).
Axes of the slice: x: 2, y: 2, z: 4, core: 2. Of those that a mesh axis runs over, the one named last changes fastest.
Arguments:
- tokens: bfloat16 [16384, 2048], P(('groups', 'seq', 'sub'), 'chan'), parts along dimension 0, may hold values from -6 to 6
- low_angle: float32 [2048], P('chan'), may hold values from 0.1 to 1.47
- high_taps: float32 [2, 2048], P(None, 'chan'), may hold values from -3 to 3
- level_mix: float32 [17, 2048], P(None, 'chan'), may hold values from -1.5 to 1.5
- w_value: bfloat16 [2048, 2048], P(None, 'chan'), may hold values from -0.125 to 0.125
- w_gate: bfloat16 [2048, 2048], P(None, 'chan'), may hold values from -0.125 to 0.125
- out_weight: bfloat16 [2048, 2048], P(None, 'chan'), may hold values from -0.125 to 0.125
Outputs:
- result: bfloat16 [16384, 2048], P(('groups', 'seq', 'sub'), 'chan'), parts along dimension 0
The draws below stay inside these ranges and needn't reach their ends.
There are 2 independent parts, one for each index of `groups`. The reference program is written for one: setup_inputs(seed, part) draws one part's arguments, and reference() takes and returns one part's arrays. A program takes and returns all parts, laid end to end along the dimension named above; an argument that names none is the same for every part. Nothing has to cross between parts.
All inputs are finite; a program needn't handle non-finite values.
Results may differ from the reference program's by a relative error of at most 0.0043.
Values may be sent and summed in bfloat16 or wider, within the bound.
No kernel may reach another device: no remote copies, remote signals or barrier semaphores. Data moves between devices by JAX's collectives and lax.ppermute only.
A program may use at most 128 MiB of HBM per device.

```python
import jax
import jax.numpy as jnp
from jax import lax

D = 2048
LEVELS = 15
TOKENS = 8192


def level_of(key, extent, cuts, least, top_value):
    gain = 1.0
    for axis_at, blocks in cuts:
        steps = jax.random.uniform(jax.random.fold_in(jax.random.fold_in(key, 6), axis_at), (blocks,), jnp.float32, least / len(cuts), top_value / len(cuts))
        gain = gain * jnp.repeat(jnp.exp(steps), extent[axis_at] // blocks).reshape((-1,) + (1,) * (len(extent) - 1 - axis_at))
    return gain


def noise(own_key, dims, scale, most, cuts=(), dtype=jnp.bfloat16):
    drawn = scale * jax.random.normal(own_key, dims, jnp.float32)
    if cuts:
        drawn = drawn * level_of(own_key, dims, cuts, -0.22, 0.18)
    return jnp.clip(drawn, -most, most).astype(dtype)


def setup_inputs(seed: int = 0, part: int = 0) -> dict:
    keys = jax.random.split(jax.random.key(seed), 8)
    part_splits = jax.random.split(jax.random.fold_in(keys[7], part), 8)
    return {
        "tokens": noise(part_splits[0], (TOKENS, D), 1.0, 6.0, ((0, 8), (1, 2))),
        "low_angle": jnp.clip(0.1 + 1.37 * jax.random.uniform(keys[1], (D,), jnp.float32) ** level_of(keys[1], (D,), ((0, 2),), -0.2, 0.2), 0.1, 1.47),
        "high_taps": noise(keys[2], (2, D), 0.7, 3.0, ((1, 2),), jnp.float32),
        "level_mix": noise(keys[3], (LEVELS + 2, D), (LEVELS + 2) ** -0.5, 1.5, ((1, 2),), jnp.float32),
        "w_value": noise(keys[4], (D, D), D ** -0.5, 0.125, ((1, 2),)),
        "w_gate": noise(keys[5], (D, D), D ** -0.5, 0.125, ((1, 2),)),
        "out_weight": noise(keys[6], (D, D), D ** -0.5, 0.125, ((1, 2),)),
    }


def filter_block(inputs):
    block, angle, high_pair, mix = inputs
    low0 = jnp.cos(angle)
    low1 = jnp.sin(angle)
    stream = block.astype(jnp.float32)
    length = stream.shape[0]
    mixed = mix[LEVELS + 1] * stream
    for level in range(LEVELS):
        reach = 2 ** level
        if reach < length:
            shifted = jnp.concatenate([jnp.zeros((reach, stream.shape[1]), jnp.float32), stream[:length - reach]], 0)
        else:
            shifted = jnp.zeros_like(stream)
        high = high_pair[0] * stream + high_pair[1] * shifted
        stream = low0 * stream + low1 * shifted
        mixed = mixed + mix[level] * high
    mixed = mixed + mix[LEVELS] * stream
    return jax.nn.gelu(mixed).astype(jnp.bfloat16)


def reference(tokens, low_angle, high_taps, level_mix, w_value, w_gate, out_weight):
    length = tokens.shape[0]
    width = tokens.shape[1]
    blocks = width // 256
    tok_blocks = tokens.reshape(length, blocks, 256).transpose(1, 0, 2)
    angle_blocks = low_angle.reshape(blocks, 256)
    high_blocks = high_taps.reshape(2, blocks, 256).transpose(1, 0, 2)
    mix_blocks = level_mix.reshape(LEVELS + 2, blocks, 256).transpose(1, 0, 2)
    activated = lax.map(filter_block, (tok_blocks, angle_blocks, high_blocks, mix_blocks))
    activated = activated.transpose(1, 0, 2).reshape(length, width)
    value = jnp.dot(activated, w_value, preferred_element_type=jnp.float32)
    gate = jnp.dot(activated, w_gate, preferred_element_type=jnp.float32)
    hidden = (value * jax.nn.sigmoid(gate)).astype(jnp.bfloat16)
    outcome = jnp.dot(hidden, out_weight, preferred_element_type=jnp.float32) + tokens.astype(jnp.float32)
    return outcome.astype(jnp.bfloat16)
```

```python
import functools

import jax
import jax.numpy as jnp
from jax import lax
from jax.experimental import pallas as pl
from jax.experimental.pallas import tpu as pltpu
from jax.sharding import PartitionSpec as P

LEVELS = 15
LANES = 128
RUN = 16
MIDDLE = 8
WIDE = 64
LINE = ("seq", "sub")
MIB = 2**20


def run_levels(stream, shifter, low0, low1, high0, high1, mix):
    mixed = mix[LEVELS + 1] * stream
    for level in range(LEVELS):
        shifted = shifter(stream, 2**level)
        high = high0 * stream + high1 * shifted
        stream = low0 * stream + low1 * shifted
        mixed = mixed + mix[level] * high
    return mixed + mix[LEVELS] * stream


def general(tokens, low_angle, high_taps, level_mix, w_value, w_gate, out_weight):
    rows = tokens.shape[0]
    channels = tokens.shape[1]
    ways = lax.axis_size(LINE)
    total = rows * ways
    narrow = channels // ways
    place = lax.axis_index(LINE) * narrow
    columns = lax.all_to_all(tokens.T, LINE, split_axis=0, concat_axis=1, tiled=True)
    angle = lax.dynamic_slice_in_dim(low_angle, place, narrow, 0)[:, None]
    high_pair = lax.dynamic_slice_in_dim(high_taps, place, narrow, 1)[:, :, None]
    mix = lax.dynamic_slice_in_dim(level_mix, place, narrow, 1)[:, :, None]

    def shifter(stream, reach):
        if reach >= total:
            return jnp.zeros_like(stream)
        return jnp.concatenate(
            [jnp.zeros((stream.shape[0], reach), jnp.float32), stream[:, : total - reach]], 1
        )

    mixed = run_levels(
        columns.astype(jnp.float32),
        shifter,
        jnp.cos(angle),
        jnp.sin(angle),
        high_pair[0],
        high_pair[1],
        mix,
    )
    filtered = jax.nn.gelu(mixed).astype(jnp.bfloat16)
    activated = lax.all_to_all(filtered, LINE, split_axis=1, concat_axis=0, tiled=True).T
    piece = lax.all_gather(activated, "chan", axis=1, tiled=True)
    value = jnp.dot(piece, w_value, preferred_element_type=jnp.float32)
    gate = jnp.dot(piece, w_gate, preferred_element_type=jnp.float32)
    hidden = (value * jax.nn.sigmoid(gate)).astype(jnp.bfloat16)
    projected = jnp.dot(
        lax.all_gather(hidden, "chan", axis=1, tiled=True),
        out_weight,
        preferred_element_type=jnp.float32,
    )
    return (projected + tokens.astype(jnp.float32)).astype(jnp.bfloat16)


def coefficients(angle, high, mix, live):
    low0, low1 = jnp.cos(angle), jnp.sin(angle)
    rows = []
    for level in range(live + 1):
        weight = jnp.zeros_like(angle)
        if level < live:
            weight = weight + mix[level] * (high[0] - high[1] * low0 / low1)
        if level > 0:
            weight = weight + mix[level - 1] * high[1] / low1
        if level == live:
            for rest in range(live, LEVELS):
                weight = weight + mix[rest] * high[0] * low0 ** (rest - live)
            weight = weight + mix[LEVELS] * low0 ** (LEVELS - live)
        weight = weight * low0**level
        if level == 0:
            weight = weight + mix[LEVELS + 1]
        rows.append(weight)
    rows.append(low1 / low0)
    return jnp.stack(rows)


def advance(stream, tail, ratio):
    reach = tail.shape[0]
    shifted = jnp.concatenate([tail, stream[: stream.shape[0] - reach]], 0)
    return stream + ratio * shifted


def levels_kernel(live, ways, place, coef_ref, *refs):
    pieces = refs[:ways]
    far = refs[ways : 2 * ways]
    near = refs[2 * ways : 3 * ways]
    tokens, stream_ref, mixed_ref, act_ref = refs[3 * ways :]
    rows = pieces[0].shape[0]
    units = rows * ways // 8
    for at in range(ways):
        tokens[pl.ds(pl.multiple_of(place[at] * rows, rows), rows), :] = pieces[at][...]

    def whole(row):
        return jnp.broadcast_to(coef_ref[row : row + 1, :], (8, LANES))[None]

    def zero(n):
        return jnp.zeros((n, 8, LANES), jnp.float32)

    ratio = whole(live + 1)

    def first(i, carry):
        start = pl.multiple_of(i * RUN * 8, RUN * 8)
        x = tokens[pl.ds(start, RUN * 8), :].astype(jnp.float32).reshape(RUN, 8, LANES)
        mixed = whole(0) * x
        row = lax.broadcasted_iota(jnp.int32, (1, 8, LANES), 1)
        kept = []
        for level, tail in enumerate(carry):
            kept.append(x[RUN - tail.shape[0] :])
            if level < 3:
                turned = pltpu.roll(jnp.concatenate([tail, x], 0), 2**level, 1)
                x = x + ratio * jnp.where(row < 2**level, turned[:RUN], turned[1:])
            else:
                x = advance(x, tail, ratio)
            mixed = mixed + whole(level + 1) * x
        stream_ref[pl.ds(i * RUN, RUN)] = x
        mixed_ref[pl.ds(i * RUN, RUN)] = mixed
        return tuple(kept)

    lax.fori_loop(0, units // RUN, first, tuple(zero(n) for n in (1, 1, 1, 1, 2, 4)))

    stream = stream_ref.reshape(units // MIDDLE, MIDDLE, 8, LANES)
    total = mixed_ref.reshape(units // MIDDLE, MIDDLE, 8, LANES)
    steps = units // MIDDLE // RUN

    def second(t, carry):
        q = t // steps
        i = t % steps
        x = stream[pl.ds(i * RUN, RUN), q]
        mixed = total[pl.ds(i * RUN, RUN), q]
        keep = jnp.where(i > 0, 1.0, 0.0)
        kept = []
        for level, tail in enumerate(carry):
            kept.append(x[RUN - tail.shape[0] :])
            x = advance(x, tail * keep, ratio)
            mixed = mixed + whole(level + 7) * x
        stream[pl.ds(i * RUN, RUN), q] = x
        total[pl.ds(i * RUN, RUN), q] = mixed
        return tuple(kept)

    lax.fori_loop(0, MIDDLE * steps, second, tuple(zero(n) for n in (1, 2, 4)))

    stream_wide = stream_ref.reshape(units // WIDE, WIDE, 8, LANES)
    total_wide = mixed_ref.reshape(units // WIDE, WIDE, 8, LANES)
    act_wide = act_ref.reshape(units // WIDE, WIDE // 2, 16, LANES)

    def third(pair, _):
        halves = []
        for odd in range(2):
            x = stream_wide[:, pair * 2 + odd]
            mixed = total_wide[:, pair * 2 + odd]
            for level in range(9, live):
                x = advance(x, zero(2 ** (level - 9)), ratio)
                mixed = mixed + whole(level + 1) * x
            halves.append(jax.nn.gelu(mixed))
        act_wide[:, pair] = jnp.concatenate(halves, 1).astype(jnp.bfloat16)
        return 0

    lax.fori_loop(0, WIDE // 2, third, 0)

    half = rows // 2
    side = place[2 * ways]
    for at in range(ways):
        start = place[ways + at] * rows
        far[at][...] = act_ref[pl.ds(pl.multiple_of(start + (1 - side) * half, half), half), :]
        near[at][...] = act_ref[pl.ds(pl.multiple_of(start + side * half, half), half), :]


def run_filter(place, coef, pieces, live):
    ways = len(pieces)
    rows = pieces[0].shape[0]
    total = rows * ways
    in_vmem = pl.BlockSpec(memory_space=pltpu.VMEM)
    return pl.pallas_call(
        functools.partial(levels_kernel, live, ways),
        out_shape=[jax.ShapeDtypeStruct((rows // 2, LANES), jnp.bfloat16)] * (2 * ways),
        in_specs=[pl.BlockSpec(memory_space=pltpu.SMEM)] + [in_vmem] * (ways + 1),
        out_specs=[in_vmem] * (2 * ways),
        scratch_shapes=[
            pltpu.VMEM((total, LANES), jnp.bfloat16),
            pltpu.VMEM((total // 8, 8, LANES), jnp.float32),
            pltpu.VMEM((total // 8, 8, LANES), jnp.float32),
            pltpu.VMEM((total, LANES), jnp.bfloat16),
        ],
        compiler_params=pltpu.CompilerParams(vmem_limit_bytes=40 * MIB),
        name="levels",
    )(place, coef, *pieces)


def project_kernel(ways, parts, steps, place, *refs):
    near = refs[:ways]
    far = refs[ways]
    value_own, gate_own = refs[ways + 1 : ways + 3]
    at = ways + 3
    value_far = refs[at : at + parts]
    gate_far = refs[at + parts : at + 2 * parts]
    out_far = refs[at + 2 * parts : at + 3 * parts]
    hidden_ref, sent_ref, act, hid = refs[at + 3 * parts :]
    step = pl.program_id(0)
    side = place[2 * ways]
    depth = value_far[0].shape[0]
    block = value_own.shape[1]
    channels = ways * LANES

    @pl.when(step == 0)
    def _():
        for s in range(ways):
            own = side * channels + place[s] * LANES
            other = (1 - side) * channels + place[s] * LANES
            act[:, pl.ds(pl.multiple_of(own, LANES), LANES)] = near[s][...]
            act[:, pl.ds(pl.multiple_of(other, LANES), LANES)] = far[s]

    def dot(a, b):
        return jnp.dot(a, b, preferred_element_type=jnp.float32)

    def put(value, gate, start):
        done = (value * jax.nn.sigmoid(gate)).astype(jnp.bfloat16)
        hid[:, pl.ds(pl.multiple_of(start, block), block)] = done

    def spread(source, weights):
        total = None
        for p in range(parts):
            start = pl.multiple_of(place[2 * ways + 1 + p] * depth, depth)
            term = dot(source[:, pl.ds(start, depth)], weights[p][...])
            total = term if total is None else total + term
        return total

    @pl.when(step < steps)
    def _():
        put(
            dot(act[...], value_own[...]),
            dot(act[...], gate_own[...]),
            side * channels + step * block,
        )

    @pl.when((step >= steps) & (step < 2 * steps))
    def _():
        put(
            spread(act, value_far),
            spread(act, gate_far),
            (1 - side) * channels + (step - steps) * block,
        )

    @pl.when(step >= 2 * steps)
    def _():
        sent_ref[...] = spread(hid, out_far).astype(jnp.bfloat16)

    @pl.when(step == 3 * steps - 1)
    def _():
        hidden_ref[...] = hid[...]


def run_project(place, near, far, value_own, gate_own, value_far, gate_far, out_far):
    ways = len(near)
    parts = len(value_far)
    rows = near[0].shape[0]
    depth, channels = value_far[0].shape
    width = value_own.shape[0]
    block = min(256, channels)
    steps = channels // block

    def fixed(shape):
        return pl.BlockSpec(shape, lambda j: (0,) * len(shape))

    def column(height, offset):
        return pl.BlockSpec((height, block), lambda j: (0, jnp.clip(j - offset, 0, steps - 1)))

    return pl.pallas_call(
        functools.partial(project_kernel, ways, parts, steps),
        grid=(3 * steps,),
        out_shape=[
            jax.ShapeDtypeStruct((rows, width), jnp.bfloat16),
            jax.ShapeDtypeStruct((rows, channels), jnp.bfloat16),
        ],
        in_specs=[pl.BlockSpec(memory_space=pltpu.SMEM)]
        + [fixed((rows, LANES))] * ways
        + [fixed((ways, rows, LANES))]
        + [column(width, 0)] * 2
        + [column(depth, steps)] * (2 * parts)
        + [column(depth, 2 * steps)] * parts,
        out_specs=[fixed((rows, width)), column(rows, 2 * steps)],
        scratch_shapes=[
            pltpu.VMEM((rows, width), jnp.bfloat16),
            pltpu.VMEM((rows, width), jnp.bfloat16),
        ],
        compiler_params=pltpu.CompilerParams(vmem_limit_bytes=40 * MIB),
        name="project",
    )(place, *near, far, value_own, gate_own, *value_far, *gate_far, *out_far)


def finish_kernel(side, hidden, weight, tokens, out_ref):
    made = jnp.dot(hidden[...], weight[...], preferred_element_type=jnp.float32)
    out_ref[...] = (made + tokens[...].astype(jnp.float32)).astype(jnp.bfloat16)


def run_finish(side, hidden, weight, tokens):
    rows, width = hidden.shape
    channels = weight.shape[1]
    block = min(256, channels)
    return pl.pallas_call(
        finish_kernel,
        grid_spec=pltpu.PrefetchScalarGridSpec(
            num_scalar_prefetch=1,
            grid=(channels // block,),
            in_specs=[
                pl.BlockSpec((rows, width), lambda j, side: (0, 0)),
                pl.BlockSpec((width, block), lambda j, side: (0, j)),
                pl.BlockSpec((rows, block), lambda j, side: (side[0], j)),
            ],
            out_specs=pl.BlockSpec((rows, block), lambda j, side: (side[0], j)),
        ),
        out_shape=jax.ShapeDtypeStruct(tokens.shape, jnp.bfloat16),
        compiler_params=pltpu.CompilerParams(vmem_limit_bytes=40 * MIB),
        name="finish",
    )(side, hidden, weight, tokens)


def add_kernel(side, got, tokens, kept, out_ref):
    out_ref[...] = (got[...].astype(jnp.float32) + tokens[...].astype(jnp.float32)).astype(
        jnp.bfloat16
    )


def add_far(side, got, tokens, result):
    rows, channels = got.shape
    block = rows // 2
    return pl.pallas_call(
        add_kernel,
        grid_spec=pltpu.PrefetchScalarGridSpec(
            num_scalar_prefetch=1,
            grid=(2,),
            in_specs=[
                pl.BlockSpec((block, channels), lambda j, side: (j, 0)),
                pl.BlockSpec((block, channels), lambda j, side: (2 * (1 - side[0]) + j, 0)),
                pl.BlockSpec(memory_space=pl.ANY),
            ],
            out_specs=pl.BlockSpec((block, channels), lambda j, side: (2 * (1 - side[0]) + j, 0)),
        ),
        out_shape=jax.ShapeDtypeStruct(tokens.shape, jnp.bfloat16),
        input_output_aliases={3: 0},
        name="add_far",
    )(side, got, tokens, result)


def swap(array, axis):
    return lax.ppermute(array, axis, [(0, 1), (1, 0)])


def around(array, offset):
    ways = lax.axis_size(LINE)
    return lax.ppermute(array, LINE, [(j, (j + offset) % ways) for j in range(ways)])


def by_tokens(tokens, low_angle, high_taps, level_mix, w_value, w_gate, out_weight):
    rows, channels = tokens.shape
    ways = lax.axis_size(LINE)
    narrow = channels // ways
    here = lax.axis_index(LINE)
    group = lax.axis_index("groups")
    core = lax.axis_index("sub")
    side = lax.axis_index("chan")
    live = min(LEVELS, (rows * ways - 1).bit_length())
    order = sorted(range(1, ways), key=lambda s: abs(2 * s - ways))

    sources = [(here - s) % ways for s in range(ways)]
    targets = [(here + s) % ways for s in range(ways)]
    quarter = [
        2 * group + core,
        2 * (1 - group) + core,
        2 * group + 1 - core,
        2 * (1 - group) + 1 - core,
    ]
    place = jnp.stack(sources + targets + [side] + quarter).astype(jnp.int32)

    def columns(s):
        return lax.dynamic_slice_in_dim(tokens, targets[s] * narrow, narrow, 1)

    pieces = [None] * ways
    for s in order:
        pieces[s] = around(columns(s), s)
    pieces[0] = columns(0)

    depth = w_value.shape[0] // 4

    def fetch(weight):
        first = swap(lax.dynamic_slice_in_dim(weight, quarter[0] * depth, depth, 0), "chan")
        second = swap(first, "groups")
        return [first, second, swap(first, "sub"), swap(second, "sub")]

    value_far, gate_far, out_far = fetch(w_value), fetch(w_gate), fetch(out_weight)

    start = here * narrow
    coef = coefficients(
        lax.dynamic_slice_in_dim(low_angle, start, narrow, 0),
        lax.dynamic_slice_in_dim(high_taps, start, narrow, 1),
        lax.dynamic_slice_in_dim(level_mix, start, narrow, 1),
        live,
    )
    outs = run_filter(place, coef, pieces, live)
    far_out, near_out = outs[:ways], outs[ways:]

    far = [far_out[0]] + [None] * (ways - 1)
    near = [near_out[0]] + [None] * (ways - 1)
    for s in order:
        far[s] = around(far_out[s], s)
    for s in order:
        near[s] = around(near_out[s], s)
    got = swap(jnp.stack(far), "chan")
    hidden, sent = run_project(
        place, near, got, w_value, w_gate, value_far, gate_far, out_far
    )
    returned = swap(sent, "chan")
    which = side.astype(jnp.int32)[None]
    result = run_finish(which, hidden, out_weight, tokens)
    return add_far(which, returned, tokens, result)


def solution(mesh):
    def shards(tokens, *rest):
        ways = mesh.shape["seq"] * mesh.shape["sub"]
        pairs = all(mesh.shape[name] == 2 for name in ("groups", "chan", "sub"))
        rows, channels = tokens.shape
        fits = channels == ways * LANES and rows % 64 == 0
        fits = fits and rows * ways == 8 * WIDE * RUN and rest[3].shape[0] % 512 == 0
        return (by_tokens if pairs and fits else general)(tokens, *rest)

    return jax.shard_map(
        shards,
        mesh=mesh,
        in_specs=(
            P(("groups", "seq", "sub"), "chan"),
            P("chan"),
            P(None, "chan"),
            P(None, "chan"),
            P(None, "chan"),
            P(None, "chan"),
            P(None, "chan"),
        ),
        out_specs=P(("groups", "seq", "sub"), "chan"),
        check_vma=False,
    )
```

```python
import functools

import jax
import jax.numpy as jnp
from jax import lax
from jax.experimental import pallas as pl
from jax.experimental.pallas import tpu as pltpu
from jax.sharding import PartitionSpec as P

LEVELS = 15
LANES = 128
PARTS = 4
SPLIT = 2
RUN = 16
MIDDLE = 8
WIDE = 64
LINE = ("seq", "sub")
GRANT = 56 * 2**20


def run_levels(stream, shifter, low0, low1, high0, high1, mix):
    mixed = mix[LEVELS + 1] * stream
    for level in range(LEVELS):
        shifted = shifter(stream, 2**level)
        high = high0 * stream + high1 * shifted
        stream = low0 * stream + low1 * shifted
        mixed = mixed + mix[level] * high
    return mixed + mix[LEVELS] * stream


def general(tokens, low_angle, high_taps, level_mix, w_value, w_gate, out_weight):
    rows = tokens.shape[0]
    channels = tokens.shape[1]
    ways = lax.axis_size(LINE)
    total = rows * ways
    narrow = channels // ways
    place = lax.axis_index(LINE) * narrow
    columns = lax.all_to_all(tokens.T, LINE, split_axis=0, concat_axis=1, tiled=True)
    angle = lax.dynamic_slice_in_dim(low_angle, place, narrow, 0)[:, None]
    high_pair = lax.dynamic_slice_in_dim(high_taps, place, narrow, 1)[:, :, None]
    mix = lax.dynamic_slice_in_dim(level_mix, place, narrow, 1)[:, :, None]

    def shifter(stream, reach):
        if reach >= total:
            return jnp.zeros_like(stream)
        return jnp.concatenate(
            [jnp.zeros((stream.shape[0], reach), jnp.float32), stream[:, : total - reach]], 1
        )

    mixed = run_levels(
        columns.astype(jnp.float32),
        shifter,
        jnp.cos(angle),
        jnp.sin(angle),
        high_pair[0],
        high_pair[1],
        mix,
    )
    filtered = jax.nn.gelu(mixed).astype(jnp.bfloat16)
    activated = lax.all_to_all(filtered, LINE, split_axis=1, concat_axis=0, tiled=True).T
    piece = lax.all_gather(activated, "chan", axis=1, tiled=True)
    value = jnp.dot(piece, w_value, preferred_element_type=jnp.float32)
    gate = jnp.dot(piece, w_gate, preferred_element_type=jnp.float32)
    hidden = (value * jax.nn.sigmoid(gate)).astype(jnp.bfloat16)
    projected = jnp.dot(
        lax.all_gather(hidden, "chan", axis=1, tiled=True),
        out_weight,
        preferred_element_type=jnp.float32,
    )
    return (projected + tokens.astype(jnp.float32)).astype(jnp.bfloat16)


def coefficients_kernel(live, place, angle_ref, high_ref, mix_ref, out_ref):
    lanes = pl.ds(pl.multiple_of(line_of(place, 0, 0) * LANES, LANES), LANES)
    low0, low1 = jnp.cos(angle_ref[:, lanes]), jnp.sin(angle_ref[:, lanes])
    high0, high1 = high_ref[0:1, lanes], high_ref[1:2, lanes]
    power = jnp.ones_like(low0)
    for level in range(live + 1):
        weight = jnp.zeros_like(low0)
        if level < live:
            weight = weight + mix_ref[level : level + 1, lanes] * (high0 - high1 * low0 / low1)
        if level > 0:
            weight = weight + mix_ref[level - 1 : level, lanes] * high1 / low1
        if level == live:
            scale = jnp.ones_like(low0)
            for rest in range(live, LEVELS):
                weight = weight + mix_ref[rest : rest + 1, lanes] * high0 * scale
                scale = scale * low0
            weight = weight + mix_ref[LEVELS : LEVELS + 1, lanes] * scale
        weight = weight * power
        if level == 0:
            weight = weight + mix_ref[LEVELS + 1 : LEVELS + 2, lanes]
        out_ref[level : level + 1, :] = weight
        power = power * low0
    out_ref[live + 1 : live + 2, :] = low1 / low0


def run_coefficients(place, angle, high, mix, live):
    return pl.pallas_call(
        functools.partial(coefficients_kernel, live),
        in_specs=[pl.BlockSpec(memory_space=pltpu.SMEM)]
        + [pl.BlockSpec(memory_space=pltpu.VMEM)] * 3,
        out_specs=pl.BlockSpec(memory_space=pltpu.VMEM),
        out_shape=jax.ShapeDtypeStruct((live + 2, LANES), jnp.float32),
        cost_estimate=pl.CostEstimate(flops=10**11, bytes_accessed=0, transcendentals=0),
        name="coefficients",
    )(place, angle[None], high, mix)


def advance(stream, tail, ratio):
    reach = tail.shape[0]
    shifted = jnp.concatenate([tail, stream[: stream.shape[0] - reach]], 0)
    return stream + ratio * shifted


def copy_all(pairs, sems):
    copies = [pltpu.make_async_copy(*pair, sems.at[at]) for at, pair in enumerate(pairs)]
    for copy in copies:
        copy.start()
    for copy in copies:
        copy.wait()


def line_of(place, back, other):
    chips = place[4]
    core = 1 - place[1] if other else place[1]
    return lax.rem(place[0] - back + chips, chips) * 2 + core


def cut_kernel(chips, place, tokens, *outs):
    for ahead in range(chips):
        for other in range(2):
            if ahead or other:
                start = pl.multiple_of(line_of(place, -ahead, other) * LANES, LANES)
                block = tokens[:, pl.ds(start, LANES)]
                if ahead:
                    outs[ahead][other] = block
                else:
                    outs[0][...] = block


def run_cut(place, tokens, chips):
    rows = tokens.shape[0]
    shapes = [(rows, LANES)] + [(2, rows, LANES)] * (chips - 1)
    return pl.pallas_call(
        functools.partial(cut_kernel, chips),
        in_specs=[
            pl.BlockSpec(memory_space=pltpu.SMEM),
            pl.BlockSpec(memory_space=pltpu.VMEM),
        ],
        out_specs=[pl.BlockSpec(memory_space=pltpu.VMEM)] * chips,
        out_shape=[jax.ShapeDtypeStruct(shape, tokens.dtype) for shape in shapes],
        name="cut",
    )(place, tokens)


def piece_kernel(place, *refs):
    count = (len(refs) - 1) // 2
    depth = refs[count].shape[0]
    part = depth // PARTS
    start = (2 * place[3] + place[1]) * depth
    pairs = []
    for at in range(count):
        for p in range(PARTS):
            rows = pl.ds(pl.multiple_of(start + p * part, part), part)
            pairs.append((refs[at].at[rows], refs[count + at].at[pl.ds(p * part, part)]))
    copy_all(pairs, refs[-1])


def run_pieces(place, weights):
    rows, channels = weights[0].shape
    count = len(weights)
    return pl.pallas_call(
        piece_kernel,
        in_specs=[pl.BlockSpec(memory_space=pltpu.SMEM)]
        + [pl.BlockSpec(memory_space=pl.ANY)] * count,
        out_specs=[pl.BlockSpec(memory_space=pltpu.VMEM)] * count,
        out_shape=[jax.ShapeDtypeStruct((rows // 4, channels), w.dtype) for w in weights],
        scratch_shapes=[pltpu.SemaphoreType.DMA((count * PARTS,))],
        name="pieces",
    )(place, *weights)


def levels_kernel(live, chips, place, coef_ref, own, *refs):
    direct = refs[: chips - 1]
    handed = refs[chips - 1 : 2 * chips - 1]
    far = refs[2 * chips - 1 : 3 * chips - 1]
    near = refs[3 * chips - 1 : 4 * chips - 1]
    tokens, stream_ref, mixed_ref, act_ref, sems = refs[4 * chips - 1 :]
    side = place[2]
    rows = own.shape[0]
    units = rows * 2 * chips // 8

    def block(line):
        return pl.ds(pl.multiple_of(line * rows, rows), rows)

    pairs = []
    for back in range(chips):
        columns = pl.ds(pl.multiple_of(line_of(place, 0, 0) * LANES, LANES), LANES)
        mine = direct[back - 1].at[0] if back else own.at[:, columns]
        pairs.append((mine, tokens.at[block(line_of(place, back, 0))]))
        pairs.append((handed[back], tokens.at[block(line_of(place, back, 1))]))
    copy_all(pairs, sems)

    def whole(row):
        return jnp.broadcast_to(coef_ref[row : row + 1, :], (8, LANES))[None]

    def zero(n):
        return jnp.zeros((n, 8, LANES), jnp.float32)

    ratio = whole(live + 1)

    def first(i, carry):
        start = pl.multiple_of(i * RUN * 8, RUN * 8)
        x = tokens[pl.ds(start, RUN * 8), :].astype(jnp.float32).reshape(RUN, 8, LANES)
        mixed = whole(0) * x
        row = lax.broadcasted_iota(jnp.int32, (1, 8, LANES), 1)
        kept = []
        for level, tail in enumerate(carry):
            kept.append(x[RUN - tail.shape[0] :])
            if level < 3:
                turned = pltpu.roll(jnp.concatenate([tail, x], 0), 2**level, 1)
                x = x + ratio * jnp.where(row < 2**level, turned[:RUN], turned[1:])
            else:
                x = advance(x, tail, ratio)
            mixed = mixed + whole(level + 1) * x
        stream_ref[pl.ds(i * RUN, RUN)] = x
        mixed_ref[pl.ds(i * RUN, RUN)] = mixed
        return tuple(kept)

    lax.fori_loop(0, units // RUN, first, tuple(zero(n) for n in (1, 1, 1, 1, 2, 4)))

    stream = stream_ref.reshape(units // MIDDLE, MIDDLE, 8, LANES)
    total = mixed_ref.reshape(units // MIDDLE, MIDDLE, 8, LANES)
    steps = units // MIDDLE // RUN

    def second(t, carry):
        q = t // steps
        i = t % steps
        x = stream[pl.ds(i * RUN, RUN), q]
        mixed = total[pl.ds(i * RUN, RUN), q]
        keep = jnp.where(i > 0, 1.0, 0.0)
        kept = []
        for level, tail in enumerate(carry):
            kept.append(x[RUN - tail.shape[0] :])
            x = advance(x, tail * keep, ratio)
            mixed = mixed + whole(level + 7) * x
        stream[pl.ds(i * RUN, RUN), q] = x
        total[pl.ds(i * RUN, RUN), q] = mixed
        return tuple(kept)

    lax.fori_loop(0, MIDDLE * steps, second, tuple(zero(n) for n in (1, 2, 4)))

    stream_wide = stream_ref.reshape(units // WIDE, WIDE, 8, LANES)
    total_wide = mixed_ref.reshape(units // WIDE, WIDE, 8, LANES)
    act_wide = act_ref.reshape(units // WIDE, WIDE // 2, 16, LANES)

    def third(pair, _):
        halves = []
        for odd in range(2):
            x = stream_wide[:, pair * 2 + odd]
            mixed = total_wide[:, pair * 2 + odd]
            for level in range(9, live):
                x = advance(x, zero(2 ** (level - 9)), ratio)
                mixed = mixed + whole(level + 1) * x
            halves.append(jax.nn.gelu(mixed))
        act_wide[:, pair] = jnp.concatenate(halves, 1).astype(jnp.bfloat16)
        return 0

    lax.fori_loop(0, WIDE // 2, third, 0)

    half = rows // 2
    pairs = []
    for ahead in range(chips):
        for other in range(2):
            start = line_of(place, -ahead, other) * rows
            for outs, which in ((far, 1 - side), (near, side)):
                begin = pl.multiple_of(start + which * half, half)
                pairs.append((act_ref.at[pl.ds(begin, half)], outs[ahead].at[other]))
    copy_all(pairs, sems)


def run_filter(place, coef, own, direct, handed, live):
    chips = len(handed)
    rows = handed[0].shape[0]
    total = rows * 2 * chips
    anywhere = pl.BlockSpec(memory_space=pltpu.HBM)
    outs = pl.pallas_call(
        functools.partial(levels_kernel, live, chips),
        out_shape=[jax.ShapeDtypeStruct((2, rows // 2, LANES), jnp.bfloat16)] * (2 * chips),
        in_specs=[
            pl.BlockSpec(memory_space=pltpu.SMEM),
            pl.BlockSpec(memory_space=pltpu.VMEM),
        ]
        + [anywhere] * (2 * chips),
        out_specs=[anywhere] * (2 * chips),
        scratch_shapes=[
            pltpu.VMEM((total, LANES), jnp.bfloat16),
            pltpu.VMEM((total // 8, 8, LANES), jnp.float32),
            pltpu.VMEM((total // 8, 8, LANES), jnp.float32),
            pltpu.VMEM((total, LANES), jnp.bfloat16),
            pltpu.SemaphoreType.DMA((4 * chips,)),
        ],
        compiler_params=pltpu.CompilerParams(vmem_limit_bytes=GRANT),
        name="levels",
    )(place, coef, own, *direct, *handed)
    return list(outs[:chips]), list(outs[chips:])


def work(rows, depth, columns):
    return pl.CostEstimate(
        flops=2 * rows * depth * columns,
        bytes_accessed=2 * (rows * depth + depth * columns + rows * columns),
        transcendentals=0,
    )


def dot(a, b):
    return jnp.dot(a, b, preferred_element_type=jnp.float32)


def spread(place, source, pieces):
    core, group = place[1], place[3]
    depth = pieces[0].shape[0]
    total = None
    for piece, far_group, far_core in zip(pieces, (0, 1, 0, 1), (0, 0, 1, 1)):
        quarter = 2 * (1 - group if far_group else group) + (1 - core if far_core else core)
        rows = pl.ds(pl.multiple_of(quarter * depth, depth), depth)
        term = dot(source[:, rows], piece[...])
        total = term if total is None else total + term
    return total


def hidden_kernel(rounds, steps, place, *refs):
    chips = sum(len(backs) for backs in rounds)
    direct = refs[:chips]
    handed, early, early_twin, late, late_twin, value_own, gate_own = refs[chips : chips + 7]
    value_far, gate_far = refs[chips + 7], refs[chips + 8 : chips + 12]
    hidden_ref, act, sems = refs[chips + 12 :]
    step = pl.program_id(0)
    side = place[2]
    channels = 2 * chips * LANES

    @pl.when(step == 0)
    def _():
        pairs = []
        for backs, mine, twin in zip(rounds, (early, late), (early_twin, late_twin)):
            for at, back in enumerate(backs):
                for other, near, far in ((0, direct[back].at[0], mine), (1, handed.at[back], twin)):
                    line = line_of(place, back, other) * LANES
                    for start, block in (
                        (side * channels + line, near),
                        ((1 - side) * channels + line, far.at[at]),
                    ):
                        lanes = pl.ds(pl.multiple_of(start, LANES), LANES)
                        pairs.append((block, act.at[:, lanes]))
        copy_all(pairs, sems)

    def put(value, gate):
        hidden_ref[...] = (value * jax.nn.sigmoid(gate)).astype(jnp.bfloat16)

    @pl.when(step < steps)
    def _():
        put(dot(act[...], value_own[...]), dot(act[...], gate_own[...]))

    @pl.when(step >= steps)
    def _():
        put(dot(act[...], value_far[...]), spread(place, act, gate_far))


def run_hidden(place, rounds, direct, handed, early, late, value_own, gate_own, value_far, gate_far):
    chips = len(direct)
    rows = handed.shape[1]
    width, channels = value_own.shape
    depth = gate_far[0].shape[0]
    block = min(512, channels)
    steps = channels // block

    def first(j):
        return jnp.minimum(j, steps - 1)

    def last(j):
        return jnp.maximum(j - steps, 0)

    def spot(j, place):
        side = place[2]
        return (0, jnp.where(j < steps, side * steps + j, (1 - side) * steps + j - steps))

    return pl.pallas_call(
        functools.partial(hidden_kernel, rounds, steps),
        grid_spec=pltpu.PrefetchScalarGridSpec(
            num_scalar_prefetch=1,
            grid=(2 * steps,),
            in_specs=[pl.BlockSpec(memory_space=pltpu.HBM)] * (chips + 5)
            + [pl.BlockSpec((width, block), lambda j, place: (0, first(j)))] * 2
            + [pl.BlockSpec((width, block), lambda j, place: (0, last(j)))]
            + [pl.BlockSpec((depth, block), lambda j, place: (0, last(j)))] * len(gate_far),
            out_specs=pl.BlockSpec((rows, block), spot),
            scratch_shapes=[
                pltpu.VMEM((rows, width), jnp.bfloat16),
                pltpu.SemaphoreType.DMA((4 * chips,)),
            ],
        ),
        out_shape=jax.ShapeDtypeStruct((rows, width), jnp.bfloat16),
        compiler_params=pltpu.CompilerParams(vmem_limit_bytes=GRANT),
        cost_estimate=work(rows, width, 2 * width),
        name="hidden",
    )(place, *direct, handed, *early, *late, value_own, gate_own, value_far, *gate_far)


def send_kernel(hidden, weight, out_ref):
    out_ref[...] = dot(hidden[...], weight[...]).astype(jnp.bfloat16)


def run_send(hidden, out_far, q):
    rows, width = hidden.shape
    channels = out_far.shape[1] // SPLIT
    block = min(256, channels)
    first = q * channels // block
    return pl.pallas_call(
        send_kernel,
        grid=(channels // block,),
        in_specs=[
            pl.BlockSpec((rows, width), lambda j: (0, 0)),
            pl.BlockSpec((width, block), lambda j: (0, first + j)),
        ],
        out_specs=pl.BlockSpec((rows, block), lambda j: (0, j)),
        out_shape=jax.ShapeDtypeStruct((rows, channels), jnp.bfloat16),
        compiler_params=pltpu.CompilerParams(vmem_limit_bytes=GRANT),
        cost_estimate=work(rows, width, channels),
        name="send",
    )(hidden, out_far)


def finish_kernel(side, hidden, weight, tokens, out_ref):
    made = dot(hidden[...], weight[...])
    out_ref[...] = (made + tokens[...].astype(jnp.float32)).astype(jnp.bfloat16)


def run_finish(side, hidden, weight, tokens):
    rows, width = hidden.shape
    channels = weight.shape[1]
    block = min(512, channels)
    return pl.pallas_call(
        finish_kernel,
        grid_spec=pltpu.PrefetchScalarGridSpec(
            num_scalar_prefetch=1,
            grid=(channels // block,),
            in_specs=[
                pl.BlockSpec((rows, width), lambda j, side: (0, 0)),
                pl.BlockSpec((width, block), lambda j, side: (0, j)),
                pl.BlockSpec((rows, block), lambda j, side: (side[0], j)),
            ],
            out_specs=pl.BlockSpec((rows, block), lambda j, side: (side[0], j)),
        ),
        out_shape=jax.ShapeDtypeStruct(tokens.shape, jnp.bfloat16),
        compiler_params=pltpu.CompilerParams(vmem_limit_bytes=GRANT),
        cost_estimate=work(rows, width, channels),
        name="finish",
    )(side, hidden, weight, tokens)


def add_kernel(side, got, tokens, kept, out_ref):
    out_ref[...] = (got[...].astype(jnp.float32) + tokens[...].astype(jnp.float32)).astype(
        jnp.bfloat16
    )


def add_far(side, q, got, tokens, result):
    rows, columns = got.shape
    block = rows // 2

    def spot(j, side):
        return (2 * (1 - side[0]) + j, q)

    return pl.pallas_call(
        add_kernel,
        grid_spec=pltpu.PrefetchScalarGridSpec(
            num_scalar_prefetch=1,
            grid=(2,),
            in_specs=[
                pl.BlockSpec((block, columns), lambda j, side: (j, 0)),
                pl.BlockSpec((block, columns), spot),
                pl.BlockSpec(memory_space=pl.ANY),
            ],
            out_specs=pl.BlockSpec((block, columns), spot),
        ),
        out_shape=jax.ShapeDtypeStruct(tokens.shape, jnp.bfloat16),
        input_output_aliases={3: 0},
        name="add_far",
    )(side, got, tokens, result)


def swap(array, axis):
    return lax.ppermute(array, axis, [(0, 1), (1, 0)])


def cross(array):
    return lax.ppermute(array, ("chan", "sub"), [(0, 3), (1, 2), (2, 1), (3, 0)])


def ahead(array, offset):
    chips = lax.axis_size("seq")
    return lax.ppermute(array, "seq", [(j, (j + offset) % chips) for j in range(chips)])


def anchor_kernel(place, *refs):
    for at in range(refs[-1].shape[0]):
        refs[-1][at] = place[at]


def anchor(place, after):
    return pl.pallas_call(
        anchor_kernel,
        in_specs=[pl.BlockSpec(memory_space=pltpu.SMEM)]
        + [pl.BlockSpec(memory_space=pl.ANY)] * len(after),
        out_specs=pl.BlockSpec(memory_space=pltpu.SMEM),
        out_shape=jax.ShapeDtypeStruct(place.shape, place.dtype),
        cost_estimate=pl.CostEstimate(flops=10**11, bytes_accessed=0, transcendentals=0),
        name="anchor",
    )(place, *after)


def by_tokens(tokens, low_angle, high_taps, level_mix, w_value, w_gate, out_weight):
    rows, channels = tokens.shape
    chips = lax.axis_size("seq")
    narrow = channels // (2 * chips)
    chip, core = lax.axis_index("seq"), lax.axis_index("sub")
    side, group = lax.axis_index("chan"), lax.axis_index("groups")
    live = min(LEVELS, (rows * 2 * chips - 1).bit_length())
    order = sorted(range(1, chips), key=lambda s: abs(2 * s - chips))
    place = jnp.stack([chip, core, side, group, chips]).astype(jnp.int32)

    blocks = run_cut(place, tokens, chips)
    blocks, weights, low_angle = lax.optimization_barrier(
        (blocks, (w_value, w_gate, out_weight), low_angle)
    )
    direct = [None] * chips
    for s in order:
        direct[s] = ahead(blocks[s], s)
    handed = [swap(blocks[0], "sub")] + [swap(direct[s][1], "sub") for s in range(1, chips)]

    value_piece, gate_piece, out_piece = run_pieces(place, weights)
    value_first = swap(value_piece, "chan")
    gate_first = swap(gate_piece, "chan")
    direct, value_first, gate_first, out_piece = lax.optimization_barrier(
        (direct, value_first, gate_first, out_piece)
    )
    value_far = lax.all_gather(value_first, ("groups", "sub"), tiled=True)
    out_first = swap(out_piece, "chan")
    gate_second = swap(gate_first, "groups")
    gate_third = swap(gate_first, "sub")

    coef = run_coefficients(place, low_angle, high_taps, level_mix, live)
    far, near = run_filter(place, coef, tokens, direct[1:], handed, live)

    far, gate_third = lax.optimization_barrier((far, gate_third))
    far_got = [far[0]] + [None] * (chips - 1)
    for s in order:
        far_got[s] = ahead(far[s], s)

    def exchange(backs):
        return (
            swap(jnp.stack([far_got[back][0] for back in backs]), "chan"),
            cross(jnp.stack([far_got[back][1] for back in backs])),
        )

    rounds = [[0] + order[:1], order[1:]]
    near, far_got[order[0]], out_first = lax.optimization_barrier(
        (near, far_got[order[0]], out_first)
    )
    out_far = lax.all_gather(out_first, ("groups", "sub"), tiled=True)
    early = exchange(rounds[0])
    near_got = [near[0]] + [None] * (chips - 1)
    for s, wait in zip(order, [None, *early]):
        near[s], wait = lax.optimization_barrier((near[s], wait))
        near_got[s] = ahead(near[s], s)
    far_got, gate_second = lax.optimization_barrier((far_got, gate_second))
    late = exchange(rounds[1])
    place = anchor(place, [far_got[s] for s in order] + list(early))
    near_got, late, place, gate_second = lax.optimization_barrier(
        (near_got, late, place, gate_second)
    )
    gate_far = [gate_first, gate_second, gate_third, swap(gate_second, "sub")]
    handed = swap(jnp.stack([block[1] for block in near_got]), "sub")
    hidden = run_hidden(
        place, rounds, near_got, handed, early, late, w_value, w_gate, value_far, gate_far
    )
    which = place[2:3]
    returned = []
    for q in range(SPLIT):
        sent = run_send(hidden, out_far, q)
        returned.append(swap(sent, "chan"))
        hidden, sent = lax.optimization_barrier((hidden, sent))
    hidden, returned[0] = lax.optimization_barrier((hidden, returned[0]))
    result = run_finish(which, hidden, out_weight, tokens)
    for q in range(SPLIT):
        result = add_far(which, q, returned[q], tokens, result)
    return result


def solution(mesh):
    def shards(tokens, *rest):
        ways = mesh.shape["seq"] * mesh.shape["sub"]
        pairs = all(mesh.shape[name] == 2 for name in ("groups", "chan", "sub"))
        rows, channels = tokens.shape
        fits = channels == ways * LANES and rows % 64 == 0
        fits = fits and rows * ways == 8 * WIDE * RUN and rest[3].shape[0] % 512 == 0
        return (by_tokens if pairs and fits else general)(tokens, *rest)

    return jax.shard_map(
        shards,
        mesh=mesh,
        in_specs=(
            P(("groups", "seq", "sub"), "chan"),
            P("chan"),
            P(None, "chan"),
            P(None, "chan"),
            P(None, "chan"),
            P(None, "chan"),
            P(None, "chan"),
        ),
        out_specs=P(("groups", "seq", "sub"), "chan"),
        check_vma=False,
    )
```

```python
import functools

import jax
import jax.numpy as jnp
from jax import lax
from jax.experimental import pallas as pl
from jax.experimental.pallas import tpu as pltpu
from jax.sharding import PartitionSpec as P

LEVELS = 15
LANES = 128
SPLIT = 2
RUN = 16
MIDDLE = 8
WIDE = 64
LINE = ("seq", "sub")
GRANT = 16 * 2**20
LITTLE = 12 * 2**20


def run_levels(stream, shifter, low0, low1, high0, high1, mix):
    mixed = mix[LEVELS + 1] * stream
    for level in range(LEVELS):
        shifted = shifter(stream, 2**level)
        high = high0 * stream + high1 * shifted
        stream = low0 * stream + low1 * shifted
        mixed = mixed + mix[level] * high
    return mixed + mix[LEVELS] * stream


def general(tokens, low_angle, high_taps, level_mix, w_value, w_gate, out_weight):
    rows = tokens.shape[0]
    channels = tokens.shape[1]
    ways = lax.axis_size(LINE)
    total = rows * ways
    narrow = channels // ways
    place = lax.axis_index(LINE) * narrow
    columns = lax.all_to_all(tokens.T, LINE, split_axis=0, concat_axis=1, tiled=True)
    angle = lax.dynamic_slice_in_dim(low_angle, place, narrow, 0)[:, None]
    high_pair = lax.dynamic_slice_in_dim(high_taps, place, narrow, 1)[:, :, None]
    mix = lax.dynamic_slice_in_dim(level_mix, place, narrow, 1)[:, :, None]

    def shifter(stream, reach):
        if reach >= total:
            return jnp.zeros_like(stream)
        return jnp.concatenate(
            [jnp.zeros((stream.shape[0], reach), jnp.float32), stream[:, : total - reach]], 1
        )

    mixed = run_levels(
        columns.astype(jnp.float32),
        shifter,
        jnp.cos(angle),
        jnp.sin(angle),
        high_pair[0],
        high_pair[1],
        mix,
    )
    filtered = jax.nn.gelu(mixed).astype(jnp.bfloat16)
    activated = lax.all_to_all(filtered, LINE, split_axis=1, concat_axis=0, tiled=True).T
    piece = lax.all_gather(activated, "chan", axis=1, tiled=True)
    value = jnp.dot(piece, w_value, preferred_element_type=jnp.float32)
    gate = jnp.dot(piece, w_gate, preferred_element_type=jnp.float32)
    hidden = (value * jax.nn.sigmoid(gate)).astype(jnp.bfloat16)
    projected = jnp.dot(
        lax.all_gather(hidden, "chan", axis=1, tiled=True),
        out_weight,
        preferred_element_type=jnp.float32,
    )
    return (projected + tokens.astype(jnp.float32)).astype(jnp.bfloat16)


def coefficients(live, lanes, angle_ref, high_ref, mix_ref, out_ref):
    low0, low1 = jnp.cos(angle_ref[:, lanes]), jnp.sin(angle_ref[:, lanes])
    high0, high1 = high_ref[0:1, lanes], high_ref[1:2, lanes]
    power = jnp.ones_like(low0)
    for level in range(live + 1):
        weight = jnp.zeros_like(low0)
        if level < live:
            weight = weight + mix_ref[level : level + 1, lanes] * (high0 - high1 * low0 / low1)
        if level > 0:
            weight = weight + mix_ref[level - 1 : level, lanes] * high1 / low1
        if level == live:
            scale = jnp.ones_like(low0)
            for rest in range(live, LEVELS):
                weight = weight + mix_ref[rest : rest + 1, lanes] * high0 * scale
                scale = scale * low0
            weight = weight + mix_ref[LEVELS : LEVELS + 1, lanes] * scale
        weight = weight * power
        if level == 0:
            weight = weight + mix_ref[LEVELS + 1 : LEVELS + 2, lanes]
        out_ref[level : level + 1, :] = weight
        power = power * low0
    out_ref[live + 1 : live + 2, :] = low1 / low0


def advance(stream, tail, ratio):
    reach = tail.shape[0]
    shifted = jnp.concatenate([tail, stream[: stream.shape[0] - reach]], 0)
    return stream + ratio * shifted


def copy_all(pairs, sems, meanwhile=None):
    copies = [pltpu.make_async_copy(*pair, sems.at[at]) for at, pair in enumerate(pairs)]
    for copy in copies:
        copy.start()
    if meanwhile:
        meanwhile()
    for copy in copies:
        copy.wait()


def line_of(place, back, other):
    chips = place[4]
    core = 1 - place[1] if other else place[1]
    return lax.rem(place[0] - back + chips, chips) * 2 + core


def cut_kernel(chips, place, tokens, *outs):
    for ahead in range(chips):
        for other in range(2):
            if ahead or other:
                start = pl.multiple_of(line_of(place, -ahead, other) * LANES, LANES)
                block = tokens[:, pl.ds(start, LANES)]
                if ahead:
                    outs[ahead][other] = block
                else:
                    outs[0][...] = block


def run_cut(place, tokens, chips):
    rows = tokens.shape[0]
    shapes = [(rows, LANES)] + [(2, rows, LANES)] * (chips - 1)
    return pl.pallas_call(
        functools.partial(cut_kernel, chips),
        in_specs=[
            pl.BlockSpec(memory_space=pltpu.SMEM),
            pl.BlockSpec(memory_space=pltpu.VMEM),
        ],
        out_specs=[pl.BlockSpec(memory_space=pltpu.VMEM)] * chips,
        out_shape=[jax.ShapeDtypeStruct(shape, tokens.dtype) for shape in shapes],
        name="cut",
    )(place, tokens)


def levels_kernel(live, chips, place, angle_ref, high_ref, mix_ref, own, *refs):
    direct = refs[: chips - 1]
    handed = refs[chips - 1 : 2 * chips - 1]
    far = refs[2 * chips - 1 : 3 * chips - 1]
    near = refs[3 * chips - 1 : 4 * chips - 1]
    tokens, stream_ref, mixed_ref, act_ref, coef_ref, sems = refs[4 * chips - 1 :]
    side = place[2]
    rows = own.shape[0]
    units = rows * 2 * chips // 8

    def block(line):
        return pl.ds(pl.multiple_of(line * rows, rows), rows)

    columns = pl.ds(pl.multiple_of(line_of(place, 0, 0) * LANES, LANES), LANES)
    pairs = []
    for back in range(chips):
        mine = direct[back - 1].at[0] if back else own.at[:, columns]
        pairs.append((mine, tokens.at[block(line_of(place, back, 0))]))
        pairs.append((handed[back], tokens.at[block(line_of(place, back, 1))]))
    copy_all(
        pairs, sems, lambda: coefficients(live, columns, angle_ref, high_ref, mix_ref, coef_ref)
    )

    def whole(row):
        return jnp.broadcast_to(coef_ref[row : row + 1, :], (8, LANES))[None]

    def zero(n):
        return jnp.zeros((n, 8, LANES), jnp.float32)

    ratio = whole(live + 1)

    def first(i, carry):
        start = pl.multiple_of(i * RUN * 8, RUN * 8)
        x = tokens[pl.ds(start, RUN * 8), :].astype(jnp.float32).reshape(RUN, 8, LANES)
        mixed = whole(0) * x
        row = lax.broadcasted_iota(jnp.int32, (1, 8, LANES), 1)
        kept = []
        for level, tail in enumerate(carry):
            kept.append(x[RUN - tail.shape[0] :])
            if level < 3:
                turned = pltpu.roll(jnp.concatenate([tail, x], 0), 2**level, 1)
                x = x + ratio * jnp.where(row < 2**level, turned[:RUN], turned[1:])
            else:
                x = advance(x, tail, ratio)
            mixed = mixed + whole(level + 1) * x
        stream_ref[pl.ds(i * RUN, RUN)] = x
        mixed_ref[pl.ds(i * RUN, RUN)] = mixed
        return tuple(kept)

    lax.fori_loop(0, units // RUN, first, tuple(zero(n) for n in (1, 1, 1, 1, 2, 4)))

    stream = stream_ref.reshape(units // MIDDLE, MIDDLE, 8, LANES)
    total = mixed_ref.reshape(units // MIDDLE, MIDDLE, 8, LANES)
    steps = units // MIDDLE // RUN

    def second(t, carry):
        q = t // steps
        i = t % steps
        x = stream[pl.ds(i * RUN, RUN), q]
        mixed = total[pl.ds(i * RUN, RUN), q]
        keep = jnp.where(i > 0, 1.0, 0.0)
        kept = []
        for level, tail in enumerate(carry):
            kept.append(x[RUN - tail.shape[0] :])
            x = advance(x, tail * keep, ratio)
            mixed = mixed + whole(level + 7) * x
        stream[pl.ds(i * RUN, RUN), q] = x
        total[pl.ds(i * RUN, RUN), q] = mixed
        return tuple(kept)

    lax.fori_loop(0, MIDDLE * steps, second, tuple(zero(n) for n in (1, 2, 4)))

    stream_wide = stream_ref.reshape(units // WIDE, WIDE, 8, LANES)
    total_wide = mixed_ref.reshape(units // WIDE, WIDE, 8, LANES)
    act_wide = act_ref.reshape(units // WIDE, WIDE // 2, 16, LANES)

    def third(pair, _):
        halves = []
        for odd in range(2):
            x = stream_wide[:, pair * 2 + odd]
            mixed = total_wide[:, pair * 2 + odd]
            for level in range(9, live):
                x = advance(x, zero(2 ** (level - 9)), ratio)
                mixed = mixed + whole(level + 1) * x
            halves.append(jax.nn.gelu(mixed))
        act_wide[:, pair] = jnp.concatenate(halves, 1).astype(jnp.bfloat16)
        return 0

    lax.fori_loop(0, WIDE // 2, third, 0)

    half = rows // 2
    pairs = []
    for ahead in range(chips):
        for other in range(2):
            start = line_of(place, -ahead, other) * rows
            for outs, which in ((far, 1 - side), (near, side)):
                begin = pl.multiple_of(start + which * half, half)
                pairs.append((act_ref.at[pl.ds(begin, half)], outs[ahead].at[other]))
    copy_all(pairs, sems)


def run_filter(place, angle, high, mix, own, direct, handed, live):
    chips = len(handed)
    rows = handed[0].shape[0]
    total = rows * 2 * chips
    anywhere = pl.BlockSpec(memory_space=pltpu.HBM)
    outs = pl.pallas_call(
        functools.partial(levels_kernel, live, chips),
        out_shape=[jax.ShapeDtypeStruct((2, rows // 2, LANES), jnp.bfloat16)] * (2 * chips),
        in_specs=[
            pl.BlockSpec(memory_space=pltpu.SMEM),
        ]
        + [pl.BlockSpec(memory_space=pltpu.VMEM)] * 3
        + [anywhere] * (2 * chips),
        out_specs=[anywhere] * (2 * chips),
        scratch_shapes=[
            pltpu.VMEM((total, LANES), jnp.bfloat16),
            pltpu.VMEM((total // 8, 8, LANES), jnp.float32),
            pltpu.VMEM((total // 8, 8, LANES), jnp.float32),
            pltpu.VMEM((total, LANES), jnp.bfloat16),
            pltpu.VMEM((live + 2, LANES), jnp.float32),
            pltpu.SemaphoreType.DMA((4 * chips,)),
        ],
        compiler_params=pltpu.CompilerParams(vmem_limit_bytes=GRANT),
        name="levels",
    )(place, angle[None], high, mix, own, *direct, *handed)
    return list(outs[:chips]), list(outs[chips:])


def work(rows, depth, columns):
    return pl.CostEstimate(
        flops=2 * rows * depth * columns,
        bytes_accessed=2 * (rows * depth + depth * columns + rows * columns),
        transcendentals=0,
    )


def dot(a, b):
    return jnp.dot(a, b, preferred_element_type=jnp.float32)


def load_kernel(place, *refs):
    value_own, gate_own = refs[:2]
    pieces = refs[2:6]
    outs, sems = refs[-6:-1], refs[-1]
    core, group = place[1], place[3]
    depth = pieces[0].shape[1]
    pairs = [(value_own, outs[0]), (gate_own, outs[1])]
    for piece, far_group, far_core in zip(pieces, (0, 1, 0, 1), (0, 0, 1, 1)):
        quarter = 2 * (1 - group if far_group else group) + (1 - core if far_core else core)
        rows = pl.ds(pl.multiple_of(quarter * depth, depth), depth)
        for at in range(2):
            pairs.append((piece.at[at], outs[2 + at].at[rows]))
    copy_all(pairs, sems)
    for at in range(place.shape[0]):
        outs[4][at] = place[at]


def run_load(place, value_own, gate_own, fetched, after):
    arrays = [value_own, gate_own, *fetched, *after]
    whole = jax.ShapeDtypeStruct(value_own.shape, value_own.dtype)
    smem = pl.BlockSpec(memory_space=pltpu.SMEM)
    return pl.pallas_call(
        load_kernel,
        in_specs=[smem] + [pl.BlockSpec(memory_space=pltpu.HBM)] * len(arrays),
        out_specs=[pl.BlockSpec(memory_space=pltpu.VMEM)] * 4 + [smem],
        out_shape=[whole] * 4 + [jax.ShapeDtypeStruct(place.shape, place.dtype)],
        scratch_shapes=[pltpu.SemaphoreType.DMA((10,))],
        compiler_params=pltpu.CompilerParams(vmem_limit_bytes=LITTLE),
        cost_estimate=pl.CostEstimate(flops=10**11, bytes_accessed=0, transcendentals=0),
        name="load",
    )(place, *arrays)


def hidden_kernel(chips, q, block, place, *refs):
    direct = refs[:chips]
    handed, straight, crossed = refs[chips : chips + 3]
    value_own, gate_own, value_far, gate_far, hidden_ref, act, sems = refs[chips + 3 :]
    side = place[2]
    channels = 2 * chips * LANES
    part = pl.ds(q * act.shape[0], act.shape[0])
    pairs = []
    for back in range(chips):
        for other, near, far in ((0, direct[back], straight), (1, handed, crossed)):
            line = line_of(place, back, other) * LANES
            for start, source in (
                (side * channels + line, near.at[back if other else 0, part]),
                ((1 - side) * channels + line, far.at[back, part]),
            ):
                lanes = pl.ds(pl.multiple_of(start, LANES), LANES)
                pairs.append((source, act.at[:, lanes]))
    copy_all(pairs, sems)

    for whose, value_ref, gate_ref in ((side, value_own, gate_own), (1 - side, value_far, gate_far)):

        @pl.loop(0, channels // block)
        def _(j):
            columns = pl.ds(pl.multiple_of(j * block, block), block)
            value = dot(act[...], value_ref[:, columns])
            gate = dot(act[...], gate_ref[:, columns])
            target = pl.ds(pl.multiple_of(whose * channels + j * block, block), block)
            hidden_ref[:, target] = (value * jax.nn.sigmoid(gate)).astype(jnp.bfloat16)


def run_hidden(place, q, direct, handed, straight, crossed, *weights):
    chips = len(direct)
    rows = handed.shape[1] // SPLIT
    width, channels = weights[0].shape
    in_vmem = pl.BlockSpec(memory_space=pltpu.VMEM)
    return pl.pallas_call(
        functools.partial(hidden_kernel, chips, q, min(512, channels)),
        in_specs=[pl.BlockSpec(memory_space=pltpu.SMEM)]
        + [pl.BlockSpec(memory_space=pltpu.HBM)] * (chips + 3)
        + [in_vmem] * len(weights),
        out_specs=in_vmem,
        scratch_shapes=[
            pltpu.VMEM((rows, width), jnp.bfloat16),
            pltpu.SemaphoreType.DMA((4 * chips,)),
        ],
        out_shape=jax.ShapeDtypeStruct((rows, width), jnp.bfloat16),
        compiler_params=pltpu.CompilerParams(vmem_limit_bytes=LITTLE),
        cost_estimate=work(rows, width, 2 * width),
        name="hidden",
    )(place, *direct, handed, straight, crossed, *weights)


def send_kernel(place, hidden, mine, twin, out_ref):
    depth = mine.shape[0]
    core = place[1]
    total = None
    for half, weight in ((core, mine), (1 - core, twin)):
        rows = pl.ds(pl.multiple_of(half * depth, depth), depth)
        term = dot(hidden[:, rows], weight[...])
        total = term if total is None else total + term
    out_ref[...] = total.astype(jnp.bfloat16)


def run_send(place, hidden, halves):
    rows, width = hidden.shape
    depth, channels = halves[0].shape
    block = min(512, channels)
    return pl.pallas_call(
        send_kernel,
        grid_spec=pltpu.PrefetchScalarGridSpec(
            num_scalar_prefetch=1,
            grid=(channels // block,),
            in_specs=[pl.BlockSpec((rows, width), lambda j, place: (0, 0))]
            + [pl.BlockSpec((depth, block), lambda j, place: (0, j))] * 2,
            out_specs=pl.BlockSpec((rows, block), lambda j, place: (0, j)),
        ),
        out_shape=jax.ShapeDtypeStruct((rows, channels), jnp.bfloat16),
        compiler_params=pltpu.CompilerParams(vmem_limit_bytes=LITTLE),
        cost_estimate=work(rows, width, channels),
        name="send",
    )(place, hidden, *halves)


def finish_kernel(side, *refs):
    parts, weight, tokens, out_ref = refs[:SPLIT], refs[SPLIT], refs[SPLIT + 1], refs[SPLIT + 2]
    rows = parts[0].shape[0]
    for q in range(SPLIT):
        at = pl.ds(q * rows, rows)
        made = dot(parts[q][...], weight[...])
        out_ref[at, :] = (made + tokens[at, :].astype(jnp.float32)).astype(jnp.bfloat16)


def run_finish(side, parts, weight, tokens):
    rows, width = parts[0].shape
    channels = weight.shape[1]
    block = min(512, channels)
    return pl.pallas_call(
        finish_kernel,
        grid_spec=pltpu.PrefetchScalarGridSpec(
            num_scalar_prefetch=1,
            grid=(channels // block,),
            in_specs=[pl.BlockSpec((rows, width), lambda j, side: (0, 0))] * SPLIT
            + [
                pl.BlockSpec((width, block), lambda j, side: (0, j)),
                pl.BlockSpec((SPLIT * rows, block), lambda j, side: (side[0], j)),
            ],
            out_specs=pl.BlockSpec((SPLIT * rows, block), lambda j, side: (side[0], j)),
        ),
        out_shape=jax.ShapeDtypeStruct(tokens.shape, jnp.bfloat16),
        compiler_params=pltpu.CompilerParams(vmem_limit_bytes=GRANT),
        cost_estimate=work(SPLIT * rows, width, channels),
        name="finish",
    )(side, *parts, weight, tokens)


def add_kernel(side, got, tokens, kept, out_ref):
    out_ref[...] = (got[...].astype(jnp.float32) + tokens[...].astype(jnp.float32)).astype(
        jnp.bfloat16
    )


def add_far(side, q, got, tokens, result):
    rows, channels = got.shape

    def spot(j, side):
        return (SPLIT * (1 - side[0]) + q, j)

    block = min(512, channels)
    return pl.pallas_call(
        add_kernel,
        grid_spec=pltpu.PrefetchScalarGridSpec(
            num_scalar_prefetch=1,
            grid=(channels // block,),
            in_specs=[
                pl.BlockSpec((rows, block), lambda j, side: (0, j)),
                pl.BlockSpec((rows, block), spot),
                pl.BlockSpec(memory_space=pl.ANY),
            ],
            out_specs=pl.BlockSpec((rows, block), spot),
        ),
        out_shape=jax.ShapeDtypeStruct(tokens.shape, jnp.bfloat16),
        input_output_aliases={3: 0},
        name="add_far",
    )(side, got, tokens, result)


def swap(array, axis):
    return lax.ppermute(array, axis, [(0, 1), (1, 0)])


def cross(array):
    return lax.ppermute(array, ("chan", "sub"), [(0, 3), (1, 2), (2, 1), (3, 0)])


def ahead(array, offset):
    chips = lax.axis_size("seq")
    return lax.ppermute(array, "seq", [(j, (j + offset) % chips) for j in range(chips)])


def by_tokens(tokens, low_angle, high_taps, level_mix, w_value, w_gate, out_weight):
    rows, channels = tokens.shape
    chips = lax.axis_size("seq")
    narrow = channels // (2 * chips)
    chip, core = lax.axis_index("seq"), lax.axis_index("sub")
    side, group = lax.axis_index("chan"), lax.axis_index("groups")
    live = min(LEVELS, (rows * 2 * chips - 1).bit_length())
    order = sorted(range(1, chips), key=lambda s: abs(2 * s - chips))
    place = jnp.stack([chip, core, side, group, chips]).astype(jnp.int32)

    blocks = run_cut(place, tokens, chips)
    blocks, weights = lax.optimization_barrier((blocks, (w_value, w_gate, out_weight)))
    direct = [None] * chips
    for s in order:
        direct[s] = ahead(blocks[s], s)
    handed = [swap(blocks[0], "sub")] + [swap(direct[s][1], "sub") for s in range(1, chips)]

    depth = w_value.shape[0] // 4
    pair = jnp.stack(
        [
            lax.dynamic_slice_in_dim(weight, (2 * group + core) * depth, depth, 0)
            for weight in weights[:2]
        ]
    )
    half = lax.dynamic_slice_in_dim(weights[2], core * 2 * depth, 2 * depth, 0)
    pair_first = swap(pair, "chan")
    direct, pair_first, half = lax.optimization_barrier((direct, pair_first, half))
    pair_second = swap(pair_first, "groups")
    half_first = swap(half, "chan")
    pair_third = swap(pair_first, "sub")

    far, near = run_filter(
        place, low_angle, high_taps, level_mix, tokens, direct[1:], handed, live
    )

    far, pair_third = lax.optimization_barrier((far, pair_third))
    far_got = [far[0]] + [None] * (chips - 1)
    for s in order:
        far_got[s] = ahead(far[s], s)

    def exchange(backs):
        return (
            swap(jnp.stack([far_got[back][0] for back in backs]), "chan"),
            cross(jnp.stack([far_got[back][1] for back in backs])),
        )

    near, far_got[order[0]] = lax.optimization_barrier((near, far_got[order[0]]))
    near, far_got = list(near), list(far_got)
    near_got = [near[0]] + [None] * (chips - 1)
    near_got[order[0]] = ahead(near[order[0]], order[0])
    near, far_got, pair_second, half_first = lax.optimization_barrier(
        (near, far_got, pair_second, half_first)
    )
    for s in order[1:]:
        near_got[s] = ahead(near[s], s)
    straight = swap(jnp.stack([block[0] for block in far_got]), "chan")
    crossed = cross(jnp.stack([block[1] for block in far_got]))
    pair_second, near_got[order[0]] = lax.optimization_barrier((pair_second, near_got[order[0]]))
    pair_fourth = swap(pair_second, "sub")
    fetched = [pair_first, pair_second, pair_third, pair_fourth]
    *loaded, place = run_load(place, w_value, w_gate, fetched, far_got[1:])
    half_first, straight = lax.optimization_barrier((half_first, straight))
    half_second = swap(half_first, "sub")
    near_got, straight, crossed, place, half_second = lax.optimization_barrier(
        (near_got, straight, crossed, place, half_second)
    )
    handed = swap(jnp.stack([block[1] for block in near_got]), "sub")
    which = place[2:3]
    hidden, returned = [], []
    for q in range(SPLIT):
        made = run_hidden(place, q, near_got, handed, straight, crossed, *loaded)
        sent = run_send(place, made, [half_first, half_second])
        place, sent = lax.optimization_barrier((place, sent))
        hidden.append(made)
        returned.append(swap(sent, "chan"))
    hidden, returned[0] = lax.optimization_barrier((hidden, returned[0]))
    result = run_finish(which, hidden, out_weight, tokens)
    for q in range(SPLIT):
        result = add_far(which, q, returned[q], tokens, result)
    return result


def solution(mesh):
    def shards(tokens, *rest):
        ways = mesh.shape["seq"] * mesh.shape["sub"]
        pairs = all(mesh.shape[name] == 2 for name in ("groups", "chan", "sub"))
        rows, channels = tokens.shape
        fits = channels == ways * LANES and rows % 64 == 0
        fits = fits and rows * ways == 8 * WIDE * RUN and rest[3].shape[0] % 512 == 0
        return (by_tokens if pairs and fits else general)(tokens, *rest)

    return jax.shard_map(
        shards,
        mesh=mesh,
        in_specs=(
            P(("groups", "seq", "sub"), "chan"),
            P("chan"),
            P(None, "chan"),
            P(None, "chan"),
            P(None, "chan"),
            P(None, "chan"),
            P(None, "chan"),
        ),
        out_specs=P(("groups", "seq", "sub"), "chan"),
        check_vma=False,
    )
```

```python
import functools

import jax
import jax.numpy as jnp
from jax import lax
from jax.experimental import pallas as pl
from jax.experimental.pallas import tpu as pltpu
from jax.sharding import PartitionSpec as P

LEVELS = 15
LANES = 128
SPLIT = 2
RUN = 16
MIDDLE = 8
WIDE = 64
LINE = ("seq", "sub")
GRANT = 16 * 2**20
LITTLE = 12 * 2**20


def run_levels(stream, shifter, low0, low1, high0, high1, mix):
    mixed = mix[LEVELS + 1] * stream
    for level in range(LEVELS):
        shifted = shifter(stream, 2**level)
        high = high0 * stream + high1 * shifted
        stream = low0 * stream + low1 * shifted
        mixed = mixed + mix[level] * high
    return mixed + mix[LEVELS] * stream


def general(tokens, low_angle, high_taps, level_mix, w_value, w_gate, out_weight):
    rows = tokens.shape[0]
    channels = tokens.shape[1]
    ways = lax.axis_size(LINE)
    total = rows * ways
    narrow = channels // ways
    place = lax.axis_index(LINE) * narrow
    columns = lax.all_to_all(tokens.T, LINE, split_axis=0, concat_axis=1, tiled=True)
    angle = lax.dynamic_slice_in_dim(low_angle, place, narrow, 0)[:, None]
    high_pair = lax.dynamic_slice_in_dim(high_taps, place, narrow, 1)[:, :, None]
    mix = lax.dynamic_slice_in_dim(level_mix, place, narrow, 1)[:, :, None]

    def shifter(stream, reach):
        if reach >= total:
            return jnp.zeros_like(stream)
        return jnp.concatenate(
            [jnp.zeros((stream.shape[0], reach), jnp.float32), stream[:, : total - reach]], 1
        )

    mixed = run_levels(
        columns.astype(jnp.float32),
        shifter,
        jnp.cos(angle),
        jnp.sin(angle),
        high_pair[0],
        high_pair[1],
        mix,
    )
    filtered = jax.nn.gelu(mixed).astype(jnp.bfloat16)
    activated = lax.all_to_all(filtered, LINE, split_axis=1, concat_axis=0, tiled=True).T
    piece = lax.all_gather(activated, "chan", axis=1, tiled=True)
    value = jnp.dot(piece, w_value, preferred_element_type=jnp.float32)
    gate = jnp.dot(piece, w_gate, preferred_element_type=jnp.float32)
    hidden = (value * jax.nn.sigmoid(gate)).astype(jnp.bfloat16)
    projected = jnp.dot(
        lax.all_gather(hidden, "chan", axis=1, tiled=True),
        out_weight,
        preferred_element_type=jnp.float32,
    )
    return (projected + tokens.astype(jnp.float32)).astype(jnp.bfloat16)


def coefficients(live, lanes, angle_ref, high_ref, mix_ref, out_ref):
    low0, low1 = jnp.cos(angle_ref[:, lanes]), jnp.sin(angle_ref[:, lanes])
    high0, high1 = high_ref[0:1, lanes], high_ref[1:2, lanes]
    power = jnp.ones_like(low0)
    for level in range(live + 1):
        weight = jnp.zeros_like(low0)
        if level < live:
            weight = weight + mix_ref[level : level + 1, lanes] * (high0 - high1 * low0 / low1)
        if level > 0:
            weight = weight + mix_ref[level - 1 : level, lanes] * high1 / low1
        if level == live:
            scale = jnp.ones_like(low0)
            for rest in range(live, LEVELS):
                weight = weight + mix_ref[rest : rest + 1, lanes] * high0 * scale
                scale = scale * low0
            weight = weight + mix_ref[LEVELS : LEVELS + 1, lanes] * scale
        weight = weight * power
        if level == 0:
            weight = weight + mix_ref[LEVELS + 1 : LEVELS + 2, lanes]
        out_ref[level : level + 1, :] = weight
        power = power * low0
    out_ref[live + 1 : live + 2, :] = low1 / low0


def advance(stream, tail, ratio):
    reach = tail.shape[0]
    shifted = jnp.concatenate([tail, stream[: stream.shape[0] - reach]], 0)
    return stream + ratio * shifted


def copy_all(pairs, sems, meanwhile=None):
    copies = [pltpu.make_async_copy(*pair, sems.at[at]) for at, pair in enumerate(pairs)]
    for copy in copies:
        copy.start()
    if meanwhile:
        meanwhile()
    for copy in copies:
        copy.wait()


def line_of(place, back, other):
    chips = place[4]
    core = 1 - place[1] if other else place[1]
    return lax.rem(place[0] - back + chips, chips) * 2 + core


def cut_kernel(chips, place, tokens, *outs):
    for ahead in range(chips):
        for other in range(2):
            if ahead or other:
                start = pl.multiple_of(line_of(place, -ahead, other) * LANES, LANES)
                block = tokens[:, pl.ds(start, LANES)]
                if ahead:
                    outs[ahead][other] = block
                else:
                    outs[0][...] = block


def run_cut(place, tokens, chips):
    rows = tokens.shape[0]
    shapes = [(rows, LANES)] + [(2, rows, LANES)] * (chips - 1)
    return pl.pallas_call(
        functools.partial(cut_kernel, chips),
        in_specs=[
            pl.BlockSpec(memory_space=pltpu.SMEM),
            pl.BlockSpec(memory_space=pltpu.VMEM),
        ],
        out_specs=[pl.BlockSpec(memory_space=pltpu.VMEM)] * chips,
        out_shape=[jax.ShapeDtypeStruct(shape, tokens.dtype) for shape in shapes],
        name="cut",
    )(place, tokens)


def levels_kernel(live, chips, place, angle_ref, high_ref, mix_ref, own, *refs):
    direct = refs[: chips - 1]
    handed = refs[chips - 1 : chips + 1]
    far = refs[chips + 1 : 2 * chips + 1]
    near = refs[2 * chips + 1 : (2 + SPLIT) * chips + 1]
    tokens, stream_ref, mixed_ref, act_ref, coef_ref = refs[(2 + SPLIT) * chips + 1 :]
    side = place[2]
    rows = own.shape[0]
    units = rows * 2 * chips // 8

    def block(line):
        return pl.ds(pl.multiple_of(line * rows, rows), rows)

    columns = pl.ds(pl.multiple_of(line_of(place, 0, 0) * LANES, LANES), LANES)
    for back in range(chips):
        tokens[block(line_of(place, back, 0)), :] = direct[back - 1][0] if back else own[...]
        tokens[block(line_of(place, back, 1)), :] = handed[1][back - 1] if back else handed[0][...]
    coefficients(live, columns, angle_ref, high_ref, mix_ref, coef_ref)

    def whole(row):
        return jnp.broadcast_to(coef_ref[row : row + 1, :], (8, LANES))[None]

    def zero(n):
        return jnp.zeros((n, 8, LANES), jnp.float32)

    ratio = whole(live + 1)

    def first(i, carry):
        start = pl.multiple_of(i * RUN * 8, RUN * 8)
        x = tokens[pl.ds(start, RUN * 8), :].astype(jnp.float32).reshape(RUN, 8, LANES)
        mixed = whole(0) * x
        row = lax.broadcasted_iota(jnp.int32, (1, 8, LANES), 1)
        kept = []
        for level, tail in enumerate(carry):
            kept.append(x[RUN - tail.shape[0] :])
            if level < 3:
                turned = pltpu.roll(jnp.concatenate([tail, x], 0), 2**level, 1)
                x = x + ratio * jnp.where(row < 2**level, turned[:RUN], turned[1:])
            else:
                x = advance(x, tail, ratio)
            mixed = mixed + whole(level + 1) * x
        stream_ref[pl.ds(i * RUN, RUN)] = x
        mixed_ref[pl.ds(i * RUN, RUN)] = mixed
        return tuple(kept)

    lax.fori_loop(0, units // RUN, first, tuple(zero(n) for n in (1, 1, 1, 1, 2, 4)))

    stream = stream_ref.reshape(units // MIDDLE, MIDDLE, 8, LANES)
    total = mixed_ref.reshape(units // MIDDLE, MIDDLE, 8, LANES)
    steps = units // MIDDLE // RUN

    def second(t, carry):
        q = t // steps
        i = t % steps
        x = stream[pl.ds(i * RUN, RUN), q]
        mixed = total[pl.ds(i * RUN, RUN), q]
        keep = jnp.where(i > 0, 1.0, 0.0)
        kept = []
        for level, tail in enumerate(carry):
            kept.append(x[RUN - tail.shape[0] :])
            x = advance(x, tail * keep, ratio)
            mixed = mixed + whole(level + 7) * x
        stream[pl.ds(i * RUN, RUN), q] = x
        total[pl.ds(i * RUN, RUN), q] = mixed
        return tuple(kept)

    lax.fori_loop(0, MIDDLE * steps, second, tuple(zero(n) for n in (1, 2, 4)))

    stream_wide = stream_ref.reshape(units // WIDE, WIDE, 8, LANES)
    total_wide = mixed_ref.reshape(units // WIDE, WIDE, 8, LANES)
    act_wide = act_ref.reshape(units // WIDE, WIDE // 2, 16, LANES)

    def third(pair, _):
        halves = []
        for odd in range(2):
            x = stream_wide[:, pair * 2 + odd]
            mixed = total_wide[:, pair * 2 + odd]
            for level in range(9, live):
                reach = 2 ** (level - 9)
                x = jnp.concatenate([x[:reach], x[reach:] + ratio * x[:-reach]], 0)
                mixed = mixed + whole(level + 1) * x
            halves.append(jax.nn.gelu(mixed))
        act_wide[:, pair] = jnp.concatenate(halves, 1).astype(jnp.bfloat16)
        return 0

    half = rows // 2
    part = half // SPLIT
    lax.fori_loop(0, WIDE // 2, third, 0)
    for ahead in range(chips):
        for other in range(2):
            start = line_of(place, -ahead, other) * rows
            begin = pl.multiple_of(start + (1 - side) * half, half)
            far[ahead][other] = act_ref[pl.ds(begin, half), :]
            for q in range(SPLIT):
                begin = pl.multiple_of(start + side * half + q * part, part)
                near[q * chips + ahead][other] = act_ref[pl.ds(begin, part), :]


def run_filter(place, angle, high, mix, own, direct, handed, live):
    chips = 1 + len(direct)
    rows = handed[0].shape[0]
    total = rows * 2 * chips
    anywhere = pl.BlockSpec(memory_space=pltpu.HBM)
    outs = pl.pallas_call(
        functools.partial(levels_kernel, live, chips),
        out_shape=[jax.ShapeDtypeStruct((2, rows // 2, LANES), jnp.bfloat16)] * chips
        + [jax.ShapeDtypeStruct((2, rows // 2 // SPLIT, LANES), jnp.bfloat16)] * (SPLIT * chips),
        in_specs=[
            pl.BlockSpec(memory_space=pltpu.SMEM),
        ]
        + [pl.BlockSpec(memory_space=pltpu.VMEM)] * (chips + 5),
        out_specs=[pl.BlockSpec(memory_space=pltpu.VMEM)] * ((1 + SPLIT) * chips),
        scratch_shapes=[
            pltpu.VMEM((total, LANES), jnp.bfloat16),
            pltpu.VMEM((total // 8, 8, LANES), jnp.float32),
            pltpu.VMEM((total // 8, 8, LANES), jnp.float32),
            pltpu.VMEM((total, LANES), jnp.bfloat16),
            pltpu.VMEM((live + 2, LANES), jnp.float32),
        ],
        compiler_params=pltpu.CompilerParams(vmem_limit_bytes=GRANT),
        name="levels",
    )(place, angle[None], high, mix, own, *direct, *handed)
    groups = [list(outs[at * chips : (at + 1) * chips]) for at in range(1 + SPLIT)]
    return groups[0], groups[1:]


def work(rows, depth, columns):
    return pl.CostEstimate(
        flops=2 * rows * depth * columns,
        bytes_accessed=2 * (rows * depth + depth * columns + rows * columns),
        transcendentals=0,
    )


def dot(a, b):
    return jnp.dot(a, b, preferred_element_type=jnp.float32)


def load_kernel(count, *refs):
    place, sources, outs = refs[0], refs[1 : 1 + count], refs[-count - 2 : -2]
    copy_all(list(zip(sources, outs)), refs[-1])
    for at in range(place.shape[0]):
        refs[-2][at] = place[at]


def run_load(place, arrays, after):
    count = len(arrays)
    smem = pl.BlockSpec(memory_space=pltpu.SMEM)
    *loaded, place = pl.pallas_call(
        functools.partial(load_kernel, count),
        in_specs=[smem] + [pl.BlockSpec(memory_space=pltpu.HBM)] * (count + len(after)),
        out_specs=[pl.BlockSpec(memory_space=pltpu.VMEM)] * count + [smem],
        out_shape=[jax.ShapeDtypeStruct(array.shape, array.dtype) for array in (*arrays, place)],
        scratch_shapes=[pltpu.SemaphoreType.DMA((count,))],
        compiler_params=pltpu.CompilerParams(vmem_limit_bytes=LITTLE),
        cost_estimate=pl.CostEstimate(flops=10**11, bytes_accessed=0, transcendentals=0),
        name="load",
    )(place, *arrays, *after)
    return loaded, place


def hidden_kernel(chips, block, place, *refs):
    direct = refs[:chips]
    handed, straight, crossed = refs[chips : chips + 3]
    own, fetched = refs[chips + 3 : chips + 5], refs[chips + 5 : chips + 9]
    hidden_ref, act, sems = refs[chips + 9 :]
    side = place[2]
    channels = 2 * chips * LANES
    pairs = []
    for back in range(chips):
        for other, near, far in ((0, direct[back], straight), (1, handed, crossed)):
            line = line_of(place, back, other) * LANES
            for start, source in (
                (side * channels + line, near.at[back if other else 0]),
                ((1 - side) * channels + line, far.at[back]),
            ):
                lanes = pl.ds(pl.multiple_of(start, LANES), LANES)
                pairs.append((source, act.at[:, lanes]))
    copy_all(pairs, sems)

    core, group = place[1], place[3]
    depth = fetched[0].shape[1]

    def own_side(at, columns):
        return dot(act[...], own[at][:, columns])

    def far_side(at, columns):
        total = None
        for piece, far_group, far_core in zip(fetched, (0, 1, 0, 1), (0, 0, 1, 1)):
            quarter = 2 * (1 - group if far_group else group) + (1 - core if far_core else core)
            rows = pl.ds(pl.multiple_of(quarter * depth, depth), depth)
            term = dot(act[:, rows], piece[at, :, columns])
            total = term if total is None else total + term
        return total

    for whose, product in ((side, own_side), (1 - side, far_side)):

        @pl.loop(0, channels // block)
        def _(j):
            columns = pl.ds(pl.multiple_of(j * block, block), block)
            target = pl.ds(pl.multiple_of(whose * channels + j * block, block), block)
            gated = product(0, columns) * jax.nn.sigmoid(product(1, columns))
            hidden_ref[:, target] = gated.astype(jnp.bfloat16)


def run_hidden(place, direct, handed, straight, crossed, *weights):
    chips = len(direct)
    rows = handed.shape[1]
    width, channels = weights[0].shape
    in_vmem = pl.BlockSpec(memory_space=pltpu.VMEM)
    return pl.pallas_call(
        functools.partial(hidden_kernel, chips, min(512, channels)),
        in_specs=[pl.BlockSpec(memory_space=pltpu.SMEM)]
        + [pl.BlockSpec(memory_space=pltpu.HBM)] * (chips + 3)
        + [in_vmem] * len(weights),
        out_specs=in_vmem,
        scratch_shapes=[
            pltpu.VMEM((rows, width), jnp.bfloat16),
            pltpu.SemaphoreType.DMA((4 * chips,)),
        ],
        out_shape=jax.ShapeDtypeStruct((rows, width), jnp.bfloat16),
        compiler_params=pltpu.CompilerParams(vmem_limit_bytes=LITTLE),
        cost_estimate=work(rows, width, 2 * width),
        name="hidden",
    )(place, *direct, handed, straight, crossed, *weights)


def send_kernel(place, hidden, mine, twin, out_ref):
    depth = mine.shape[0]
    core = place[1]
    total = None
    for half, weight in ((core, mine), (1 - core, twin)):
        rows = pl.ds(pl.multiple_of(half * depth, depth), depth)
        term = dot(hidden[:, rows], weight[...])
        total = term if total is None else total + term
    out_ref[...] = total.astype(jnp.bfloat16)


def run_send(place, hidden, halves):
    rows, width = hidden.shape
    depth, channels = halves[0].shape
    block = min(512, channels)
    return pl.pallas_call(
        send_kernel,
        grid_spec=pltpu.PrefetchScalarGridSpec(
            num_scalar_prefetch=1,
            grid=(channels // block,),
            in_specs=[pl.BlockSpec((rows, width), lambda j, place: (0, 0))]
            + [pl.BlockSpec((depth, block), lambda j, place: (0, j))] * 2,
            out_specs=pl.BlockSpec((rows, block), lambda j, place: (0, j)),
        ),
        out_shape=jax.ShapeDtypeStruct((rows, channels), jnp.bfloat16),
        compiler_params=pltpu.CompilerParams(vmem_limit_bytes=LITTLE),
        cost_estimate=work(rows, width, channels),
        name="send",
    )(place, hidden, *halves)


def finish_kernel(side, *refs):
    parts, weight, tokens, out_ref = refs[:SPLIT], refs[SPLIT], refs[SPLIT + 1], refs[SPLIT + 2]
    rows = parts[0].shape[0]
    for q in range(SPLIT):
        at = pl.ds(q * rows, rows)
        made = dot(parts[q][...], weight[...])
        out_ref[at, :] = (made + tokens[at, :].astype(jnp.float32)).astype(jnp.bfloat16)


def run_finish(side, parts, weight, tokens):
    rows, width = parts[0].shape
    channels = weight.shape[1]
    block = min(512, channels)
    return pl.pallas_call(
        finish_kernel,
        grid_spec=pltpu.PrefetchScalarGridSpec(
            num_scalar_prefetch=1,
            grid=(channels // block,),
            in_specs=[pl.BlockSpec((rows, width), lambda j, side: (0, 0))] * SPLIT
            + [
                pl.BlockSpec((width, block), lambda j, side: (0, j)),
                pl.BlockSpec((SPLIT * rows, block), lambda j, side: (side[0], j)),
            ],
            out_specs=pl.BlockSpec((SPLIT * rows, block), lambda j, side: (side[0], j)),
        ),
        out_shape=jax.ShapeDtypeStruct(tokens.shape, jnp.bfloat16),
        compiler_params=pltpu.CompilerParams(vmem_limit_bytes=GRANT),
        cost_estimate=work(SPLIT * rows, width, channels),
        name="finish",
    )(side, *parts, weight, tokens)


def add_kernel(side, got, tokens, kept, out_ref):
    out_ref[...] = (got[...].astype(jnp.float32) + tokens[...].astype(jnp.float32)).astype(
        jnp.bfloat16
    )


def add_far(side, q, got, tokens, result):
    rows, channels = got.shape

    def spot(j, side):
        return (SPLIT * (1 - side[0]) + q, j)

    block = min(512, channels)
    return pl.pallas_call(
        add_kernel,
        grid_spec=pltpu.PrefetchScalarGridSpec(
            num_scalar_prefetch=1,
            grid=(channels // block,),
            in_specs=[
                pl.BlockSpec((rows, block), lambda j, side: (0, j)),
                pl.BlockSpec((rows, block), spot),
                pl.BlockSpec(memory_space=pl.ANY),
            ],
            out_specs=pl.BlockSpec((rows, block), spot),
        ),
        out_shape=jax.ShapeDtypeStruct(tokens.shape, jnp.bfloat16),
        input_output_aliases={3: 0},
        name="add_far",
    )(side, got, tokens, result)


def swap(array, axis):
    return lax.ppermute(array, axis, [(0, 1), (1, 0)])


def cross(array):
    return lax.ppermute(array, ("chan", "sub"), [(0, 3), (1, 2), (2, 1), (3, 0)])


def ahead(array, offset):
    chips = lax.axis_size("seq")
    return lax.ppermute(array, "seq", [(j, (j + offset) % chips) for j in range(chips)])


def twins_kernel(chips, *refs):
    copy_all([(refs[at].at[1], refs[chips].at[at]) for at in range(chips)], refs[-1])


def run_twins(blocks):
    rows = blocks[0].shape[1]
    return pl.pallas_call(
        functools.partial(twins_kernel, len(blocks)),
        in_specs=[pl.BlockSpec(memory_space=pltpu.HBM)] * len(blocks),
        out_specs=pl.BlockSpec(memory_space=pltpu.VMEM),
        out_shape=jax.ShapeDtypeStruct((len(blocks), rows, LANES), blocks[0].dtype),
        scratch_shapes=[pltpu.SemaphoreType.DMA((len(blocks),))],
        compiler_params=pltpu.CompilerParams(vmem_limit_bytes=LITTLE),
        name="twins",
    )(*blocks)


def by_tokens(tokens, low_angle, high_taps, level_mix, w_value, w_gate, out_weight):
    rows, channels = tokens.shape
    chips = lax.axis_size("seq")
    narrow = channels // (2 * chips)
    chip, core = lax.axis_index("seq"), lax.axis_index("sub")
    side, group = lax.axis_index("chan"), lax.axis_index("groups")
    live = min(LEVELS, (rows * 2 * chips - 1).bit_length())
    order = sorted(range(1, chips), key=lambda s: abs(2 * s - chips))
    place = jnp.stack([chip, core, side, group, chips]).astype(jnp.int32)

    mine = lax.dynamic_slice_in_dim(tokens, (chip * 2 + core) * narrow, narrow, 1)
    blocks = run_cut(place, tokens, chips)
    blocks, weights = lax.optimization_barrier((blocks, (w_value, w_gate, out_weight)))
    direct = [None] * chips
    for s in order:
        direct[s] = ahead(blocks[s], s)
    handed = [swap(blocks[0], "sub"), swap(run_twins(direct[1:]), "sub")]

    depth = w_value.shape[0] // 4
    pair = jnp.stack(
        [
            lax.dynamic_slice_in_dim(weight, (2 * group + core) * depth, depth, 0)
            for weight in weights[:2]
        ]
    )
    half = lax.dynamic_slice_in_dim(weights[2], core * 2 * depth, 2 * depth, 0)
    pair_first = swap(pair, "chan")
    direct, pair_first, half = lax.optimization_barrier((direct, pair_first, half))
    pair_second = swap(pair_first, "groups")
    half_first = swap(half, "chan")
    pair_third = swap(pair_first, "sub")

    far, near = run_filter(
        place, low_angle, high_taps, level_mix, mine, direct[1:], handed, live
    )

    far, pair_third = lax.optimization_barrier((far, pair_third))
    far_got = [far[0]] + [None] * (chips - 1)
    for s in order:
        far_got[s] = ahead(far[s], s)

    def exchange(backs):
        return (
            swap(jnp.stack([far_got[back][0] for back in backs]), "chan"),
            cross(jnp.stack([far_got[back][1] for back in backs])),
        )

    near_got = [[part[0]] + [None] * (chips - 1) for part in near]
    for s in order:
        near[0][s], far_got[s] = lax.optimization_barrier((near[0][s], far_got[s]))
        near_got[0][s] = ahead(near[0][s], s)
    rows = near[0][0].shape[1]

    def exchange(q, first, second):
        part = slice(q * rows, (q + 1) * rows)
        straight, first = lax.optimization_barrier(
            (jnp.stack([block[0, part] for block in far_got]), first)
        )
        crossed, second = lax.optimization_barrier(
            (jnp.stack([block[1, part] for block in far_got]), second)
        )
        return swap(straight, "chan"), cross(crossed)

    got = exchange(0, half_first, pair_second)
    near_got[0][order[0]], pair_second = lax.optimization_barrier(
        (near_got[0][order[0]], pair_second)
    )
    pair_fourth = swap(pair_second, "sub")
    loaded, place = run_load(
        place, [w_value, w_gate, pair_first, pair_second, pair_third], far_got[1:]
    )
    near_got[0], got, place, pair_fourth, half_first = lax.optimization_barrier(
        (near_got[0], got, place, pair_fourth, half_first)
    )
    half_second = swap(half_first, "sub")
    loaded.append(pair_fourth)
    which = place[2:3]
    hidden, returned = [], []
    for q in range(SPLIT):
        handed = swap(run_twins(near_got[q]), "sub")
        if q + 1 < SPLIT:
            for s in order:
                near[q + 1][s], near_got[q][s] = lax.optimization_barrier(
                    (near[q + 1][s], near_got[q][s])
                )
                near_got[q + 1][s] = ahead(near[q + 1][s], s)
            later = exchange(q + 1, *got)
        made = run_hidden(place, near_got[q], handed, *got, *loaded)
        sent = run_send(place, made, [half_first, half_second])
        if q + 1 < SPLIT:
            near_got[q + 1], later, sent = lax.optimization_barrier((near_got[q + 1], later, sent))
            got = later
        hidden.append(made)
        returned.append(swap(sent, "chan"))
    hidden, returned[0] = lax.optimization_barrier((hidden, returned[0]))
    result = run_finish(which, hidden, out_weight, tokens)
    for q in range(SPLIT):
        result = add_far(which, q, returned[q], tokens, result)
    return result


def solution(mesh):
    def shards(tokens, *rest):
        ways = mesh.shape["seq"] * mesh.shape["sub"]
        pairs = all(mesh.shape[name] == 2 for name in ("groups", "chan", "sub"))
        rows, channels = tokens.shape
        fits = channels == ways * LANES and rows % 64 == 0
        fits = fits and rows * ways == 8 * WIDE * RUN and rest[3].shape[0] % 512 == 0
        return (by_tokens if pairs and fits else general)(tokens, *rest)

    return jax.shard_map(
        shards,
        mesh=mesh,
        in_specs=(
            P(("groups", "seq", "sub"), "chan"),
            P("chan"),
            P(None, "chan"),
            P(None, "chan"),
            P(None, "chan"),
            P(None, "chan"),
            P(None, "chan"),
        ),
        out_specs=P(("groups", "seq", "sub"), "chan"),
        check_vma=False,
    )
```

```python
import functools

import jax
import jax.numpy as jnp
from jax import lax
from jax.experimental import pallas as pl
from jax.experimental.pallas import tpu as pltpu
from jax.sharding import PartitionSpec as P

LEVELS = 15
LANES = 128
SPLIT = 2
RUN = 16
MIDDLE = 8
WIDE = 64
LINE = ("seq", "sub")
GRANT = 16 * 2**20
LITTLE = 12 * 2**20
LARGE = 54 * 2**20
PARTS = 4
HOP = 5*10**9


def run_levels(stream, shifter, low0, low1, high0, high1, mix):
    mixed = mix[LEVELS + 1] * stream
    for level in range(LEVELS):
        shifted = shifter(stream, 2**level)
        high = high0 * stream + high1 * shifted
        stream = low0 * stream + low1 * shifted
        mixed = mixed + mix[level] * high
    return mixed + mix[LEVELS] * stream


def general(tokens, low_angle, high_taps, level_mix, w_value, w_gate, out_weight):
    rows = tokens.shape[0]
    channels = tokens.shape[1]
    ways = lax.axis_size(LINE)
    total = rows * ways
    narrow = channels // ways
    place = lax.axis_index(LINE) * narrow
    columns = lax.all_to_all(tokens.T, LINE, split_axis=0, concat_axis=1, tiled=True)
    angle = lax.dynamic_slice_in_dim(low_angle, place, narrow, 0)[:, None]
    high_pair = lax.dynamic_slice_in_dim(high_taps, place, narrow, 1)[:, :, None]
    mix = lax.dynamic_slice_in_dim(level_mix, place, narrow, 1)[:, :, None]

    def shifter(stream, reach):
        if reach >= total:
            return jnp.zeros_like(stream)
        return jnp.concatenate(
            [jnp.zeros((stream.shape[0], reach), jnp.float32), stream[:, : total - reach]], 1
        )

    mixed = run_levels(
        columns.astype(jnp.float32),
        shifter,
        jnp.cos(angle),
        jnp.sin(angle),
        high_pair[0],
        high_pair[1],
        mix,
    )
    filtered = jax.nn.gelu(mixed).astype(jnp.bfloat16)
    activated = lax.all_to_all(filtered, LINE, split_axis=1, concat_axis=0, tiled=True).T
    piece = lax.all_gather(activated, "chan", axis=1, tiled=True)
    value = jnp.dot(piece, w_value, preferred_element_type=jnp.float32)
    gate = jnp.dot(piece, w_gate, preferred_element_type=jnp.float32)
    hidden = (value * jax.nn.sigmoid(gate)).astype(jnp.bfloat16)
    projected = jnp.dot(
        lax.all_gather(hidden, "chan", axis=1, tiled=True),
        out_weight,
        preferred_element_type=jnp.float32,
    )
    return (projected + tokens.astype(jnp.float32)).astype(jnp.bfloat16)


def coefficients(live, lanes, angle_ref, high_ref, mix_ref, out_ref):
    low0, low1 = jnp.cos(angle_ref[:, lanes]), jnp.sin(angle_ref[:, lanes])
    high0, high1 = high_ref[0:1, lanes], high_ref[1:2, lanes]
    power = jnp.ones_like(low0)
    for level in range(live + 1):
        weight = jnp.zeros_like(low0)
        if level < live:
            weight = weight + mix_ref[level : level + 1, lanes] * (high0 - high1 * low0 / low1)
        if level > 0:
            weight = weight + mix_ref[level - 1 : level, lanes] * high1 / low1
        if level == live:
            scale = jnp.ones_like(low0)
            for rest in range(live, LEVELS):
                weight = weight + mix_ref[rest : rest + 1, lanes] * high0 * scale
                scale = scale * low0
            weight = weight + mix_ref[LEVELS : LEVELS + 1, lanes] * scale
        weight = weight * power
        if level == 0:
            weight = weight + mix_ref[LEVELS + 1 : LEVELS + 2, lanes]
        out_ref[level : level + 1, :] = weight
        power = power * low0
    out_ref[live + 1 : live + 2, :] = low1 / low0


def advance(stream, tail, ratio):
    reach = tail.shape[0]
    shifted = jnp.concatenate([tail, stream[: stream.shape[0] - reach]], 0)
    return stream + ratio * shifted


def copy_all(pairs, sems, meanwhile=None):
    copies = [pltpu.make_async_copy(*pair, sems.at[at]) for at, pair in enumerate(pairs)]
    for copy in copies:
        copy.start()
    if meanwhile:
        meanwhile()
    for copy in copies:
        copy.wait()


def line_of(place, back, other):
    chips = place[4]
    core = 1 - place[1] if other else place[1]
    return lax.rem(place[0] - back + chips, chips) * 2 + core


def pair_kernel(value, gate, pair, sems):
    core, group = lax.axis_index("sub"), lax.axis_index("groups")
    depth = pair.shape[1]
    part = depth // PARTS
    pairs = []
    for at, weight in enumerate((value, gate)):
        for p in range(PARTS):
            here = pl.ds(pl.multiple_of((2 * group + core) * depth + p * part, part), part)
            pairs.append((weight.at[here], pair.at[at, pl.ds(p * part, part)]))
    copy_all(pairs, sems)


def run_pair(value, gate):
    width, channels = value.shape
    return pl.pallas_call(
        pair_kernel,
        in_specs=[pl.BlockSpec(memory_space=pltpu.HBM)] * 2,
        out_specs=pl.BlockSpec(memory_space=pltpu.VMEM),
        out_shape=jax.ShapeDtypeStruct((2, width // 4, channels), value.dtype),
        scratch_shapes=[pltpu.SemaphoreType.DMA((2 * PARTS,))],
        compiler_params=pltpu.CompilerParams(vmem_limit_bytes=LARGE),
        name="pair",
    )(value, gate)


def levels_kernel(live, chips, place, angle_ref, high_ref, mix_ref, own, *refs):
    direct = refs[: chips - 1]
    handed = refs[chips - 1 : chips + 1]
    outs = refs[chips + 1 : chips + 5]
    tokens, stream_ref, mixed_ref, act_ref, coef_ref = refs[chips + 5 :]
    side = place[2]
    rows = own.shape[0]
    units = rows * 2 * chips // 8

    def block(line):
        return pl.ds(pl.multiple_of(line * rows, rows), rows)

    columns = pl.ds(pl.multiple_of(line_of(place, 0, 0) * LANES, LANES), LANES)
    lanes = pl.ds(pl.multiple_of(place[1] * LANES, LANES), LANES)
    for back in range(chips):
        mine = direct[back - 1][:, lanes] if back else own[...]
        tokens[block(line_of(place, back, 0)), :] = mine
        tokens[block(line_of(place, back, 1)), :] = handed[1][back - 1] if back else handed[0][...]
    coefficients(live, columns, angle_ref, high_ref, mix_ref, coef_ref)

    def whole(row):
        return jnp.broadcast_to(coef_ref[row : row + 1, :], (8, LANES))[None]

    def zero(n):
        return jnp.zeros((n, 8, LANES), jnp.float32)

    ratio = whole(live + 1)

    def first(i, carry):
        start = pl.multiple_of(i * RUN * 8, RUN * 8)
        x = tokens[pl.ds(start, RUN * 8), :].astype(jnp.float32).reshape(RUN, 8, LANES)
        mixed = whole(0) * x
        row = lax.broadcasted_iota(jnp.int32, (1, 8, LANES), 1)
        kept = []
        for level, tail in enumerate(carry):
            kept.append(x[RUN - tail.shape[0] :])
            if level < 3:
                turned = pltpu.roll(jnp.concatenate([tail, x], 0), 2**level, 1)
                x = x + ratio * jnp.where(row < 2**level, turned[:RUN], turned[1:])
            else:
                x = advance(x, tail, ratio)
            mixed = mixed + whole(level + 1) * x
        stream_ref[pl.ds(i * RUN, RUN)] = x
        mixed_ref[pl.ds(i * RUN, RUN)] = mixed
        return tuple(kept)

    lax.fori_loop(0, units // RUN, first, tuple(zero(n) for n in (1, 1, 1, 1, 2, 4)))

    stream = stream_ref.reshape(units // MIDDLE, MIDDLE, 8, LANES)
    total = mixed_ref.reshape(units // MIDDLE, MIDDLE, 8, LANES)
    steps = units // MIDDLE // RUN

    def second(t, carry):
        q = t // steps
        i = t % steps
        x = stream[pl.ds(i * RUN, RUN), q]
        mixed = total[pl.ds(i * RUN, RUN), q]
        keep = jnp.where(i > 0, 1.0, 0.0)
        kept = []
        for level, tail in enumerate(carry):
            kept.append(x[RUN - tail.shape[0] :])
            x = advance(x, tail * keep, ratio)
            mixed = mixed + whole(level + 7) * x
        stream[pl.ds(i * RUN, RUN), q] = x
        total[pl.ds(i * RUN, RUN), q] = mixed
        return tuple(kept)

    lax.fori_loop(0, MIDDLE * steps, second, tuple(zero(n) for n in (1, 2, 4)))

    stream_wide = stream_ref.reshape(units // WIDE, WIDE, 8, LANES)
    total_wide = mixed_ref.reshape(units // WIDE, WIDE, 8, LANES)
    act_wide = act_ref.reshape(units // WIDE, WIDE // 2, 16, LANES)

    def third(pair, _):
        halves = []
        for odd in range(2):
            x = stream_wide[:, pair * 2 + odd]
            mixed = total_wide[:, pair * 2 + odd]
            for level in range(9, live):
                reach = 2 ** (level - 9)
                x = jnp.concatenate([x[:reach], x[reach:] + ratio * x[:-reach]], 0)
                mixed = mixed + whole(level + 1) * x
            halves.append(jax.nn.gelu(mixed))
        act_wide[:, pair] = jnp.concatenate(halves, 1).astype(jnp.bfloat16)
        return 0

    half = rows // 2
    lax.fori_loop(0, WIDE // 2, third, 0)
    for ahead in range(chips):
        for other in range(2):
            start = line_of(place, -ahead, other) * rows
            for at, which in enumerate((1 - side, side)):
                begin = pl.multiple_of(start + which * half, half)
                outs[2 * other + at][ahead] = act_ref[pl.ds(begin, half), :]


def run_filter(place, angle, high, mix, own, direct, handed, live):
    chips = 1 + len(direct)
    rows = handed[0].shape[0]
    total = rows * 2 * chips
    anywhere = pl.BlockSpec(memory_space=pltpu.HBM)
    return pl.pallas_call(
        functools.partial(levels_kernel, live, chips),
        out_shape=[jax.ShapeDtypeStruct((chips, rows // 2, LANES), jnp.bfloat16)] * 4,
        in_specs=[
            pl.BlockSpec(memory_space=pltpu.SMEM),
        ]
        + [pl.BlockSpec(memory_space=pltpu.VMEM)] * (chips + 5),
        out_specs=[pl.BlockSpec(memory_space=pltpu.VMEM)] * 4,
        scratch_shapes=[
            pltpu.VMEM((total, LANES), jnp.bfloat16),
            pltpu.VMEM((total // 8, 8, LANES), jnp.float32),
            pltpu.VMEM((total // 8, 8, LANES), jnp.float32),
            pltpu.VMEM((total, LANES), jnp.bfloat16),
            pltpu.VMEM((live + 2, LANES), jnp.float32),
        ],
        compiler_params=pltpu.CompilerParams(vmem_limit_bytes=GRANT),
        name="levels",
    )(place, angle[None], high, mix, own, *direct, *handed)


def join_kernel(*refs):
    sources, outs = refs[:4], refs[4:]
    chips, half, _ = sources[0].shape
    part = half // SPLIT
    for group in range(1 + SPLIT):
        rows = slice(None) if group == 0 else pl.ds((group - 1) * part, part)
        for ahead in range(chips):
            for other in range(2):
                source = sources[2 * other + (group > 0)]
                outs[group * chips + ahead][other] = source[ahead, rows]


def run_join(arrays):
    chips, half, _ = arrays[0].shape
    in_vmem = pl.BlockSpec(memory_space=pltpu.VMEM)
    sizes = [half] * chips + [half // SPLIT] * (SPLIT * chips)
    outs = pl.pallas_call(
        join_kernel,
        in_specs=[in_vmem] * 4,
        out_specs=[in_vmem] * len(sizes),
        out_shape=[jax.ShapeDtypeStruct((2, size, LANES), jnp.bfloat16) for size in sizes],
        compiler_params=pltpu.CompilerParams(vmem_limit_bytes=LITTLE),
        name="join",
    )(*arrays)
    groups = [list(outs[at * chips : (at + 1) * chips]) for at in range(1 + SPLIT)]
    return groups[0], groups[1:]


def work(rows, depth, columns):
    return pl.CostEstimate(
        flops=2 * rows * depth * columns,
        bytes_accessed=2 * (rows * depth + depth * columns + rows * columns),
        transcendentals=0,
    )


def dot(a, b):
    return jnp.dot(a, b, preferred_element_type=jnp.float32)


def load_kernel(count, *refs):
    place, sources, outs = refs[0], refs[1 : 1 + count], refs[-count - 2 : -2]
    copy_all(list(zip(sources, outs)), refs[-1])
    for at in range(place.shape[0]):
        refs[-2][at] = place[at]


def run_load(place, arrays, after):
    count = len(arrays)
    smem = pl.BlockSpec(memory_space=pltpu.SMEM)
    *loaded, place = pl.pallas_call(
        functools.partial(load_kernel, count),
        in_specs=[smem] + [pl.BlockSpec(memory_space=pltpu.HBM)] * (count + len(after)),
        out_specs=[pl.BlockSpec(memory_space=pltpu.VMEM)] * count + [smem],
        out_shape=[jax.ShapeDtypeStruct(array.shape, array.dtype) for array in (*arrays, place)],
        scratch_shapes=[pltpu.SemaphoreType.DMA((count,))],
        compiler_params=pltpu.CompilerParams(vmem_limit_bytes=LITTLE),
        cost_estimate=pl.CostEstimate(flops=10**11, bytes_accessed=0, transcendentals=0),
        name="load",
    )(place, *arrays, *after)
    return loaded, place


def hidden_kernel(chips, block, place, *refs):
    direct = refs[:chips]
    got, own, fetched = refs[chips], refs[chips + 1 : chips + 3], refs[chips + 3 : chips + 7]
    hidden_ref, act, sems = refs[chips + 7 :]
    side = place[2]
    channels = 2 * chips * LANES
    pairs = []
    for back in range(chips):
        for other in range(2):
            line = line_of(place, back, other) * LANES
            for start, source in (
                (side * channels + line, direct[back].at[other]),
                ((1 - side) * channels + line, got.at[back, other]),
            ):
                lanes = pl.ds(pl.multiple_of(start, LANES), LANES)
                pairs.append((source, act.at[:, lanes]))
    copy_all(pairs, sems)

    core, group = place[1], place[3]
    depth = fetched[0].shape[1]

    def own_side(at, columns):
        return dot(act[...], own[at][:, columns])

    def far_side(at, columns):
        total = None
        for piece, far_group, far_core in zip(fetched, (0, 1, 0, 1), (0, 0, 1, 1)):
            quarter = 2 * (1 - group if far_group else group) + (1 - core if far_core else core)
            rows = pl.ds(pl.multiple_of(quarter * depth, depth), depth)
            term = dot(act[:, rows], piece[at, :, columns])
            total = term if total is None else total + term
        return total

    for whose, product in ((side, own_side), (1 - side, far_side)):

        @pl.loop(0, channels // block)
        def _(j):
            columns = pl.ds(pl.multiple_of(j * block, block), block)
            target = pl.ds(pl.multiple_of(whose * channels + j * block, block), block)
            gated = product(0, columns) * jax.nn.sigmoid(product(1, columns))
            hidden_ref[:, target] = gated.astype(jnp.bfloat16)


def run_hidden(place, direct, got, *weights):
    chips = len(direct)
    rows = got.shape[2]
    width, channels = weights[0].shape
    in_vmem = pl.BlockSpec(memory_space=pltpu.VMEM)
    return pl.pallas_call(
        functools.partial(hidden_kernel, chips, min(512, channels)),
        in_specs=[pl.BlockSpec(memory_space=pltpu.SMEM)]
        + [pl.BlockSpec(memory_space=pltpu.HBM)] * (chips + 1)
        + [in_vmem] * len(weights),
        out_specs=in_vmem,
        scratch_shapes=[
            pltpu.VMEM((rows, width), jnp.bfloat16),
            pltpu.SemaphoreType.DMA((4 * chips,)),
        ],
        out_shape=jax.ShapeDtypeStruct((rows, width), jnp.bfloat16),
        compiler_params=pltpu.CompilerParams(vmem_limit_bytes=LITTLE),
        cost_estimate=work(rows, width, 2 * width),
        name="hidden",
    )(place, *direct, got, *weights)


def send_kernel(place, hidden, mine, twin, out_ref):
    depth = mine.shape[0]
    core = place[1]
    total = None
    for half, weight in ((core, mine), (1 - core, twin)):
        rows = pl.ds(pl.multiple_of(half * depth, depth), depth)
        term = dot(hidden[:, rows], weight[...])
        total = term if total is None else total + term
    out_ref[...] = total.astype(jnp.bfloat16)


def run_send(place, hidden, halves):
    rows, width = hidden.shape
    depth, channels = halves[0].shape
    block = min(512, channels)
    return pl.pallas_call(
        send_kernel,
        grid_spec=pltpu.PrefetchScalarGridSpec(
            num_scalar_prefetch=1,
            grid=(channels // block,),
            in_specs=[pl.BlockSpec((rows, width), lambda j, place: (0, 0))]
            + [pl.BlockSpec((depth, block), lambda j, place: (0, j))] * 2,
            out_specs=pl.BlockSpec((rows, block), lambda j, place: (0, j)),
        ),
        out_shape=jax.ShapeDtypeStruct((rows, channels), jnp.bfloat16),
        compiler_params=pltpu.CompilerParams(vmem_limit_bytes=LITTLE),
        cost_estimate=work(rows, width, channels),
        name="send",
    )(place, hidden, *halves)


def finish_kernel(side, *refs):
    parts, weight, tokens, out_ref = refs[:SPLIT], refs[SPLIT], refs[SPLIT + 1], refs[SPLIT + 2]
    rows = parts[0].shape[0]
    for q in range(SPLIT):
        at = pl.ds(q * rows, rows)
        made = dot(parts[q][...], weight[...])
        out_ref[at, :] = (made + tokens[at, :].astype(jnp.float32)).astype(jnp.bfloat16)


def run_finish(side, parts, weight, tokens):
    rows, width = parts[0].shape
    channels = weight.shape[1]
    block = min(512, channels)
    return pl.pallas_call(
        finish_kernel,
        grid_spec=pltpu.PrefetchScalarGridSpec(
            num_scalar_prefetch=1,
            grid=(channels // block,),
            in_specs=[pl.BlockSpec((rows, width), lambda j, side: (0, 0))] * SPLIT
            + [
                pl.BlockSpec((width, block), lambda j, side: (0, j)),
                pl.BlockSpec((SPLIT * rows, block), lambda j, side: (side[0], j)),
            ],
            out_specs=pl.BlockSpec((SPLIT * rows, block), lambda j, side: (side[0], j)),
        ),
        out_shape=jax.ShapeDtypeStruct(tokens.shape, jnp.bfloat16),
        compiler_params=pltpu.CompilerParams(vmem_limit_bytes=GRANT),
        cost_estimate=work(SPLIT * rows, width, channels),
        name="finish",
    )(side, *parts, weight, tokens)


def add_kernel(side, got, tokens, kept, out_ref):
    out_ref[...] = (got[...].astype(jnp.float32) + tokens[...].astype(jnp.float32)).astype(
        jnp.bfloat16
    )


def add_far(side, q, got, tokens, result):
    rows, channels = got.shape

    def spot(j, side):
        return (SPLIT * (1 - side[0]) + q, j)

    block = min(512, channels)
    return pl.pallas_call(
        add_kernel,
        grid_spec=pltpu.PrefetchScalarGridSpec(
            num_scalar_prefetch=1,
            grid=(channels // block,),
            in_specs=[
                pl.BlockSpec((rows, block), lambda j, side: (0, j)),
                pl.BlockSpec((rows, block), spot),
                pl.BlockSpec(memory_space=pl.ANY),
            ],
            out_specs=pl.BlockSpec((rows, block), spot),
        ),
        out_shape=jax.ShapeDtypeStruct(tokens.shape, jnp.bfloat16),
        input_output_aliases={3: 0},
        compiler_params=pltpu.CompilerParams(vmem_limit_bytes=LARGE),
        name="add_far",
    )(side, got, tokens, result)


def swap(array, axis):
    return lax.ppermute(array, axis, [(0, 1), (1, 0)])


def ahead(array, offset):
    chips = lax.axis_size("seq")
    return lax.ppermute(array, "seq", [(j, (j + offset) % chips) for j in range(chips)])


def anchor_kernel(*refs):
    refs[-1][...] = jnp.zeros(refs[-1].shape, refs[-1].dtype)


def anchor(after):
    return pl.pallas_call(
        anchor_kernel,
        in_specs=[pl.BlockSpec(memory_space=pltpu.HBM)] * len(after),
        out_specs=pl.BlockSpec(memory_space=pltpu.VMEM),
        out_shape=jax.ShapeDtypeStruct((8, LANES), jnp.float32),
        compiler_params=pltpu.CompilerParams(vmem_limit_bytes=LITTLE),
        cost_estimate=pl.CostEstimate(flops=10**11, bytes_accessed=0, transcendentals=0),
        name="anchor",
    )(*after)


def others_kernel(place, *refs):
    lanes = pl.ds(pl.multiple_of((1 - place[1]) * LANES, LANES), LANES)
    for at, block in enumerate(refs[:-1]):
        refs[-1][at] = block[:, lanes]


def run_others(place, blocks):
    in_vmem = pl.BlockSpec(memory_space=pltpu.VMEM)
    rows = blocks[0].shape[0]
    return pl.pallas_call(
        others_kernel,
        in_specs=[pl.BlockSpec(memory_space=pltpu.SMEM)] + [in_vmem] * len(blocks),
        out_specs=in_vmem,
        out_shape=jax.ShapeDtypeStruct((len(blocks), rows, LANES), blocks[0].dtype),
        compiler_params=pltpu.CompilerParams(vmem_limit_bytes=LITTLE),
        cost_estimate=pl.CostEstimate(flops=HOP, bytes_accessed=0, transcendentals=0),
        name="others",
    )(place, *blocks)


def by_tokens(tokens, low_angle, high_taps, level_mix, w_value, w_gate, out_weight):
    rows, channels = tokens.shape
    chips = lax.axis_size("seq")
    narrow = channels // (2 * chips)
    chip, core = lax.axis_index("seq"), lax.axis_index("sub")
    side, group = lax.axis_index("chan"), lax.axis_index("groups")
    live = min(LEVELS, (rows * 2 * chips - 1).bit_length())
    order = sorted(range(1, chips), key=lambda s: abs(2 * s - chips))
    place = jnp.stack([chip, core, side, group, chips]).astype(jnp.int32)

    pair = run_pair(w_value, w_gate)
    tokens, pair = lax.optimization_barrier((tokens, pair))
    def columns(back, first, count):
        start = ((chip - back) % chips * 2 + first) * narrow
        return lax.dynamic_slice_in_dim(tokens, start, count * narrow, 1)

    blocks = [columns(-s, 0, 2) for s in range(1, chips)]
    mine, other = columns(0, core, 1), columns(0, 1 - core, 1)
    blocks, out_piece = lax.optimization_barrier((blocks, out_weight))
    direct = [None] * chips
    for s in order:
        direct[s] = ahead(blocks[s - 1], s)
    handed = [swap(other, "sub"), swap(run_others(place, direct[1:]), "sub")]

    depth = w_value.shape[0] // 4
    half = lax.dynamic_slice_in_dim(out_piece, core * 2 * depth, 2 * depth, 0)
    pair_first = swap(pair, "chan")
    direct, pair_first, half = lax.optimization_barrier((direct, pair_first, half))
    pair_second = swap(pair_first, "groups")
    half_first = swap(half, "chan")
    pair_third = swap(pair_first, "sub")

    *kept, given_far, given_near = run_filter(
        place, low_angle, high_taps, level_mix, mine, direct[1:], handed, live
    )

    far, near = run_join([*kept, swap(given_far, "sub"), swap(given_near, "sub")])
    far, pair_third = lax.optimization_barrier((far, pair_third))
    far_got = [far[0]] + [None] * (chips - 1)
    for s in order:
        far_got[s] = ahead(far[s], s)

    def exchange(backs):
        return (
            swap(jnp.stack([far_got[back][0] for back in backs]), "chan"),
            cross(jnp.stack([far_got[back][1] for back in backs])),
        )

    both = anchor([pair_second, half_first])
    far_got, pair_second, half_first, both = lax.optimization_barrier(
        (far_got, pair_second, half_first, both)
    )
    far_got = list(far_got)
    near_got = [[part[0]] + [None] * (chips - 1) for part in near]
    for s in order:
        near[0][s], far_got[s] = lax.optimization_barrier((near[0][s], far_got[s]))
        near_got[0][s] = ahead(near[0][s], s)
    rows = near[0][0].shape[1]

    def exchange(q, before):
        part = slice(q * rows, (q + 1) * rows)
        mine, before = lax.optimization_barrier(
            (jnp.stack([block[:, part] for block in far_got]), before)
        )
        return swap(mine, "chan")

    got = [exchange(q, half_first) for q in range(SPLIT)]
    near_got[0][order[0]], pair_second = lax.optimization_barrier(
        (near_got[0][order[0]], pair_second)
    )
    pair_fourth = swap(pair_second, "sub")
    loaded, place = run_load(
        place, [w_value, w_gate, pair_first, pair_second, pair_third], far_got[1:]
    )
    near_got[0], got[0], place, pair_fourth, half_first = lax.optimization_barrier(
        (near_got[0], got[0], place, pair_fourth, half_first)
    )
    half_second = swap(half_first, "sub")
    loaded.append(pair_fourth)
    which = place[2:3]
    hidden, returned = [], []
    for q in range(SPLIT):
        if q + 1 < SPLIT:
            for s in order:
                near[q + 1][s], near_got[q][s] = lax.optimization_barrier(
                    (near[q + 1][s], near_got[q][s])
                )
                near_got[q + 1][s] = ahead(near[q + 1][s], s)
        made = run_hidden(place, near_got[q], got[q], *loaded)
        sent = run_send(place, made, [half_first, half_second])
        if q + 1 < SPLIT:
            near_got[q + 1], got[q + 1], sent = lax.optimization_barrier(
                (near_got[q + 1], got[q + 1], sent)
            )
        hidden.append(made)
        returned.append(swap(sent, "chan"))
    hidden, returned[0] = lax.optimization_barrier((hidden, returned[0]))
    result = run_finish(which, hidden, out_weight, tokens)
    for q in range(SPLIT):
        result = add_far(which, q, returned[q], tokens, result)
    return result


def solution(mesh):
    def shards(tokens, *rest):
        ways = mesh.shape["seq"] * mesh.shape["sub"]
        pairs = all(mesh.shape[name] == 2 for name in ("groups", "chan", "sub"))
        rows, channels = tokens.shape
        fits = channels == ways * LANES and rows % 64 == 0
        fits = fits and rows * ways == 8 * WIDE * RUN and rest[3].shape[0] % 512 == 0
        return (by_tokens if pairs and fits else general)(tokens, *rest)

    return jax.shard_map(
        shards,
        mesh=mesh,
        in_specs=(
            P(("groups", "seq", "sub"), "chan"),
            P("chan"),
            P(None, "chan"),
            P(None, "chan"),
            P(None, "chan"),
            P(None, "chan"),
            P(None, "chan"),
        ),
        out_specs=P(("groups", "seq", "sub"), "chan"),
        check_vma=False,
    )
```

```python
import functools

import jax
import jax.numpy as jnp
from jax import lax
from jax.experimental import pallas as pl
from jax.experimental.pallas import tpu as pltpu
from jax.sharding import PartitionSpec as P

LEVELS = 15
LANES = 128
SPLIT = 2
RUN = 16
MIDDLE = 8
WIDE = 64
LINE = ("seq", "sub")
GRANT = 16 * 2**20
LITTLE = 12 * 2**20
LARGE = 54 * 2**20
PARTS = 4
HOP = 5*10**9


def run_levels(stream, shifter, low0, low1, high0, high1, mix):
    mixed = mix[LEVELS + 1] * stream
    for level in range(LEVELS):
        shifted = shifter(stream, 2**level)
        high = high0 * stream + high1 * shifted
        stream = low0 * stream + low1 * shifted
        mixed = mixed + mix[level] * high
    return mixed + mix[LEVELS] * stream


def general(tokens, low_angle, high_taps, level_mix, w_value, w_gate, out_weight):
    rows = tokens.shape[0]
    channels = tokens.shape[1]
    ways = lax.axis_size(LINE)
    total = rows * ways
    narrow = channels // ways
    place = lax.axis_index(LINE) * narrow
    columns = lax.all_to_all(tokens.T, LINE, split_axis=0, concat_axis=1, tiled=True)
    angle = lax.dynamic_slice_in_dim(low_angle, place, narrow, 0)[:, None]
    high_pair = lax.dynamic_slice_in_dim(high_taps, place, narrow, 1)[:, :, None]
    mix = lax.dynamic_slice_in_dim(level_mix, place, narrow, 1)[:, :, None]

    def shifter(stream, reach):
        if reach >= total:
            return jnp.zeros_like(stream)
        return jnp.concatenate(
            [jnp.zeros((stream.shape[0], reach), jnp.float32), stream[:, : total - reach]], 1
        )

    mixed = run_levels(
        columns.astype(jnp.float32),
        shifter,
        jnp.cos(angle),
        jnp.sin(angle),
        high_pair[0],
        high_pair[1],
        mix,
    )
    filtered = jax.nn.gelu(mixed).astype(jnp.bfloat16)
    activated = lax.all_to_all(filtered, LINE, split_axis=1, concat_axis=0, tiled=True).T
    piece = lax.all_gather(activated, "chan", axis=1, tiled=True)
    value = jnp.dot(piece, w_value, preferred_element_type=jnp.float32)
    gate = jnp.dot(piece, w_gate, preferred_element_type=jnp.float32)
    hidden = (value * jax.nn.sigmoid(gate)).astype(jnp.bfloat16)
    projected = jnp.dot(
        lax.all_gather(hidden, "chan", axis=1, tiled=True),
        out_weight,
        preferred_element_type=jnp.float32,
    )
    return (projected + tokens.astype(jnp.float32)).astype(jnp.bfloat16)


def coefficients(live, lanes, angle_ref, high_ref, mix_ref, out_ref):
    low0, low1 = jnp.cos(angle_ref[:, lanes]), jnp.sin(angle_ref[:, lanes])
    high0, high1 = high_ref[0:1, lanes], high_ref[1:2, lanes]
    power = jnp.ones_like(low0)
    for level in range(live + 1):
        weight = jnp.zeros_like(low0)
        if level < live:
            weight = weight + mix_ref[level : level + 1, lanes] * (high0 - high1 * low0 / low1)
        if level > 0:
            weight = weight + mix_ref[level - 1 : level, lanes] * high1 / low1
        if level == live:
            scale = jnp.ones_like(low0)
            for rest in range(live, LEVELS):
                weight = weight + mix_ref[rest : rest + 1, lanes] * high0 * scale
                scale = scale * low0
            weight = weight + mix_ref[LEVELS : LEVELS + 1, lanes] * scale
        weight = weight * power
        if level == 0:
            weight = weight + mix_ref[LEVELS + 1 : LEVELS + 2, lanes]
        out_ref[level : level + 1, :] = weight
        power = power * low0
    out_ref[live + 1 : live + 2, :] = low1 / low0


def advance(stream, tail, ratio):
    reach = tail.shape[0]
    shifted = jnp.concatenate([tail, stream[: stream.shape[0] - reach]], 0)
    return stream + ratio * shifted


def copy_all(pairs, sems, meanwhile=None):
    copies = [pltpu.make_async_copy(*pair, sems.at[at]) for at, pair in enumerate(pairs)]
    for copy in copies:
        copy.start()
    if meanwhile:
        meanwhile()
    for copy in copies:
        copy.wait()


def line_of(place, back, other):
    chips = place[4]
    core = 1 - place[1] if other else place[1]
    return lax.rem(place[0] - back + chips, chips) * 2 + core


def pair_kernel(value, gate, pair, sems):
    core, group = lax.axis_index("sub"), lax.axis_index("groups")
    depth = pair.shape[1]
    part = depth // PARTS
    pairs = []
    for at, weight in enumerate((value, gate)):
        for p in range(PARTS):
            here = pl.ds(pl.multiple_of((2 * group + core) * depth + p * part, part), part)
            pairs.append((weight.at[here], pair.at[at, pl.ds(p * part, part)]))
    copy_all(pairs, sems)


def run_pair(value, gate):
    width, channels = value.shape
    return pl.pallas_call(
        pair_kernel,
        in_specs=[pl.BlockSpec(memory_space=pltpu.HBM)] * 2,
        out_specs=pl.BlockSpec(memory_space=pltpu.VMEM),
        out_shape=jax.ShapeDtypeStruct((2, width // 4, channels), value.dtype),
        scratch_shapes=[pltpu.SemaphoreType.DMA((2 * PARTS,))],
        compiler_params=pltpu.CompilerParams(vmem_limit_bytes=LARGE),
        name="pair",
    )(value, gate)


def levels_kernel(live, chips, place, angle_ref, high_ref, mix_ref, own, *refs):
    direct = refs[: chips - 1]
    handed = refs[chips - 1 : chips + 1]
    outs = refs[chips + 1 : chips + 5]
    tokens, stream_ref, mixed_ref, act_ref, coef_ref = refs[chips + 5 :]
    side = place[2]
    rows = own.shape[0]
    units = rows * 2 * chips // 8

    def block(line):
        return pl.ds(pl.multiple_of(line * rows, rows), rows)

    columns = pl.ds(pl.multiple_of(line_of(place, 0, 0) * LANES, LANES), LANES)
    lanes = pl.ds(pl.multiple_of(place[1] * LANES, LANES), LANES)
    for back in range(chips):
        mine = direct[back - 1][:, lanes] if back else own[...]
        tokens[block(line_of(place, back, 0)), :] = mine
        tokens[block(line_of(place, back, 1)), :] = handed[1][back - 1] if back else handed[0][...]
    coefficients(live, columns, angle_ref, high_ref, mix_ref, coef_ref)

    def whole(row):
        return jnp.broadcast_to(coef_ref[row : row + 1, :], (8, LANES))[None]

    def zero(n):
        return jnp.zeros((n, 8, LANES), jnp.float32)

    ratio = whole(live + 1)

    def first(i, carry):
        start = pl.multiple_of(i * RUN * 8, RUN * 8)
        x = tokens[pl.ds(start, RUN * 8), :].astype(jnp.float32).reshape(RUN, 8, LANES)
        mixed = whole(0) * x
        row = lax.broadcasted_iota(jnp.int32, (1, 8, LANES), 1)
        kept = []
        for level, tail in enumerate(carry):
            kept.append(x[RUN - tail.shape[0] :])
            if level < 3:
                turned = pltpu.roll(jnp.concatenate([tail, x], 0), 2**level, 1)
                x = x + ratio * jnp.where(row < 2**level, turned[:RUN], turned[1:])
            else:
                x = advance(x, tail, ratio)
            mixed = mixed + whole(level + 1) * x
        stream_ref[pl.ds(i * RUN, RUN)] = x
        mixed_ref[pl.ds(i * RUN, RUN)] = mixed
        return tuple(kept)

    lax.fori_loop(0, units // RUN, first, tuple(zero(n) for n in (1, 1, 1, 1, 2, 4)))

    stream = stream_ref.reshape(units // MIDDLE, MIDDLE, 8, LANES)
    total = mixed_ref.reshape(units // MIDDLE, MIDDLE, 8, LANES)
    steps = units // MIDDLE // RUN

    def second(t, carry):
        q = t // steps
        i = t % steps
        x = stream[pl.ds(i * RUN, RUN), q]
        mixed = total[pl.ds(i * RUN, RUN), q]
        keep = jnp.where(i > 0, 1.0, 0.0)
        kept = []
        for level, tail in enumerate(carry):
            kept.append(x[RUN - tail.shape[0] :])
            x = advance(x, tail * keep, ratio)
            mixed = mixed + whole(level + 7) * x
        stream[pl.ds(i * RUN, RUN), q] = x
        total[pl.ds(i * RUN, RUN), q] = mixed
        return tuple(kept)

    lax.fori_loop(0, MIDDLE * steps, second, tuple(zero(n) for n in (1, 2, 4)))

    stream_wide = stream_ref.reshape(units // WIDE, WIDE, 8, LANES)
    total_wide = mixed_ref.reshape(units // WIDE, WIDE, 8, LANES)
    act_wide = act_ref.reshape(units // WIDE, WIDE // 2, 16, LANES)

    def third(pair, _):
        halves = []
        for odd in range(2):
            x = stream_wide[:, pair * 2 + odd]
            mixed = total_wide[:, pair * 2 + odd]
            for level in range(9, live):
                reach = 2 ** (level - 9)
                x = jnp.concatenate([x[:reach], x[reach:] + ratio * x[:-reach]], 0)
                mixed = mixed + whole(level + 1) * x
            halves.append(jax.nn.gelu(mixed))
        act_wide[:, pair] = jnp.concatenate(halves, 1).astype(jnp.bfloat16)
        return 0

    half = rows // 2
    lax.fori_loop(0, WIDE // 2, third, 0)
    for ahead in range(chips):
        for other in range(2):
            start = line_of(place, -ahead, other) * rows
            for at, which in enumerate((1 - side, side)):
                begin = pl.multiple_of(start + which * half, half)
                outs[2 * other + at][ahead] = act_ref[pl.ds(begin, half), :]


def run_filter(place, angle, high, mix, own, direct, handed, live):
    chips = 1 + len(direct)
    rows = handed[0].shape[0]
    total = rows * 2 * chips
    anywhere = pl.BlockSpec(memory_space=pltpu.HBM)
    return pl.pallas_call(
        functools.partial(levels_kernel, live, chips),
        out_shape=[jax.ShapeDtypeStruct((chips, rows // 2, LANES), jnp.bfloat16)] * 4,
        in_specs=[
            pl.BlockSpec(memory_space=pltpu.SMEM),
        ]
        + [pl.BlockSpec(memory_space=pltpu.VMEM)] * (chips + 5),
        out_specs=[pl.BlockSpec(memory_space=pltpu.VMEM)] * 4,
        scratch_shapes=[
            pltpu.VMEM((total, LANES), jnp.bfloat16),
            pltpu.VMEM((total // 8, 8, LANES), jnp.float32),
            pltpu.VMEM((total // 8, 8, LANES), jnp.float32),
            pltpu.VMEM((total, LANES), jnp.bfloat16),
            pltpu.VMEM((live + 2, LANES), jnp.float32),
        ],
        compiler_params=pltpu.CompilerParams(vmem_limit_bytes=GRANT),
        name="levels",
    )(place, angle[None], high, mix, own, *direct, *handed)


def join_kernel(*refs):
    sources, outs = refs[:4], refs[4:]
    chips, half, _ = sources[0].shape
    part = half // SPLIT
    for group in range(1 + SPLIT):
        rows = slice(None) if group == 0 else pl.ds((group - 1) * part, part)
        for ahead in range(chips):
            for other in range(2):
                source = sources[2 * other + (group > 0)]
                outs[group * chips + ahead][other] = source[ahead, rows]


def run_join(arrays):
    chips, half, _ = arrays[0].shape
    in_vmem = pl.BlockSpec(memory_space=pltpu.VMEM)
    sizes = [half] * chips + [half // SPLIT] * (SPLIT * chips)
    outs = pl.pallas_call(
        join_kernel,
        in_specs=[in_vmem] * 4,
        out_specs=[in_vmem] * len(sizes),
        out_shape=[jax.ShapeDtypeStruct((2, size, LANES), jnp.bfloat16) for size in sizes],
        compiler_params=pltpu.CompilerParams(vmem_limit_bytes=LITTLE),
        name="join",
    )(*arrays)
    groups = [list(outs[at * chips : (at + 1) * chips]) for at in range(1 + SPLIT)]
    return groups[0], groups[1:]


def work(rows, depth, columns):
    return pl.CostEstimate(
        flops=2 * rows * depth * columns,
        bytes_accessed=2 * (rows * depth + depth * columns + rows * columns),
        transcendentals=0,
    )


def dot(a, b):
    return jnp.dot(a, b, preferred_element_type=jnp.float32)


def load_kernel(count, *refs):
    place, sources, outs = refs[0], refs[1 : 1 + count], refs[-count - 2 : -2]
    copy_all(list(zip(sources, outs)), refs[-1])
    for at in range(place.shape[0]):
        refs[-2][at] = place[at]


def run_load(place, arrays, after):
    count = len(arrays)
    smem = pl.BlockSpec(memory_space=pltpu.SMEM)
    *loaded, place = pl.pallas_call(
        functools.partial(load_kernel, count),
        in_specs=[smem] + [pl.BlockSpec(memory_space=pltpu.HBM)] * (count + len(after)),
        out_specs=[pl.BlockSpec(memory_space=pltpu.VMEM)] * count + [smem],
        out_shape=[jax.ShapeDtypeStruct(array.shape, array.dtype) for array in (*arrays, place)],
        scratch_shapes=[pltpu.SemaphoreType.DMA((count,))],
        compiler_params=pltpu.CompilerParams(vmem_limit_bytes=LITTLE),
        cost_estimate=pl.CostEstimate(flops=10**11, bytes_accessed=0, transcendentals=0),
        name="load",
    )(place, *arrays, *after)
    return loaded, place


def hidden_kernel(chips, block, place, *refs):
    direct = refs[:chips]
    got, own, fetched = refs[chips], refs[chips + 1 : chips + 3], refs[chips + 3 : chips + 7]
    hidden_ref, act, sems = refs[chips + 7 :]
    side = place[2]
    channels = 2 * chips * LANES
    pairs = []
    for back in range(chips):
        for other in range(2):
            line = line_of(place, back, other) * LANES
            for start, source in (
                (side * channels + line, direct[back].at[other]),
                ((1 - side) * channels + line, got.at[back, other]),
            ):
                lanes = pl.ds(pl.multiple_of(start, LANES), LANES)
                pairs.append((source, act.at[:, lanes]))
    copy_all(pairs, sems)

    core, group = place[1], place[3]
    depth = fetched[0].shape[1]

    def own_side(at, columns):
        return dot(act[...], own[at][:, columns])

    def far_side(at, columns):
        total = None
        for piece, far_group, far_core in zip(fetched, (0, 1, 0, 1), (0, 0, 1, 1)):
            quarter = 2 * (1 - group if far_group else group) + (1 - core if far_core else core)
            rows = pl.ds(pl.multiple_of(quarter * depth, depth), depth)
            term = dot(act[:, rows], piece[at, :, columns])
            total = term if total is None else total + term
        return total

    for whose, product in ((side, own_side), (1 - side, far_side)):

        @pl.loop(0, channels // block)
        def _(j):
            columns = pl.ds(pl.multiple_of(j * block, block), block)
            target = pl.ds(pl.multiple_of(whose * channels + j * block, block), block)
            gated = product(0, columns) * jax.nn.sigmoid(product(1, columns))
            hidden_ref[:, target] = gated.astype(jnp.bfloat16)


def run_hidden(place, direct, got, *weights):
    chips = len(direct)
    rows = got.shape[2]
    width, channels = weights[0].shape
    in_vmem = pl.BlockSpec(memory_space=pltpu.VMEM)
    return pl.pallas_call(
        functools.partial(hidden_kernel, chips, min(512, channels)),
        in_specs=[pl.BlockSpec(memory_space=pltpu.SMEM)]
        + [pl.BlockSpec(memory_space=pltpu.HBM)] * (chips + 1)
        + [in_vmem] * len(weights),
        out_specs=in_vmem,
        scratch_shapes=[
            pltpu.VMEM((rows, width), jnp.bfloat16),
            pltpu.SemaphoreType.DMA((4 * chips,)),
        ],
        out_shape=jax.ShapeDtypeStruct((rows, width), jnp.bfloat16),
        compiler_params=pltpu.CompilerParams(vmem_limit_bytes=LITTLE),
        cost_estimate=work(rows, width, 2 * width),
        name="hidden",
    )(place, *direct, got, *weights)


def send_kernel(place, hidden, mine, twin, out_ref):
    depth = mine.shape[0]
    core = place[1]
    total = None
    for half, weight in ((core, mine), (1 - core, twin)):
        rows = pl.ds(pl.multiple_of(half * depth, depth), depth)
        term = dot(hidden[:, rows], weight[...])
        total = term if total is None else total + term
    out_ref[...] = total.astype(jnp.bfloat16)


def run_send(place, hidden, halves):
    rows, width = hidden.shape
    depth, channels = halves[0].shape
    block = min(512, channels)
    return pl.pallas_call(
        send_kernel,
        grid_spec=pltpu.PrefetchScalarGridSpec(
            num_scalar_prefetch=1,
            grid=(channels // block,),
            in_specs=[pl.BlockSpec((rows, width), lambda j, place: (0, 0))]
            + [pl.BlockSpec((depth, block), lambda j, place: (0, j))] * 2,
            out_specs=pl.BlockSpec((rows, block), lambda j, place: (0, j)),
        ),
        out_shape=jax.ShapeDtypeStruct((rows, channels), jnp.bfloat16),
        compiler_params=pltpu.CompilerParams(vmem_limit_bytes=LITTLE),
        cost_estimate=work(rows, width, channels),
        name="send",
    )(place, hidden, *halves)


def finish_kernel(side, *refs):
    parts, weight, tokens, out_ref = refs[:SPLIT], refs[SPLIT], refs[SPLIT + 1], refs[SPLIT + 2]
    rows = parts[0].shape[0]
    for q in range(SPLIT):
        at = pl.ds(q * rows, rows)
        made = dot(parts[q][...], weight[...])
        out_ref[at, :] = (made + tokens[at, :].astype(jnp.float32)).astype(jnp.bfloat16)


def run_finish(side, parts, weight, tokens):
    rows, width = parts[0].shape
    channels = weight.shape[1]
    block = min(512, channels)
    return pl.pallas_call(
        finish_kernel,
        grid_spec=pltpu.PrefetchScalarGridSpec(
            num_scalar_prefetch=1,
            grid=(channels // block,),
            in_specs=[pl.BlockSpec((rows, width), lambda j, side: (0, 0))] * SPLIT
            + [
                pl.BlockSpec((width, block), lambda j, side: (0, j)),
                pl.BlockSpec((SPLIT * rows, block), lambda j, side: (side[0], j)),
            ],
            out_specs=pl.BlockSpec((SPLIT * rows, block), lambda j, side: (side[0], j)),
        ),
        out_shape=jax.ShapeDtypeStruct(tokens.shape, jnp.bfloat16),
        compiler_params=pltpu.CompilerParams(vmem_limit_bytes=GRANT),
        cost_estimate=work(SPLIT * rows, width, channels),
        name="finish",
    )(side, *parts, weight, tokens)


def add_kernel(q, side, got, tokens, kept, out_ref, before, after, loads, stores):
    rows = got.shape[0]
    part = rows // PARTS
    start = (SPLIT * (1 - side[0]) + q) * rows

    def here(p):
        return pl.ds(pl.multiple_of(start + p * part, part), part)

    def piece(p):
        return pl.ds(p * part, part)

    def load(p):
        return pltpu.make_async_copy(tokens.at[here(p)], before.at[piece(p)], loads.at[p])

    def store(p):
        return pltpu.make_async_copy(after.at[piece(p)], out_ref.at[here(p)], stores.at[p])

    for p in range(PARTS):
        load(p).start()
    for p in range(PARTS):
        load(p).wait()
        added = got[piece(p), :].astype(jnp.float32) + before[piece(p), :].astype(jnp.float32)
        after[piece(p), :] = added.astype(jnp.bfloat16)
        store(p).start()
    for p in range(PARTS):
        store(p).wait()


def add_far(side, q, got, tokens, result):
    anywhere = pl.BlockSpec(memory_space=pl.ANY)
    return pl.pallas_call(
        functools.partial(add_kernel, q),
        in_specs=[
            pl.BlockSpec(memory_space=pltpu.SMEM),
            pl.BlockSpec(memory_space=pltpu.VMEM),
            anywhere,
            anywhere,
        ],
        out_specs=anywhere,
        out_shape=jax.ShapeDtypeStruct(tokens.shape, jnp.bfloat16),
        input_output_aliases={3: 0},
        scratch_shapes=[
            pltpu.VMEM(got.shape, got.dtype),
            pltpu.VMEM(got.shape, got.dtype),
            pltpu.SemaphoreType.DMA((PARTS,)),
            pltpu.SemaphoreType.DMA((PARTS,)),
        ],
        compiler_params=pltpu.CompilerParams(vmem_limit_bytes=LITTLE),
        name="add_far",
    )(side, got, tokens, result)


def swap(array, axis):
    return lax.ppermute(array, axis, [(0, 1), (1, 0)])


def ahead(array, offset):
    chips = lax.axis_size("seq")
    return lax.ppermute(array, "seq", [(j, (j + offset) % chips) for j in range(chips)])


def anchor_kernel(*refs):
    refs[-1][...] = jnp.zeros(refs[-1].shape, refs[-1].dtype)


def anchor(after):
    return pl.pallas_call(
        anchor_kernel,
        in_specs=[pl.BlockSpec(memory_space=pltpu.HBM)] * len(after),
        out_specs=pl.BlockSpec(memory_space=pltpu.VMEM),
        out_shape=jax.ShapeDtypeStruct((8, LANES), jnp.float32),
        compiler_params=pltpu.CompilerParams(vmem_limit_bytes=LITTLE),
        cost_estimate=pl.CostEstimate(flops=10**11, bytes_accessed=0, transcendentals=0),
        name="anchor",
    )(*after)


def others_kernel(place, *refs):
    lanes = pl.ds(pl.multiple_of((1 - place[1]) * LANES, LANES), LANES)
    for at, block in enumerate(refs[:-1]):
        refs[-1][at] = block[:, lanes]


def run_others(place, blocks):
    in_vmem = pl.BlockSpec(memory_space=pltpu.VMEM)
    rows = blocks[0].shape[0]
    return pl.pallas_call(
        others_kernel,
        in_specs=[pl.BlockSpec(memory_space=pltpu.SMEM)] + [in_vmem] * len(blocks),
        out_specs=in_vmem,
        out_shape=jax.ShapeDtypeStruct((len(blocks), rows, LANES), blocks[0].dtype),
        compiler_params=pltpu.CompilerParams(vmem_limit_bytes=LITTLE),
        cost_estimate=pl.CostEstimate(flops=HOP, bytes_accessed=0, transcendentals=0),
        name="others",
    )(place, *blocks)


def by_tokens(tokens, low_angle, high_taps, level_mix, w_value, w_gate, out_weight):
    rows, channels = tokens.shape
    chips = lax.axis_size("seq")
    narrow = channels // (2 * chips)
    chip, core = lax.axis_index("seq"), lax.axis_index("sub")
    side, group = lax.axis_index("chan"), lax.axis_index("groups")
    live = min(LEVELS, (rows * 2 * chips - 1).bit_length())
    order = sorted(range(1, chips), key=lambda s: abs(2 * s - chips))
    place = jnp.stack([chip, core, side, group, chips]).astype(jnp.int32)

    pair = run_pair(w_value, w_gate)
    tokens, pair = lax.optimization_barrier((tokens, pair))
    def columns(back, first, count):
        start = ((chip - back) % chips * 2 + first) * narrow
        return lax.dynamic_slice_in_dim(tokens, start, count * narrow, 1)

    blocks = [columns(-s, 0, 2) for s in range(1, chips)]
    mine, other = columns(0, core, 1), columns(0, 1 - core, 1)
    blocks, out_piece = lax.optimization_barrier((blocks, out_weight))
    direct = [None] * chips
    for s in order:
        direct[s] = ahead(blocks[s - 1], s)
    handed = [swap(other, "sub"), swap(run_others(place, direct[1:]), "sub")]

    depth = w_value.shape[0] // 4
    half = lax.dynamic_slice_in_dim(out_piece, core * 2 * depth, 2 * depth, 0)
    pair_first = swap(pair, "chan")
    direct, pair_first, half = lax.optimization_barrier((direct, pair_first, half))
    pair_second = swap(pair_first, "groups")
    half_first = swap(half, "chan")
    pair_third = swap(pair_first, "sub")

    *kept, given_far, given_near = run_filter(
        place, low_angle, high_taps, level_mix, mine, direct[1:], handed, live
    )

    far, near = run_join([*kept, swap(given_far, "sub"), swap(given_near, "sub")])
    far, pair_third = lax.optimization_barrier((far, pair_third))
    far_got = [far[0]] + [None] * (chips - 1)
    for s in order:
        far_got[s] = ahead(far[s], s)

    def exchange(backs):
        return (
            swap(jnp.stack([far_got[back][0] for back in backs]), "chan"),
            cross(jnp.stack([far_got[back][1] for back in backs])),
        )

    both = anchor([pair_second, half_first])
    far_got, pair_second, half_first, both = lax.optimization_barrier(
        (far_got, pair_second, half_first, both)
    )
    far_got = list(far_got)
    near_got = [[part[0]] + [None] * (chips - 1) for part in near]
    for s in order:
        near[0][s], far_got[s] = lax.optimization_barrier((near[0][s], far_got[s]))
        near_got[0][s] = ahead(near[0][s], s)
    rows = near[0][0].shape[1]

    def exchange(q, before):
        part = slice(q * rows, (q + 1) * rows)
        mine, before = lax.optimization_barrier(
            (jnp.stack([block[:, part] for block in far_got]), before)
        )
        return swap(mine, "chan")

    got = [exchange(q, half_first) for q in range(SPLIT)]
    near_got[0][order[0]], pair_second = lax.optimization_barrier(
        (near_got[0][order[0]], pair_second)
    )
    pair_fourth = swap(pair_second, "sub")
    loaded, place = run_load(
        place, [w_value, w_gate, pair_first, pair_second, pair_third], far_got[1:]
    )
    near_got[0], got[0], place, pair_fourth, half_first = lax.optimization_barrier(
        (near_got[0], got[0], place, pair_fourth, half_first)
    )
    half_second = swap(half_first, "sub")
    loaded.append(pair_fourth)
    which = place[2:3]
    hidden, returned = [], []
    for q in range(SPLIT):
        if q + 1 < SPLIT:
            for s in order:
                near[q + 1][s], near_got[q][s] = lax.optimization_barrier(
                    (near[q + 1][s], near_got[q][s])
                )
                near_got[q + 1][s] = ahead(near[q + 1][s], s)
        made = run_hidden(place, near_got[q], got[q], *loaded)
        sent = run_send(place, made, [half_first, half_second])
        if q + 1 < SPLIT:
            near_got[q + 1], got[q + 1], sent = lax.optimization_barrier(
                (near_got[q + 1], got[q + 1], sent)
            )
        hidden.append(made)
        returned.append(swap(sent, "chan"))
    hidden, returned[0] = lax.optimization_barrier((hidden, returned[0]))
    result = run_finish(which, hidden, out_weight, tokens)
    for q in range(SPLIT):
        result = add_far(which, q, returned[q], tokens, result)
    return result


def solution(mesh):
    def shards(tokens, *rest):
        ways = mesh.shape["seq"] * mesh.shape["sub"]
        pairs = all(mesh.shape[name] == 2 for name in ("groups", "chan", "sub"))
        rows, channels = tokens.shape
        fits = channels == ways * LANES and rows % 64 == 0
        fits = fits and rows * ways == 8 * WIDE * RUN and rest[3].shape[0] % 512 == 0
        return (by_tokens if pairs and fits else general)(tokens, *rest)

    return jax.shard_map(
        shards,
        mesh=mesh,
        in_specs=(
            P(("groups", "seq", "sub"), "chan"),
            P("chan"),
            P(None, "chan"),
            P(None, "chan"),
            P(None, "chan"),
            P(None, "chan"),
            P(None, "chan"),
        ),
        out_specs=P(("groups", "seq", "sub"), "chan"),
        check_vma=False,
    )
```

```python
import functools

import jax
import jax.numpy as jnp
from jax import lax
from jax.experimental import pallas as pl
from jax.experimental.pallas import tpu as pltpu
from jax.sharding import PartitionSpec as P

LEVELS = 15
LANES = 128
SPLIT = 2
RUN = 16
MIDDLE = 8
WIDE = 64
LINE = ("seq", "sub")
GRANT = 16 * 2**20
LITTLE = 12 * 2**20
LARGE = 54 * 2**20
PARTS = 4
HOP = 5*10**9


def run_levels(stream, shifter, low0, low1, high0, high1, mix):
    mixed = mix[LEVELS + 1] * stream
    for level in range(LEVELS):
        shifted = shifter(stream, 2**level)
        high = high0 * stream + high1 * shifted
        stream = low0 * stream + low1 * shifted
        mixed = mixed + mix[level] * high
    return mixed + mix[LEVELS] * stream


def general(tokens, low_angle, high_taps, level_mix, w_value, w_gate, out_weight):
    rows = tokens.shape[0]
    channels = tokens.shape[1]
    ways = lax.axis_size(LINE)
    total = rows * ways
    narrow = channels // ways
    place = lax.axis_index(LINE) * narrow
    columns = lax.all_to_all(tokens.T, LINE, split_axis=0, concat_axis=1, tiled=True)
    angle = lax.dynamic_slice_in_dim(low_angle, place, narrow, 0)[:, None]
    high_pair = lax.dynamic_slice_in_dim(high_taps, place, narrow, 1)[:, :, None]
    mix = lax.dynamic_slice_in_dim(level_mix, place, narrow, 1)[:, :, None]

    def shifter(stream, reach):
        if reach >= total:
            return jnp.zeros_like(stream)
        return jnp.concatenate(
            [jnp.zeros((stream.shape[0], reach), jnp.float32), stream[:, : total - reach]], 1
        )

    mixed = run_levels(
        columns.astype(jnp.float32),
        shifter,
        jnp.cos(angle),
        jnp.sin(angle),
        high_pair[0],
        high_pair[1],
        mix,
    )
    filtered = jax.nn.gelu(mixed).astype(jnp.bfloat16)
    activated = lax.all_to_all(filtered, LINE, split_axis=1, concat_axis=0, tiled=True).T
    piece = lax.all_gather(activated, "chan", axis=1, tiled=True)
    value = jnp.dot(piece, w_value, preferred_element_type=jnp.float32)
    gate = jnp.dot(piece, w_gate, preferred_element_type=jnp.float32)
    hidden = (value * jax.nn.sigmoid(gate)).astype(jnp.bfloat16)
    projected = jnp.dot(
        lax.all_gather(hidden, "chan", axis=1, tiled=True),
        out_weight,
        preferred_element_type=jnp.float32,
    )
    return (projected + tokens.astype(jnp.float32)).astype(jnp.bfloat16)


def coefficients(live, lanes, angle_ref, high_ref, mix_ref, out_ref):
    low0, low1 = jnp.cos(angle_ref[:, lanes]), jnp.sin(angle_ref[:, lanes])
    high0, high1 = high_ref[0:1, lanes], high_ref[1:2, lanes]
    power = jnp.ones_like(low0)
    for level in range(live + 1):
        weight = jnp.zeros_like(low0)
        if level < live:
            weight = weight + mix_ref[level : level + 1, lanes] * (high0 - high1 * low0 / low1)
        if level > 0:
            weight = weight + mix_ref[level - 1 : level, lanes] * high1 / low1
        if level == live:
            scale = jnp.ones_like(low0)
            for rest in range(live, LEVELS):
                weight = weight + mix_ref[rest : rest + 1, lanes] * high0 * scale
                scale = scale * low0
            weight = weight + mix_ref[LEVELS : LEVELS + 1, lanes] * scale
        weight = weight * power
        if level == 0:
            weight = weight + mix_ref[LEVELS + 1 : LEVELS + 2, lanes]
        out_ref[level : level + 1, :] = weight
        power = power * low0
    out_ref[live + 1 : live + 2, :] = low1 / low0


def advance(stream, tail, ratio):
    reach = tail.shape[0]
    shifted = jnp.concatenate([tail, stream[: stream.shape[0] - reach]], 0)
    return stream + ratio * shifted


def copy_all(pairs, sems, meanwhile=None):
    copies = [pltpu.make_async_copy(*pair, sems.at[at]) for at, pair in enumerate(pairs)]
    for copy in copies:
        copy.start()
    if meanwhile:
        meanwhile()
    for copy in copies:
        copy.wait()


def line_of(place, back, other):
    chips = place[4]
    core = 1 - place[1] if other else place[1]
    return lax.rem(place[0] - back + chips, chips) * 2 + core


def pair_kernel(value, gate, pair, sems):
    core, group = lax.axis_index("sub"), lax.axis_index("groups")
    depth = pair.shape[1]
    part = depth // PARTS
    pairs = []
    for at, weight in enumerate((value, gate)):
        for p in range(PARTS):
            here = pl.ds(pl.multiple_of((2 * group + core) * depth + p * part, part), part)
            pairs.append((weight.at[here], pair.at[at, pl.ds(p * part, part)]))
    copy_all(pairs, sems)


def run_pair(value, gate):
    width, channels = value.shape
    return pl.pallas_call(
        pair_kernel,
        in_specs=[pl.BlockSpec(memory_space=pltpu.HBM)] * 2,
        out_specs=pl.BlockSpec(memory_space=pltpu.VMEM),
        out_shape=jax.ShapeDtypeStruct((2, width // 4, channels), value.dtype),
        scratch_shapes=[pltpu.SemaphoreType.DMA((2 * PARTS,))],
        compiler_params=pltpu.CompilerParams(vmem_limit_bytes=LARGE),
        name="pair",
    )(value, gate)


def levels_kernel(live, chips, place, angle_ref, high_ref, mix_ref, own, *refs):
    direct = refs[: chips - 1]
    handed = refs[chips - 1 : chips + 1]
    outs = refs[chips + 1 : chips + 5]
    tokens, stream_ref, mixed_ref, act_ref, coef_ref = refs[chips + 5 :]
    side = place[2]
    rows = own.shape[0]
    units = rows * 2 * chips // 8

    def block(line):
        return pl.ds(pl.multiple_of(line * rows, rows), rows)

    columns = pl.ds(pl.multiple_of(line_of(place, 0, 0) * LANES, LANES), LANES)
    lanes = pl.ds(pl.multiple_of(place[1] * LANES, LANES), LANES)
    for back in range(chips):
        mine = direct[back - 1][:, lanes] if back else own[...]
        tokens[block(line_of(place, back, 0)), :] = mine
        tokens[block(line_of(place, back, 1)), :] = handed[1][back - 1] if back else handed[0][...]
    coefficients(live, columns, angle_ref, high_ref, mix_ref, coef_ref)

    def whole(row):
        return jnp.broadcast_to(coef_ref[row : row + 1, :], (8, LANES))[None]

    def zero(n):
        return jnp.zeros((n, 8, LANES), jnp.float32)

    ratio = whole(live + 1)

    def first(i, carry):
        start = pl.multiple_of(i * RUN * 8, RUN * 8)
        x = tokens[pl.ds(start, RUN * 8), :].astype(jnp.float32).reshape(RUN, 8, LANES)
        mixed = whole(0) * x
        row = lax.broadcasted_iota(jnp.int32, (1, 8, LANES), 1)
        kept = []
        for level, tail in enumerate(carry):
            kept.append(x[RUN - tail.shape[0] :])
            if level < 3:
                turned = pltpu.roll(jnp.concatenate([tail, x], 0), 2**level, 1)
                x = x + ratio * jnp.where(row < 2**level, turned[:RUN], turned[1:])
            else:
                x = advance(x, tail, ratio)
            mixed = mixed + whole(level + 1) * x
        stream_ref[pl.ds(i * RUN, RUN)] = x
        mixed_ref[pl.ds(i * RUN, RUN)] = mixed
        return tuple(kept)

    lax.fori_loop(0, units // RUN, first, tuple(zero(n) for n in (1, 1, 1, 1, 2, 4)))

    stream = stream_ref.reshape(units // MIDDLE, MIDDLE, 8, LANES)
    total = mixed_ref.reshape(units // MIDDLE, MIDDLE, 8, LANES)
    steps = units // MIDDLE // RUN

    def second(t, carry):
        q = t // steps
        i = t % steps
        x = stream[pl.ds(i * RUN, RUN), q]
        mixed = total[pl.ds(i * RUN, RUN), q]
        keep = jnp.where(i > 0, 1.0, 0.0)
        kept = []
        for level, tail in enumerate(carry):
            kept.append(x[RUN - tail.shape[0] :])
            x = advance(x, tail * keep, ratio)
            mixed = mixed + whole(level + 7) * x
        stream[pl.ds(i * RUN, RUN), q] = x
        total[pl.ds(i * RUN, RUN), q] = mixed
        return tuple(kept)

    lax.fori_loop(0, MIDDLE * steps, second, tuple(zero(n) for n in (1, 2, 4)))

    stream_wide = stream_ref.reshape(units // WIDE, WIDE, 8, LANES)
    total_wide = mixed_ref.reshape(units // WIDE, WIDE, 8, LANES)
    act_wide = act_ref.reshape(units // WIDE, WIDE // 2, 16, LANES)

    def third(pair, _):
        halves = []
        for odd in range(2):
            x = stream_wide[:, pair * 2 + odd]
            mixed = total_wide[:, pair * 2 + odd]
            for level in range(9, live):
                reach = 2 ** (level - 9)
                x = jnp.concatenate([x[:reach], x[reach:] + ratio * x[:-reach]], 0)
                mixed = mixed + whole(level + 1) * x
            halves.append(jax.nn.gelu(mixed))
        act_wide[:, pair] = jnp.concatenate(halves, 1).astype(jnp.bfloat16)
        return 0

    half = rows // 2
    lax.fori_loop(0, WIDE // 2, third, 0)
    for ahead in range(chips):
        for other in range(2):
            start = line_of(place, -ahead, other) * rows
            for at, which in enumerate((1 - side, side)):
                begin = pl.multiple_of(start + which * half, half)
                outs[2 * other + at][ahead] = act_ref[pl.ds(begin, half), :]


def run_filter(place, angle, high, mix, own, direct, handed, live):
    chips = 1 + len(direct)
    rows = handed[0].shape[0]
    total = rows * 2 * chips
    anywhere = pl.BlockSpec(memory_space=pltpu.HBM)
    return pl.pallas_call(
        functools.partial(levels_kernel, live, chips),
        out_shape=[jax.ShapeDtypeStruct((chips, rows // 2, LANES), jnp.bfloat16)] * 4,
        in_specs=[
            pl.BlockSpec(memory_space=pltpu.SMEM),
        ]
        + [pl.BlockSpec(memory_space=pltpu.VMEM)] * (chips + 5),
        out_specs=[pl.BlockSpec(memory_space=pltpu.VMEM)] * 4,
        scratch_shapes=[
            pltpu.VMEM((total, LANES), jnp.bfloat16),
            pltpu.VMEM((total // 8, 8, LANES), jnp.float32),
            pltpu.VMEM((total // 8, 8, LANES), jnp.float32),
            pltpu.VMEM((total, LANES), jnp.bfloat16),
            pltpu.VMEM((live + 2, LANES), jnp.float32),
        ],
        compiler_params=pltpu.CompilerParams(vmem_limit_bytes=GRANT),
        name="levels",
    )(place, angle[None], high, mix, own, *direct, *handed)


def join_kernel(*refs):
    sources, outs = refs[:4], refs[4:]
    chips, half, _ = sources[0].shape
    part = half // SPLIT
    for group in range(1 + SPLIT):
        rows = slice(None) if group == 0 else pl.ds((group - 1) * part, part)
        for ahead in range(chips):
            for other in range(2):
                source = sources[2 * other + (group > 0)]
                outs[group * chips + ahead][other] = source[ahead, rows]


def run_join(arrays):
    chips, half, _ = arrays[0].shape
    in_vmem = pl.BlockSpec(memory_space=pltpu.VMEM)
    sizes = [half] * chips + [half // SPLIT] * (SPLIT * chips)
    outs = pl.pallas_call(
        join_kernel,
        in_specs=[in_vmem] * 4,
        out_specs=[in_vmem] * len(sizes),
        out_shape=[jax.ShapeDtypeStruct((2, size, LANES), jnp.bfloat16) for size in sizes],
        compiler_params=pltpu.CompilerParams(vmem_limit_bytes=LITTLE),
        name="join",
    )(*arrays)
    groups = [list(outs[at * chips : (at + 1) * chips]) for at in range(1 + SPLIT)]
    return groups[0], groups[1:]


def work(rows, depth, columns):
    return pl.CostEstimate(
        flops=2 * rows * depth * columns,
        bytes_accessed=2 * (rows * depth + depth * columns + rows * columns),
        transcendentals=0,
    )


def dot(a, b):
    return jnp.dot(a, b, preferred_element_type=jnp.float32)


def load_kernel(count, *refs):
    place, sources, outs = refs[0], refs[1 : 1 + count], refs[-count - 2 : -2]
    copy_all(list(zip(sources, outs)), refs[-1])
    for at in range(place.shape[0]):
        refs[-2][at] = place[at]


def run_load(place, arrays, after):
    count = len(arrays)
    smem = pl.BlockSpec(memory_space=pltpu.SMEM)
    *loaded, place = pl.pallas_call(
        functools.partial(load_kernel, count),
        in_specs=[smem] + [pl.BlockSpec(memory_space=pltpu.HBM)] * (count + len(after)),
        out_specs=[pl.BlockSpec(memory_space=pltpu.VMEM)] * count + [smem],
        out_shape=[jax.ShapeDtypeStruct(array.shape, array.dtype) for array in (*arrays, place)],
        scratch_shapes=[pltpu.SemaphoreType.DMA((count,))],
        compiler_params=pltpu.CompilerParams(vmem_limit_bytes=LITTLE),
        cost_estimate=pl.CostEstimate(flops=10**11, bytes_accessed=0, transcendentals=0),
        name="load",
    )(place, *arrays, *after)
    return loaded, place


def hidden_kernel(chips, block, place, *refs):
    direct = refs[:chips]
    got, own, fetched = refs[chips], refs[chips + 1 : chips + 3], refs[chips + 3 : chips + 7]
    hidden_ref, act, sems = refs[chips + 7 :]
    side = place[2]
    channels = 2 * chips * LANES
    pairs = []
    for back in range(chips):
        for other in range(2):
            line = line_of(place, back, other) * LANES
            for start, source in (
                (side * channels + line, direct[back].at[other]),
                ((1 - side) * channels + line, got.at[back, other]),
            ):
                lanes = pl.ds(pl.multiple_of(start, LANES), LANES)
                pairs.append((source, act.at[:, lanes]))
    copy_all(pairs, sems)

    core, group = place[1], place[3]
    depth = fetched[0].shape[1]

    def own_side(at, columns):
        return dot(act[...], own[at][:, columns])

    def far_side(at, columns):
        total = None
        for piece, far_group, far_core in zip(fetched, (0, 1, 0, 1), (0, 0, 1, 1)):
            quarter = 2 * (1 - group if far_group else group) + (1 - core if far_core else core)
            rows = pl.ds(pl.multiple_of(quarter * depth, depth), depth)
            term = dot(act[:, rows], piece[at, :, columns])
            total = term if total is None else total + term
        return total

    for whose, product in ((side, own_side), (1 - side, far_side)):

        @pl.loop(0, channels // block)
        def _(j):
            columns = pl.ds(pl.multiple_of(j * block, block), block)
            target = pl.ds(pl.multiple_of(whose * channels + j * block, block), block)
            gated = product(0, columns) * jax.nn.sigmoid(product(1, columns))
            hidden_ref[:, target] = gated.astype(jnp.bfloat16)


def run_hidden(place, direct, got, *weights):
    chips = len(direct)
    rows = got.shape[2]
    width, channels = weights[0].shape
    in_vmem = pl.BlockSpec(memory_space=pltpu.VMEM)
    return pl.pallas_call(
        functools.partial(hidden_kernel, chips, min(512, channels)),
        in_specs=[pl.BlockSpec(memory_space=pltpu.SMEM)]
        + [pl.BlockSpec(memory_space=pltpu.HBM)] * (chips + 1)
        + [in_vmem] * len(weights),
        out_specs=in_vmem,
        scratch_shapes=[
            pltpu.VMEM((rows, width), jnp.bfloat16),
            pltpu.SemaphoreType.DMA((4 * chips,)),
        ],
        out_shape=jax.ShapeDtypeStruct((rows, width), jnp.bfloat16),
        compiler_params=pltpu.CompilerParams(vmem_limit_bytes=LITTLE),
        cost_estimate=work(rows, width, 2 * width),
        name="hidden",
    )(place, *direct, got, *weights)


def send_kernel(place, hidden, mine, twin, out_ref):
    depth = mine.shape[0]
    core = place[1]
    total = None
    for half, weight in ((core, mine), (1 - core, twin)):
        rows = pl.ds(pl.multiple_of(half * depth, depth), depth)
        term = dot(hidden[:, rows], weight[...])
        total = term if total is None else total + term
    out_ref[...] = total.astype(jnp.bfloat16)


def run_send(place, hidden, halves):
    rows, width = hidden.shape
    depth, channels = halves[0].shape
    block = min(512, channels)
    return pl.pallas_call(
        send_kernel,
        grid_spec=pltpu.PrefetchScalarGridSpec(
            num_scalar_prefetch=1,
            grid=(channels // block,),
            in_specs=[pl.BlockSpec((rows, width), lambda j, place: (0, 0))]
            + [pl.BlockSpec((depth, block), lambda j, place: (0, j))] * 2,
            out_specs=pl.BlockSpec((rows, block), lambda j, place: (0, j)),
        ),
        out_shape=jax.ShapeDtypeStruct((rows, channels), jnp.bfloat16),
        compiler_params=pltpu.CompilerParams(vmem_limit_bytes=LITTLE),
        cost_estimate=work(rows, width, channels),
        name="send",
    )(place, hidden, *halves)


def finish_kernel(side, *refs):
    parts, weight, tokens, out_ref = refs[:SPLIT], refs[SPLIT], refs[SPLIT + 1], refs[SPLIT + 2]
    rows = parts[0].shape[0]
    for q in range(SPLIT):
        at = pl.ds(q * rows, rows)
        made = dot(parts[q][...], weight[...])
        out_ref[at, :] = (made + tokens[at, :].astype(jnp.float32)).astype(jnp.bfloat16)


def run_finish(side, parts, weight, tokens):
    rows, width = parts[0].shape
    channels = weight.shape[1]
    block = min(512, channels)
    return pl.pallas_call(
        finish_kernel,
        grid_spec=pltpu.PrefetchScalarGridSpec(
            num_scalar_prefetch=1,
            grid=(channels // block,),
            in_specs=[pl.BlockSpec((rows, width), lambda j, side: (0, 0))] * SPLIT
            + [
                pl.BlockSpec((width, block), lambda j, side: (0, j)),
                pl.BlockSpec((SPLIT * rows, block), lambda j, side: (side[0], j)),
            ],
            out_specs=pl.BlockSpec((SPLIT * rows, block), lambda j, side: (side[0], j)),
        ),
        out_shape=jax.ShapeDtypeStruct(tokens.shape, jnp.bfloat16),
        compiler_params=pltpu.CompilerParams(vmem_limit_bytes=GRANT),
        cost_estimate=work(SPLIT * rows, width, channels),
        name="finish",
    )(side, *parts, weight, tokens)


def add_kernel(q, side, got, tokens, kept, out_ref, before, after, loads, stores):
    rows = got.shape[0]
    part = rows // PARTS
    start = (SPLIT * (1 - side[0]) + q) * rows

    def here(p):
        return pl.ds(pl.multiple_of(start + p * part, part), part)

    def piece(p):
        return pl.ds(p * part, part)

    def load(p):
        return pltpu.make_async_copy(tokens.at[here(p)], before.at[piece(p)], loads.at[p])

    def store(p):
        return pltpu.make_async_copy(after.at[piece(p)], out_ref.at[here(p)], stores.at[p])

    for p in range(PARTS):
        load(p).start()
    for p in range(PARTS):
        load(p).wait()
        added = got[piece(p), :].astype(jnp.float32) + before[piece(p), :].astype(jnp.float32)
        after[piece(p), :] = added.astype(jnp.bfloat16)
        store(p).start()
    for p in range(PARTS):
        store(p).wait()


def add_far(side, q, got, tokens, result):
    anywhere = pl.BlockSpec(memory_space=pl.ANY)
    return pl.pallas_call(
        functools.partial(add_kernel, q),
        in_specs=[
            pl.BlockSpec(memory_space=pltpu.SMEM),
            pl.BlockSpec(memory_space=pltpu.VMEM),
            anywhere,
            anywhere,
        ],
        out_specs=anywhere,
        out_shape=jax.ShapeDtypeStruct(tokens.shape, jnp.bfloat16),
        input_output_aliases={3: 0},
        scratch_shapes=[
            pltpu.VMEM(got.shape, got.dtype),
            pltpu.VMEM(got.shape, got.dtype),
            pltpu.SemaphoreType.DMA((PARTS,)),
            pltpu.SemaphoreType.DMA((PARTS,)),
        ],
        compiler_params=pltpu.CompilerParams(vmem_limit_bytes=LITTLE),
        name="add_far",
    )(side, got, tokens, result)


def swap(array, axis):
    return lax.ppermute(array, axis, [(0, 1), (1, 0)])


def ahead(array, offset):
    chips = lax.axis_size("seq")
    return lax.ppermute(array, "seq", [(j, (j + offset) % chips) for j in range(chips)])


def anchor_kernel(*refs):
    refs[-1][...] = jnp.zeros(refs[-1].shape, refs[-1].dtype)


def anchor(after):
    return pl.pallas_call(
        anchor_kernel,
        in_specs=[pl.BlockSpec(memory_space=pltpu.HBM)] * len(after),
        out_specs=pl.BlockSpec(memory_space=pltpu.VMEM),
        out_shape=jax.ShapeDtypeStruct((8, LANES), jnp.float32),
        compiler_params=pltpu.CompilerParams(vmem_limit_bytes=LITTLE),
        cost_estimate=pl.CostEstimate(flops=10**11, bytes_accessed=0, transcendentals=0),
        name="anchor",
    )(*after)


def others_kernel(place, *refs):
    lanes = pl.ds(pl.multiple_of((1 - place[1]) * LANES, LANES), LANES)
    for at, block in enumerate(refs[:-1]):
        refs[-1][at] = block[:, lanes]


def run_others(place, blocks):
    in_vmem = pl.BlockSpec(memory_space=pltpu.VMEM)
    rows = blocks[0].shape[0]
    return pl.pallas_call(
        others_kernel,
        in_specs=[pl.BlockSpec(memory_space=pltpu.SMEM)] + [in_vmem] * len(blocks),
        out_specs=in_vmem,
        out_shape=jax.ShapeDtypeStruct((len(blocks), rows, LANES), blocks[0].dtype),
        compiler_params=pltpu.CompilerParams(vmem_limit_bytes=LITTLE),
        cost_estimate=pl.CostEstimate(flops=HOP, bytes_accessed=0, transcendentals=0),
        name="others",
    )(place, *blocks)


def by_tokens(tokens, low_angle, high_taps, level_mix, w_value, w_gate, out_weight):
    rows, channels = tokens.shape
    chips = lax.axis_size("seq")
    narrow = channels // (2 * chips)
    chip, core = lax.axis_index("seq"), lax.axis_index("sub")
    side, group = lax.axis_index("chan"), lax.axis_index("groups")
    live = min(LEVELS, (rows * 2 * chips - 1).bit_length())
    order = sorted(range(1, chips), key=lambda s: abs(2 * s - chips))
    place = jnp.stack([chip, core, side, group, chips]).astype(jnp.int32)

    pair = run_pair(w_value, w_gate)
    tokens, pair = lax.optimization_barrier((tokens, pair))
    def columns(back, first, count):
        start = ((chip - back) % chips * 2 + first) * narrow
        return lax.dynamic_slice_in_dim(tokens, start, count * narrow, 1)

    blocks = [columns(-s, 0, 2) for s in range(1, chips)]
    mine, other = columns(0, core, 1), columns(0, 1 - core, 1)
    blocks, out_piece = lax.optimization_barrier((blocks, out_weight))
    direct = [None] * chips
    for s in order:
        direct[s] = ahead(blocks[s - 1], s)
    handed = [swap(other, "sub"), swap(run_others(place, direct[1:]), "sub")]

    depth = w_value.shape[0] // 4
    half = lax.dynamic_slice_in_dim(out_piece, core * 2 * depth, 2 * depth, 0)
    pair_first = swap(pair, "chan")
    direct[2], pair_first, half = lax.optimization_barrier((direct[2], pair_first, half))
    pair_second = swap(pair_first, "groups")
    half_first = swap(half, "chan")
    pair_third = swap(pair_first, "sub")

    *kept, given_far, given_near = run_filter(
        place, low_angle, high_taps, level_mix, mine, direct[1:], handed, live
    )

    far, near = run_join([*kept, swap(given_far, "sub"), swap(given_near, "sub")])
    far, pair_third = lax.optimization_barrier((far, pair_third))
    far_got = [far[0]] + [None] * (chips - 1)
    for s in order:
        far_got[s] = ahead(far[s], s)

    def exchange(backs):
        return (
            swap(jnp.stack([far_got[back][0] for back in backs]), "chan"),
            cross(jnp.stack([far_got[back][1] for back in backs])),
        )

    both = anchor([pair_second, half_first])
    far_got, pair_second, half_first, both = lax.optimization_barrier(
        (far_got, pair_second, half_first, both)
    )
    far_got = list(far_got)
    near_got = [[part[0]] + [None] * (chips - 1) for part in near]
    for s in order:
        near[0][s], far_got[s] = lax.optimization_barrier((near[0][s], far_got[s]))
        near_got[0][s] = ahead(near[0][s], s)
    rows = near[0][0].shape[1]

    def exchange(q, before):
        part = slice(q * rows, (q + 1) * rows)
        mine, before = lax.optimization_barrier(
            (jnp.stack([block[:, part] for block in far_got]), before)
        )
        return swap(mine, "chan")

    got = [exchange(q, half_first) for q in range(SPLIT)]
    near_got[0][order[0]], pair_second = lax.optimization_barrier(
        (near_got[0][order[0]], pair_second)
    )
    pair_fourth = swap(pair_second, "sub")
    loaded, place = run_load(
        place, [w_value, w_gate, pair_first, pair_second, pair_third], far_got[1:]
    )
    near_got[0], got[0], place, pair_fourth, half_first = lax.optimization_barrier(
        (near_got[0], got[0], place, pair_fourth, half_first)
    )
    half_second = swap(half_first, "sub")
    loaded.append(pair_fourth)
    which = place[2:3]
    hidden, returned = [], []
    for q in range(SPLIT):
        if q + 1 < SPLIT:
            for s in order:
                near[q + 1][s], near_got[q][s] = lax.optimization_barrier(
                    (near[q + 1][s], near_got[q][s])
                )
                near_got[q + 1][s] = ahead(near[q + 1][s], s)
        made = run_hidden(place, near_got[q], got[q], *loaded)
        sent = run_send(place, made, [half_first, half_second])
        if q + 1 < SPLIT:
            near_got[q + 1], got[q + 1], sent = lax.optimization_barrier(
                (near_got[q + 1], got[q + 1], sent)
            )
        hidden.append(made)
        returned.append(swap(sent, "chan"))
    hidden, returned[0] = lax.optimization_barrier((hidden, returned[0]))
    result = run_finish(which, hidden, out_weight, tokens)
    for q in range(SPLIT):
        result = add_far(which, q, returned[q], tokens, result)
    return result


def solution(mesh):
    def shards(tokens, *rest):
        ways = mesh.shape["seq"] * mesh.shape["sub"]
        pairs = all(mesh.shape[name] == 2 for name in ("groups", "chan", "sub"))
        rows, channels = tokens.shape
        fits = channels == ways * LANES and rows % 64 == 0
        fits = fits and rows * ways == 8 * WIDE * RUN and rest[3].shape[0] % 512 == 0
        return (by_tokens if pairs and fits else general)(tokens, *rest)

    return jax.shard_map(
        shards,
        mesh=mesh,
        in_specs=(
            P(("groups", "seq", "sub"), "chan"),
            P("chan"),
            P(None, "chan"),
            P(None, "chan"),
            P(None, "chan"),
            P(None, "chan"),
            P(None, "chan"),
        ),
        out_specs=P(("groups", "seq", "sub"), "chan"),
        check_vma=False,
    )
```

```python
import functools

import jax
import jax.numpy as jnp
from jax import lax
from jax.experimental import pallas as pl
from jax.experimental.pallas import tpu as pltpu
from jax.sharding import PartitionSpec as P

LEVELS = 15
LANES = 128
SPLIT = 2
RUN = 16
MIDDLE = 8
WIDE = 64
LINE = ("seq", "sub")
GRANT = 16 * 2**20
LITTLE = 12 * 2**20
LARGE = 54 * 2**20
PARTS = 4
HOP = 5*10**9


def run_levels(stream, shifter, low0, low1, high0, high1, mix):
    mixed = mix[LEVELS + 1] * stream
    for level in range(LEVELS):
        shifted = shifter(stream, 2**level)
        high = high0 * stream + high1 * shifted
        stream = low0 * stream + low1 * shifted
        mixed = mixed + mix[level] * high
    return mixed + mix[LEVELS] * stream


def general(tokens, low_angle, high_taps, level_mix, w_value, w_gate, out_weight):
    rows = tokens.shape[0]
    channels = tokens.shape[1]
    ways = lax.axis_size(LINE)
    total = rows * ways
    narrow = channels // ways
    place = lax.axis_index(LINE) * narrow
    columns = lax.all_to_all(tokens.T, LINE, split_axis=0, concat_axis=1, tiled=True)
    angle = lax.dynamic_slice_in_dim(low_angle, place, narrow, 0)[:, None]
    high_pair = lax.dynamic_slice_in_dim(high_taps, place, narrow, 1)[:, :, None]
    mix = lax.dynamic_slice_in_dim(level_mix, place, narrow, 1)[:, :, None]

    def shifter(stream, reach):
        if reach >= total:
            return jnp.zeros_like(stream)
        return jnp.concatenate(
            [jnp.zeros((stream.shape[0], reach), jnp.float32), stream[:, : total - reach]], 1
        )

    mixed = run_levels(
        columns.astype(jnp.float32),
        shifter,
        jnp.cos(angle),
        jnp.sin(angle),
        high_pair[0],
        high_pair[1],
        mix,
    )
    filtered = jax.nn.gelu(mixed).astype(jnp.bfloat16)
    activated = lax.all_to_all(filtered, LINE, split_axis=1, concat_axis=0, tiled=True).T
    piece = lax.all_gather(activated, "chan", axis=1, tiled=True)
    value = jnp.dot(piece, w_value, preferred_element_type=jnp.float32)
    gate = jnp.dot(piece, w_gate, preferred_element_type=jnp.float32)
    hidden = (value * jax.nn.sigmoid(gate)).astype(jnp.bfloat16)
    projected = jnp.dot(
        lax.all_gather(hidden, "chan", axis=1, tiled=True),
        out_weight,
        preferred_element_type=jnp.float32,
    )
    return (projected + tokens.astype(jnp.float32)).astype(jnp.bfloat16)


def coefficients(live, lanes, angle_ref, high_ref, mix_ref, out_ref):
    low0, low1 = jnp.cos(angle_ref[:, lanes]), jnp.sin(angle_ref[:, lanes])
    high0, high1 = high_ref[0:1, lanes], high_ref[1:2, lanes]
    power = jnp.ones_like(low0)
    for level in range(live + 1):
        weight = jnp.zeros_like(low0)
        if level < live:
            weight = weight + mix_ref[level : level + 1, lanes] * (high0 - high1 * low0 / low1)
        if level > 0:
            weight = weight + mix_ref[level - 1 : level, lanes] * high1 / low1
        if level == live:
            scale = jnp.ones_like(low0)
            for rest in range(live, LEVELS):
                weight = weight + mix_ref[rest : rest + 1, lanes] * high0 * scale
                scale = scale * low0
            weight = weight + mix_ref[LEVELS : LEVELS + 1, lanes] * scale
        weight = weight * power
        if level == 0:
            weight = weight + mix_ref[LEVELS + 1 : LEVELS + 2, lanes]
        out_ref[level : level + 1, :] = weight
        power = power * low0
    out_ref[live + 1 : live + 2, :] = low1 / low0


def advance(stream, tail, ratio):
    reach = tail.shape[0]
    shifted = jnp.concatenate([tail, stream[: stream.shape[0] - reach]], 0)
    return stream + ratio * shifted


def copy_all(pairs, sems, meanwhile=None):
    copies = [pltpu.make_async_copy(*pair, sems.at[at]) for at, pair in enumerate(pairs)]
    for copy in copies:
        copy.start()
    if meanwhile:
        meanwhile()
    for copy in copies:
        copy.wait()


def line_of(place, back, other):
    chips = place[4]
    core = 1 - place[1] if other else place[1]
    return lax.rem(place[0] - back + chips, chips) * 2 + core


def pair_kernel(value, gate, pair, sems):
    core, group = lax.axis_index("sub"), lax.axis_index("groups")
    depth = pair.shape[1]
    part = depth // PARTS
    pairs = []
    for at, weight in enumerate((value, gate)):
        for p in range(PARTS):
            here = pl.ds(pl.multiple_of((2 * group + core) * depth + p * part, part), part)
            pairs.append((weight.at[here], pair.at[at, pl.ds(p * part, part)]))
    copy_all(pairs, sems)


def run_pair(value, gate):
    width, channels = value.shape
    return pl.pallas_call(
        pair_kernel,
        in_specs=[pl.BlockSpec(memory_space=pltpu.HBM)] * 2,
        out_specs=pl.BlockSpec(memory_space=pltpu.VMEM),
        out_shape=jax.ShapeDtypeStruct((2, width // 4, channels), value.dtype),
        scratch_shapes=[pltpu.SemaphoreType.DMA((2 * PARTS,))],
        compiler_params=pltpu.CompilerParams(vmem_limit_bytes=LARGE),
        name="pair",
    )(value, gate)


def levels_kernel(live, chips, place, angle_ref, high_ref, mix_ref, own, *refs):
    direct = refs[: chips - 1]
    handed = refs[chips - 1 : chips + 1]
    outs = refs[chips + 1 : chips + 5]
    tokens, stream_ref, mixed_ref, act_ref, coef_ref = refs[chips + 5 :]
    side = place[2]
    rows = own.shape[0]
    units = rows * 2 * chips // 8

    def block(line):
        return pl.ds(pl.multiple_of(line * rows, rows), rows)

    columns = pl.ds(pl.multiple_of(line_of(place, 0, 0) * LANES, LANES), LANES)
    lanes = pl.ds(pl.multiple_of(place[1] * LANES, LANES), LANES)
    for back in range(chips):
        mine = direct[back - 1][:, lanes] if back else own[...]
        tokens[block(line_of(place, back, 0)), :] = mine
        tokens[block(line_of(place, back, 1)), :] = handed[1][back - 1] if back else handed[0][...]
    coefficients(live, columns, angle_ref, high_ref, mix_ref, coef_ref)

    def whole(row):
        return jnp.broadcast_to(coef_ref[row : row + 1, :], (8, LANES))[None]

    def zero(n):
        return jnp.zeros((n, 8, LANES), jnp.float32)

    ratio = whole(live + 1)

    def first(i, carry):
        start = pl.multiple_of(i * RUN * 8, RUN * 8)
        x = tokens[pl.ds(start, RUN * 8), :].astype(jnp.float32).reshape(RUN, 8, LANES)
        mixed = whole(0) * x
        row = lax.broadcasted_iota(jnp.int32, (1, 8, LANES), 1)
        kept = []
        for level, tail in enumerate(carry):
            kept.append(x[RUN - tail.shape[0] :])
            if level < 3:
                turned = pltpu.roll(jnp.concatenate([tail, x], 0), 2**level, 1)
                x = x + ratio * jnp.where(row < 2**level, turned[:RUN], turned[1:])
            else:
                x = advance(x, tail, ratio)
            mixed = mixed + whole(level + 1) * x
        stream_ref[pl.ds(i * RUN, RUN)] = x
        mixed_ref[pl.ds(i * RUN, RUN)] = mixed
        return tuple(kept)

    lax.fori_loop(0, units // RUN, first, tuple(zero(n) for n in (1, 1, 1, 1, 2, 4)))

    stream = stream_ref.reshape(units // MIDDLE, MIDDLE, 8, LANES)
    total = mixed_ref.reshape(units // MIDDLE, MIDDLE, 8, LANES)
    steps = units // MIDDLE // RUN

    def second(t, carry):
        q = t // steps
        i = t % steps
        x = stream[pl.ds(i * RUN, RUN), q]
        mixed = total[pl.ds(i * RUN, RUN), q]
        keep = jnp.where(i > 0, 1.0, 0.0)
        kept = []
        for level, tail in enumerate(carry):
            kept.append(x[RUN - tail.shape[0] :])
            x = advance(x, tail * keep, ratio)
            mixed = mixed + whole(level + 7) * x
        stream[pl.ds(i * RUN, RUN), q] = x
        total[pl.ds(i * RUN, RUN), q] = mixed
        return tuple(kept)

    lax.fori_loop(0, MIDDLE * steps, second, tuple(zero(n) for n in (1, 2, 4)))

    stream_wide = stream_ref.reshape(units // WIDE, WIDE, 8, LANES)
    total_wide = mixed_ref.reshape(units // WIDE, WIDE, 8, LANES)
    act_wide = act_ref.reshape(units // WIDE, WIDE // 2, 16, LANES)

    def third(pair, _):
        halves = []
        for odd in range(2):
            x = stream_wide[:, pair * 2 + odd]
            mixed = total_wide[:, pair * 2 + odd]
            for level in range(9, live):
                reach = 2 ** (level - 9)
                x = jnp.concatenate([x[:reach], x[reach:] + ratio * x[:-reach]], 0)
                mixed = mixed + whole(level + 1) * x
            halves.append(jax.nn.gelu(mixed))
        act_wide[:, pair] = jnp.concatenate(halves, 1).astype(jnp.bfloat16)
        return 0

    half = rows // 2
    lax.fori_loop(0, WIDE // 2, third, 0)
    for ahead in range(chips):
        for other in range(2):
            start = line_of(place, -ahead, other) * rows
            for at, which in enumerate((1 - side, side)):
                begin = pl.multiple_of(start + which * half, half)
                outs[2 * other + at][ahead] = act_ref[pl.ds(begin, half), :]


def run_filter(place, angle, high, mix, own, direct, handed, live):
    chips = 1 + len(direct)
    rows = handed[0].shape[0]
    total = rows * 2 * chips
    anywhere = pl.BlockSpec(memory_space=pltpu.HBM)
    return pl.pallas_call(
        functools.partial(levels_kernel, live, chips),
        out_shape=[jax.ShapeDtypeStruct((chips, rows // 2, LANES), jnp.bfloat16)] * 4,
        in_specs=[
            pl.BlockSpec(memory_space=pltpu.SMEM),
        ]
        + [pl.BlockSpec(memory_space=pltpu.VMEM)] * (chips + 5),
        out_specs=[pl.BlockSpec(memory_space=pltpu.VMEM)] * 4,
        scratch_shapes=[
            pltpu.VMEM((total, LANES), jnp.bfloat16),
            pltpu.VMEM((total // 8, 8, LANES), jnp.float32),
            pltpu.VMEM((total // 8, 8, LANES), jnp.float32),
            pltpu.VMEM((total, LANES), jnp.bfloat16),
            pltpu.VMEM((live + 2, LANES), jnp.float32),
        ],
        compiler_params=pltpu.CompilerParams(vmem_limit_bytes=GRANT),
        name="levels",
    )(place, angle[None], high, mix, own, *direct, *handed)


def join_kernel(*refs):
    sources, outs = refs[:4], refs[4:]
    chips, half, _ = sources[0].shape
    part = half // SPLIT
    for group in range(1 + SPLIT):
        rows = slice(None) if group == 0 else pl.ds((group - 1) * part, part)
        for ahead in range(chips):
            for other in range(2):
                source = sources[2 * other + (group > 0)]
                outs[group * chips + ahead][other] = source[ahead, rows]


def run_join(arrays):
    chips, half, _ = arrays[0].shape
    in_vmem = pl.BlockSpec(memory_space=pltpu.VMEM)
    sizes = [half] * chips + [half // SPLIT] * (SPLIT * chips)
    outs = pl.pallas_call(
        join_kernel,
        in_specs=[in_vmem] * 4,
        out_specs=[in_vmem] * len(sizes),
        out_shape=[jax.ShapeDtypeStruct((2, size, LANES), jnp.bfloat16) for size in sizes],
        compiler_params=pltpu.CompilerParams(vmem_limit_bytes=LITTLE),
        name="join",
    )(*arrays)
    groups = [list(outs[at * chips : (at + 1) * chips]) for at in range(1 + SPLIT)]
    return groups[0], groups[1:]


def work(rows, depth, columns):
    return pl.CostEstimate(
        flops=2 * rows * depth * columns,
        bytes_accessed=2 * (rows * depth + depth * columns + rows * columns),
        transcendentals=0,
    )


def dot(a, b):
    return jnp.dot(a, b, preferred_element_type=jnp.float32)


def load_kernel(count, *refs):
    place, sources, outs = refs[0], refs[1 : 1 + count], refs[-count - 2 : -2]
    copy_all(list(zip(sources, outs)), refs[-1])
    for at in range(place.shape[0]):
        refs[-2][at] = place[at]


def run_load(place, arrays, after):
    count = len(arrays)
    smem = pl.BlockSpec(memory_space=pltpu.SMEM)
    *loaded, place = pl.pallas_call(
        functools.partial(load_kernel, count),
        in_specs=[smem] + [pl.BlockSpec(memory_space=pltpu.HBM)] * (count + len(after)),
        out_specs=[pl.BlockSpec(memory_space=pltpu.VMEM)] * count + [smem],
        out_shape=[jax.ShapeDtypeStruct(array.shape, array.dtype) for array in (*arrays, place)],
        scratch_shapes=[pltpu.SemaphoreType.DMA((count,))],
        compiler_params=pltpu.CompilerParams(vmem_limit_bytes=LITTLE),
        cost_estimate=pl.CostEstimate(flops=10**11, bytes_accessed=0, transcendentals=0),
        name="load",
    )(place, *arrays, *after)
    return loaded, place


def hidden_kernel(chips, block, place, *refs):
    direct = refs[:chips]
    got, own, fetched = refs[chips], refs[chips + 1 : chips + 3], refs[chips + 3 : chips + 7]
    hidden_ref, act, sems = refs[chips + 7 :]
    side = place[2]
    channels = 2 * chips * LANES
    pairs = []
    for back in range(chips):
        for other in range(2):
            line = line_of(place, back, other) * LANES
            for start, source in (
                (side * channels + line, direct[back].at[other]),
                ((1 - side) * channels + line, got.at[back, other]),
            ):
                lanes = pl.ds(pl.multiple_of(start, LANES), LANES)
                pairs.append((source, act.at[:, lanes]))
    copy_all(pairs, sems)

    core, group = place[1], place[3]
    depth = fetched[0].shape[1]

    def own_side(at, columns):
        return dot(act[...], own[at][:, columns])

    def far_side(at, columns):
        total = None
        for piece, far_group, far_core in zip(fetched, (0, 1, 0, 1), (0, 0, 1, 1)):
            quarter = 2 * (1 - group if far_group else group) + (1 - core if far_core else core)
            rows = pl.ds(pl.multiple_of(quarter * depth, depth), depth)
            term = dot(act[:, rows], piece[at, :, columns])
            total = term if total is None else total + term
        return total

    for whose, product in ((side, own_side), (1 - side, far_side)):

        @pl.loop(0, channels // block)
        def _(j):
            columns = pl.ds(pl.multiple_of(j * block, block), block)
            target = pl.ds(pl.multiple_of(whose * channels + j * block, block), block)
            gated = product(0, columns) * jax.nn.sigmoid(product(1, columns))
            hidden_ref[:, target] = gated.astype(jnp.bfloat16)


def run_hidden(place, direct, got, *weights):
    chips = len(direct)
    rows = got.shape[2]
    width, channels = weights[0].shape
    in_vmem = pl.BlockSpec(memory_space=pltpu.VMEM)
    return pl.pallas_call(
        functools.partial(hidden_kernel, chips, min(512, channels)),
        in_specs=[pl.BlockSpec(memory_space=pltpu.SMEM)]
        + [pl.BlockSpec(memory_space=pltpu.HBM)] * (chips + 1)
        + [in_vmem] * len(weights),
        out_specs=in_vmem,
        scratch_shapes=[
            pltpu.VMEM((rows, width), jnp.bfloat16),
            pltpu.SemaphoreType.DMA((4 * chips,)),
        ],
        out_shape=jax.ShapeDtypeStruct((rows, width), jnp.bfloat16),
        compiler_params=pltpu.CompilerParams(vmem_limit_bytes=LITTLE),
        name="hidden",
    )(place, *direct, got, *weights)


def send_kernel(place, hidden, mine, twin, out_ref):
    depth = mine.shape[0]
    core = place[1]
    total = None
    for half, weight in ((core, mine), (1 - core, twin)):
        rows = pl.ds(pl.multiple_of(half * depth, depth), depth)
        term = dot(hidden[:, rows], weight[...])
        total = term if total is None else total + term
    out_ref[...] = total.astype(jnp.bfloat16)


def run_send(place, hidden, halves):
    rows = hidden.shape[0]
    channels = halves[0].shape[1]
    in_vmem = pl.BlockSpec(memory_space=pltpu.VMEM)
    return pl.pallas_call(
        send_kernel,
        in_specs=[pl.BlockSpec(memory_space=pltpu.SMEM)] + [in_vmem] * 3,
        out_specs=in_vmem,
        out_shape=jax.ShapeDtypeStruct((rows, channels), jnp.bfloat16),
        compiler_params=pltpu.CompilerParams(vmem_limit_bytes=LITTLE),
        name="send",
    )(place, hidden, *halves)


def finish_kernel(side, *refs):
    parts, weight, tokens, out_ref = refs[:SPLIT], refs[SPLIT], refs[SPLIT + 1], refs[SPLIT + 2]
    rows = parts[0].shape[0]
    for q in range(SPLIT):
        at = pl.ds(q * rows, rows)
        made = dot(parts[q][...], weight[...])
        out_ref[at, :] = (made + tokens[at, :].astype(jnp.float32)).astype(jnp.bfloat16)


def run_finish(side, parts, weight, tokens):
    rows, width = parts[0].shape
    channels = weight.shape[1]
    block = min(512, channels)
    return pl.pallas_call(
        finish_kernel,
        grid_spec=pltpu.PrefetchScalarGridSpec(
            num_scalar_prefetch=1,
            grid=(channels // block,),
            in_specs=[pl.BlockSpec((rows, width), lambda j, side: (0, 0))] * SPLIT
            + [
                pl.BlockSpec((width, block), lambda j, side: (0, j)),
                pl.BlockSpec((SPLIT * rows, block), lambda j, side: (side[0], j)),
            ],
            out_specs=pl.BlockSpec((SPLIT * rows, block), lambda j, side: (side[0], j)),
        ),
        out_shape=jax.ShapeDtypeStruct(tokens.shape, jnp.bfloat16),
        compiler_params=pltpu.CompilerParams(vmem_limit_bytes=GRANT),
        cost_estimate=work(SPLIT * rows, width, channels),
        name="finish",
    )(side, *parts, weight, tokens)


def add_kernel(q, side, got, tokens, kept, out_ref, before, after, loads, stores):
    rows = got.shape[0]
    part = rows // PARTS
    start = (SPLIT * (1 - side[0]) + q) * rows

    def here(p):
        return pl.ds(pl.multiple_of(start + p * part, part), part)

    def piece(p):
        return pl.ds(p * part, part)

    def load(p):
        return pltpu.make_async_copy(tokens.at[here(p)], before.at[piece(p)], loads.at[p])

    def store(p):
        return pltpu.make_async_copy(after.at[piece(p)], out_ref.at[here(p)], stores.at[p])

    for p in range(PARTS):
        load(p).start()
    for p in range(PARTS):
        load(p).wait()
        added = got[piece(p), :].astype(jnp.float32) + before[piece(p), :].astype(jnp.float32)
        after[piece(p), :] = added.astype(jnp.bfloat16)
        store(p).start()
    for p in range(PARTS):
        store(p).wait()


def add_far(side, q, got, tokens, result):
    anywhere = pl.BlockSpec(memory_space=pl.ANY)
    return pl.pallas_call(
        functools.partial(add_kernel, q),
        in_specs=[
            pl.BlockSpec(memory_space=pltpu.SMEM),
            pl.BlockSpec(memory_space=pltpu.VMEM),
            anywhere,
            anywhere,
        ],
        out_specs=anywhere,
        out_shape=jax.ShapeDtypeStruct(tokens.shape, jnp.bfloat16),
        input_output_aliases={3: 0},
        scratch_shapes=[
            pltpu.VMEM(got.shape, got.dtype),
            pltpu.VMEM(got.shape, got.dtype),
            pltpu.SemaphoreType.DMA((PARTS,)),
            pltpu.SemaphoreType.DMA((PARTS,)),
        ],
        compiler_params=pltpu.CompilerParams(vmem_limit_bytes=LITTLE),
        name="add_far",
    )(side, got, tokens, result)


def swap(array, axis):
    return lax.ppermute(array, axis, [(0, 1), (1, 0)])


def ahead(array, offset):
    chips = lax.axis_size("seq")
    return lax.ppermute(array, "seq", [(j, (j + offset) % chips) for j in range(chips)])


def anchor_kernel(*refs):
    refs[-1][...] = jnp.zeros(refs[-1].shape, refs[-1].dtype)


def anchor(after):
    return pl.pallas_call(
        anchor_kernel,
        in_specs=[pl.BlockSpec(memory_space=pltpu.HBM)] * len(after),
        out_specs=pl.BlockSpec(memory_space=pltpu.VMEM),
        out_shape=jax.ShapeDtypeStruct((8, LANES), jnp.float32),
        compiler_params=pltpu.CompilerParams(vmem_limit_bytes=LITTLE),
        cost_estimate=pl.CostEstimate(flops=10**11, bytes_accessed=0, transcendentals=0),
        name="anchor",
    )(*after)


def others_kernel(place, *refs):
    lanes = pl.ds(pl.multiple_of((1 - place[1]) * LANES, LANES), LANES)
    for at, block in enumerate(refs[:-1]):
        refs[-1][at] = block[:, lanes]


def run_others(place, blocks):
    in_vmem = pl.BlockSpec(memory_space=pltpu.VMEM)
    rows = blocks[0].shape[0]
    return pl.pallas_call(
        others_kernel,
        in_specs=[pl.BlockSpec(memory_space=pltpu.SMEM)] + [in_vmem] * len(blocks),
        out_specs=in_vmem,
        out_shape=jax.ShapeDtypeStruct((len(blocks), rows, LANES), blocks[0].dtype),
        compiler_params=pltpu.CompilerParams(vmem_limit_bytes=LITTLE),
        cost_estimate=pl.CostEstimate(flops=HOP, bytes_accessed=0, transcendentals=0),
        name="others",
    )(place, *blocks)


def by_tokens(tokens, low_angle, high_taps, level_mix, w_value, w_gate, out_weight):
    rows, channels = tokens.shape
    chips = lax.axis_size("seq")
    narrow = channels // (2 * chips)
    chip, core = lax.axis_index("seq"), lax.axis_index("sub")
    side, group = lax.axis_index("chan"), lax.axis_index("groups")
    live = min(LEVELS, (rows * 2 * chips - 1).bit_length())
    order = sorted(range(1, chips), key=lambda s: abs(2 * s - chips))
    place = jnp.stack([chip, core, side, group, chips]).astype(jnp.int32)

    pair = run_pair(w_value, w_gate)
    tokens, pair = lax.optimization_barrier((tokens, pair))
    def columns(back, first, count):
        start = ((chip - back) % chips * 2 + first) * narrow
        return lax.dynamic_slice_in_dim(tokens, start, count * narrow, 1)

    blocks = [columns(-s, 0, 2) for s in range(1, chips)]
    mine, other = columns(0, core, 1), columns(0, 1 - core, 1)
    blocks, out_piece = lax.optimization_barrier((blocks, out_weight))
    direct = [None] * chips
    for s in order:
        direct[s] = ahead(blocks[s - 1], s)
    handed = [swap(other, "sub"), swap(run_others(place, direct[1:]), "sub")]

    depth = w_value.shape[0] // 4
    half = lax.dynamic_slice_in_dim(out_piece, core * 2 * depth, 2 * depth, 0)
    pair_first = swap(pair, "chan")
    direct[2], pair_first, half = lax.optimization_barrier((direct[2], pair_first, half))
    pair_second = swap(pair_first, "groups")
    half_first = swap(half, "chan")
    pair_third = swap(pair_first, "sub")

    *kept, given_far, given_near = run_filter(
        place, low_angle, high_taps, level_mix, mine, direct[1:], handed, live
    )

    far, near = run_join([*kept, swap(given_far, "sub"), swap(given_near, "sub")])
    far, pair_third = lax.optimization_barrier((far, pair_third))
    far_got = [far[0]] + [None] * (chips - 1)
    for s in order:
        far_got[s] = ahead(far[s], s)

    def exchange(backs):
        return (
            swap(jnp.stack([far_got[back][0] for back in backs]), "chan"),
            cross(jnp.stack([far_got[back][1] for back in backs])),
        )

    both = anchor([pair_second, half_first])
    far_got, pair_second, half_first, both = lax.optimization_barrier(
        (far_got, pair_second, half_first, both)
    )
    far_got = list(far_got)
    near_got = [[part[0]] + [None] * (chips - 1) for part in near]
    for s in order:
        near[0][s], far_got[s] = lax.optimization_barrier((near[0][s], far_got[s]))
        near_got[0][s] = ahead(near[0][s], s)
    rows = near[0][0].shape[1]

    def exchange(q, before):
        part = slice(q * rows, (q + 1) * rows)
        mine, before = lax.optimization_barrier(
            (jnp.stack([block[:, part] for block in far_got]), before)
        )
        return swap(mine, "chan")

    got = [exchange(q, half_first) for q in range(SPLIT)]
    pair_fourth = swap(pair_second, "sub")
    loaded, place = run_load(
        place, [w_value, w_gate, pair_first, pair_second, pair_third], far_got[1:]
    )
    near_got[0], got[0], place, pair_fourth, half_first = lax.optimization_barrier(
        (near_got[0], got[0], place, pair_fourth, half_first)
    )
    half_second = swap(half_first, "sub")
    loaded.append(pair_fourth)
    which = place[2:3]
    hidden, returned = [], []
    for q in range(SPLIT):
        if q + 1 < SPLIT:
            for s in order:
                near[q + 1][s], near_got[q][s] = lax.optimization_barrier(
                    (near[q + 1][s], near_got[q][s])
                )
                near_got[q + 1][s] = ahead(near[q + 1][s], s)
        made = run_hidden(place, near_got[q], got[q], *loaded)
        sent = run_send(place, made, [half_first, half_second])
        if q + 1 < SPLIT:
            near_got[q + 1], got[q + 1], sent = lax.optimization_barrier(
                (near_got[q + 1], got[q + 1], sent)
            )
        hidden.append(made)
        returned.append(swap(sent, "chan"))
    hidden, returned[0] = lax.optimization_barrier((hidden, returned[0]))
    result = run_finish(which, hidden, out_weight, tokens)
    for q in range(SPLIT):
        result = add_far(which, q, returned[q], tokens, result)
    return result


def solution(mesh):
    def shards(tokens, *rest):
        ways = mesh.shape["seq"] * mesh.shape["sub"]
        pairs = all(mesh.shape[name] == 2 for name in ("groups", "chan", "sub"))
        rows, channels = tokens.shape
        fits = channels == ways * LANES and rows % 64 == 0
        fits = fits and rows * ways == 8 * WIDE * RUN and rest[3].shape[0] % 512 == 0
        return (by_tokens if pairs and fits else general)(tokens, *rest)

    return jax.shard_map(
        shards,
        mesh=mesh,
        in_specs=(
            P(("groups", "seq", "sub"), "chan"),
            P("chan"),
            P(None, "chan"),
            P(None, "chan"),
            P(None, "chan"),
            P(None, "chan"),
            P(None, "chan"),
        ),
        out_specs=P(("groups", "seq", "sub"), "chan"),
        check_vma=False,
    )
```

```python
import functools

import jax
import jax.numpy as jnp
from jax import lax
from jax.experimental import pallas as pl
from jax.experimental.pallas import tpu as pltpu
from jax.sharding import PartitionSpec as P

LEVELS = 15
LANES = 128
SPLIT = 2
RUN = 16
MIDDLE = 8
WIDE = 64
LINE = ("seq", "sub")
GRANT = 16 * 2**20
LITTLE = 12 * 2**20
LARGE = 54 * 2**20
PARTS = 8
HOP = 5*10**9


def run_levels(stream, shifter, low0, low1, high0, high1, mix):
    mixed = mix[LEVELS + 1] * stream
    for level in range(LEVELS):
        shifted = shifter(stream, 2**level)
        high = high0 * stream + high1 * shifted
        stream = low0 * stream + low1 * shifted
        mixed = mixed + mix[level] * high
    return mixed + mix[LEVELS] * stream


def general(tokens, low_angle, high_taps, level_mix, w_value, w_gate, out_weight):
    rows = tokens.shape[0]
    channels = tokens.shape[1]
    ways = lax.axis_size(LINE)
    total = rows * ways
    narrow = channels // ways
    place = lax.axis_index(LINE) * narrow
    columns = lax.all_to_all(tokens.T, LINE, split_axis=0, concat_axis=1, tiled=True)
    angle = lax.dynamic_slice_in_dim(low_angle, place, narrow, 0)[:, None]
    high_pair = lax.dynamic_slice_in_dim(high_taps, place, narrow, 1)[:, :, None]
    mix = lax.dynamic_slice_in_dim(level_mix, place, narrow, 1)[:, :, None]

    def shifter(stream, reach):
        if reach >= total:
            return jnp.zeros_like(stream)
        return jnp.concatenate(
            [jnp.zeros((stream.shape[0], reach), jnp.float32), stream[:, : total - reach]], 1
        )

    mixed = run_levels(
        columns.astype(jnp.float32),
        shifter,
        jnp.cos(angle),
        jnp.sin(angle),
        high_pair[0],
        high_pair[1],
        mix,
    )
    filtered = jax.nn.gelu(mixed).astype(jnp.bfloat16)
    activated = lax.all_to_all(filtered, LINE, split_axis=1, concat_axis=0, tiled=True).T
    piece = lax.all_gather(activated, "chan", axis=1, tiled=True)
    value = jnp.dot(piece, w_value, preferred_element_type=jnp.float32)
    gate = jnp.dot(piece, w_gate, preferred_element_type=jnp.float32)
    hidden = (value * jax.nn.sigmoid(gate)).astype(jnp.bfloat16)
    projected = jnp.dot(
        lax.all_gather(hidden, "chan", axis=1, tiled=True),
        out_weight,
        preferred_element_type=jnp.float32,
    )
    return (projected + tokens.astype(jnp.float32)).astype(jnp.bfloat16)


def coefficients(live, lanes, angle_ref, high_ref, mix_ref, out_ref):
    low0, low1 = jnp.cos(angle_ref[:, lanes]), jnp.sin(angle_ref[:, lanes])
    high0, high1 = high_ref[0:1, lanes], high_ref[1:2, lanes]
    power = jnp.ones_like(low0)
    for level in range(live + 1):
        weight = jnp.zeros_like(low0)
        if level < live:
            weight = weight + mix_ref[level : level + 1, lanes] * (high0 - high1 * low0 / low1)
        if level > 0:
            weight = weight + mix_ref[level - 1 : level, lanes] * high1 / low1
        if level == live:
            scale = jnp.ones_like(low0)
            for rest in range(live, LEVELS):
                weight = weight + mix_ref[rest : rest + 1, lanes] * high0 * scale
                scale = scale * low0
            weight = weight + mix_ref[LEVELS : LEVELS + 1, lanes] * scale
        weight = weight * power
        if level == 0:
            weight = weight + mix_ref[LEVELS + 1 : LEVELS + 2, lanes]
        out_ref[level : level + 1, :] = weight
        power = power * low0
    out_ref[live + 1 : live + 2, :] = low1 / low0


def advance(stream, tail, ratio):
    reach = tail.shape[0]
    shifted = jnp.concatenate([tail, stream[: stream.shape[0] - reach]], 0)
    return stream + ratio * shifted


def copy_all(pairs, sems, meanwhile=None):
    copies = [pltpu.make_async_copy(*pair, sems.at[at]) for at, pair in enumerate(pairs)]
    for copy in copies:
        copy.start()
    if meanwhile:
        meanwhile()
    for copy in copies:
        copy.wait()


def line_of(place, back, other):
    chips = place[4]
    core = 1 - place[1] if other else place[1]
    return lax.rem(place[0] - back + chips, chips) * 2 + core


def pair_kernel(value, gate, pair, sems):
    core, group = lax.axis_index("sub"), lax.axis_index("groups")
    depth = pair.shape[1]
    part = depth // PARTS
    pairs = []
    for at, weight in enumerate((value, gate)):
        for p in range(PARTS):
            here = pl.ds(pl.multiple_of((2 * group + core) * depth + p * part, part), part)
            pairs.append((weight.at[here], pair.at[at, pl.ds(p * part, part)]))
    copy_all(pairs, sems)


def run_pair(value, gate):
    width, channels = value.shape
    return pl.pallas_call(
        pair_kernel,
        in_specs=[pl.BlockSpec(memory_space=pltpu.HBM)] * 2,
        out_specs=pl.BlockSpec(memory_space=pltpu.VMEM),
        out_shape=jax.ShapeDtypeStruct((2, width // 4, channels), value.dtype),
        scratch_shapes=[pltpu.SemaphoreType.DMA((2 * PARTS,))],
        compiler_params=pltpu.CompilerParams(vmem_limit_bytes=LARGE),
        name="pair",
    )(value, gate)


def levels_kernel(live, chips, place, angle_ref, high_ref, mix_ref, own, *refs):
    direct = refs[: chips - 1]
    handed = refs[chips - 1 : chips + 1]
    outs = refs[chips + 1 : chips + 5]
    tokens, stream_ref, mixed_ref, act_ref, coef_ref = refs[chips + 5 :]
    side = place[2]
    rows = own.shape[0]
    units = rows * 2 * chips // 8

    def block(line):
        return pl.ds(pl.multiple_of(line * rows, rows), rows)

    columns = pl.ds(pl.multiple_of(line_of(place, 0, 0) * LANES, LANES), LANES)
    lanes = pl.ds(pl.multiple_of(place[1] * LANES, LANES), LANES)
    for back in range(chips):
        mine = direct[back - 1][:, lanes] if back else own[...]
        tokens[block(line_of(place, back, 0)), :] = mine
        tokens[block(line_of(place, back, 1)), :] = handed[1][back - 1] if back else handed[0][...]
    coefficients(live, columns, angle_ref, high_ref, mix_ref, coef_ref)

    def whole(row):
        return jnp.broadcast_to(coef_ref[row : row + 1, :], (8, LANES))[None]

    def zero(n):
        return jnp.zeros((n, 8, LANES), jnp.float32)

    ratio = whole(live + 1)

    def first(i, carry):
        start = pl.multiple_of(i * RUN * 8, RUN * 8)
        x = tokens[pl.ds(start, RUN * 8), :].astype(jnp.float32).reshape(RUN, 8, LANES)
        mixed = whole(0) * x
        row = lax.broadcasted_iota(jnp.int32, (1, 8, LANES), 1)
        kept = []
        for level, tail in enumerate(carry):
            kept.append(x[RUN - tail.shape[0] :])
            if level < 3:
                turned = pltpu.roll(jnp.concatenate([tail, x], 0), 2**level, 1)
                x = x + ratio * jnp.where(row < 2**level, turned[:RUN], turned[1:])
            else:
                x = advance(x, tail, ratio)
            mixed = mixed + whole(level + 1) * x
        stream_ref[pl.ds(i * RUN, RUN)] = x
        mixed_ref[pl.ds(i * RUN, RUN)] = mixed
        return tuple(kept)

    lax.fori_loop(0, units // RUN, first, tuple(zero(n) for n in (1, 1, 1, 1, 2, 4)))

    stream = stream_ref.reshape(units // MIDDLE, MIDDLE, 8, LANES)
    total = mixed_ref.reshape(units // MIDDLE, MIDDLE, 8, LANES)
    steps = units // MIDDLE // RUN

    def second(t, carry):
        q = t // steps
        i = t % steps
        x = stream[pl.ds(i * RUN, RUN), q]
        mixed = total[pl.ds(i * RUN, RUN), q]
        keep = jnp.where(i > 0, 1.0, 0.0)
        kept = []
        for level, tail in enumerate(carry):
            kept.append(x[RUN - tail.shape[0] :])
            x = advance(x, tail * keep, ratio)
            mixed = mixed + whole(level + 7) * x
        stream[pl.ds(i * RUN, RUN), q] = x
        total[pl.ds(i * RUN, RUN), q] = mixed
        return tuple(kept)

    lax.fori_loop(0, MIDDLE * steps, second, tuple(zero(n) for n in (1, 2, 4)))

    stream_wide = stream_ref.reshape(units // WIDE, WIDE, 8, LANES)
    total_wide = mixed_ref.reshape(units // WIDE, WIDE, 8, LANES)
    act_wide = act_ref.reshape(units // WIDE, WIDE // 2, 16, LANES)

    def third(pair, _):
        halves = []
        for odd in range(2):
            x = stream_wide[:, pair * 2 + odd]
            mixed = total_wide[:, pair * 2 + odd]
            for level in range(9, live):
                reach = 2 ** (level - 9)
                x = jnp.concatenate([x[:reach], x[reach:] + ratio * x[:-reach]], 0)
                mixed = mixed + whole(level + 1) * x
            halves.append(jax.nn.gelu(mixed))
        act_wide[:, pair] = jnp.concatenate(halves, 1).astype(jnp.bfloat16)
        return 0

    half = rows // 2
    lax.fori_loop(0, WIDE // 2, third, 0)
    for ahead in range(chips):
        for other in range(2):
            start = line_of(place, -ahead, other) * rows
            for at, which in enumerate((1 - side, side)):
                begin = pl.multiple_of(start + which * half, half)
                outs[2 * other + at][ahead] = act_ref[pl.ds(begin, half), :]


def run_filter(place, angle, high, mix, own, direct, handed, live):
    chips = 1 + len(direct)
    rows = handed[0].shape[0]
    total = rows * 2 * chips
    anywhere = pl.BlockSpec(memory_space=pltpu.HBM)
    return pl.pallas_call(
        functools.partial(levels_kernel, live, chips),
        out_shape=[jax.ShapeDtypeStruct((chips, rows // 2, LANES), jnp.bfloat16)] * 4,
        in_specs=[
            pl.BlockSpec(memory_space=pltpu.SMEM),
        ]
        + [pl.BlockSpec(memory_space=pltpu.VMEM)] * (chips + 5),
        out_specs=[pl.BlockSpec(memory_space=pltpu.VMEM)] * 4,
        scratch_shapes=[
            pltpu.VMEM((total, LANES), jnp.bfloat16),
            pltpu.VMEM((total // 8, 8, LANES), jnp.float32),
            pltpu.VMEM((total // 8, 8, LANES), jnp.float32),
            pltpu.VMEM((total, LANES), jnp.bfloat16),
            pltpu.VMEM((live + 2, LANES), jnp.float32),
        ],
        compiler_params=pltpu.CompilerParams(vmem_limit_bytes=GRANT),
        name="levels",
    )(place, angle[None], high, mix, own, *direct, *handed)


def join_kernel(*refs):
    sources, outs = refs[:4], refs[4:]
    chips, half, _ = sources[0].shape
    part = half // SPLIT
    for group in range(1 + SPLIT):
        rows = slice(None) if group == 0 else pl.ds((group - 1) * part, part)
        for ahead in range(chips):
            for other in range(2):
                source = sources[2 * other + (group > 0)]
                outs[group * chips + ahead][other] = source[ahead, rows]


def run_join(arrays):
    chips, half, _ = arrays[0].shape
    in_vmem = pl.BlockSpec(memory_space=pltpu.VMEM)
    sizes = [half] * chips + [half // SPLIT] * (SPLIT * chips)
    outs = pl.pallas_call(
        join_kernel,
        in_specs=[in_vmem] * 4,
        out_specs=[in_vmem] * len(sizes),
        out_shape=[jax.ShapeDtypeStruct((2, size, LANES), jnp.bfloat16) for size in sizes],
        compiler_params=pltpu.CompilerParams(vmem_limit_bytes=LITTLE),
        name="join",
    )(*arrays)
    groups = [list(outs[at * chips : (at + 1) * chips]) for at in range(1 + SPLIT)]
    return groups[0], groups[1:]


def work(rows, depth, columns):
    return pl.CostEstimate(
        flops=2 * rows * depth * columns,
        bytes_accessed=2 * (rows * depth + depth * columns + rows * columns),
        transcendentals=0,
    )


def dot(a, b):
    return jnp.dot(a, b, preferred_element_type=jnp.float32)


def load_kernel(count, *refs):
    place, sources, outs = refs[0], refs[1 : 1 + count], refs[-count - 2 : -2]
    copy_all(list(zip(sources, outs)), refs[-1])
    for at in range(place.shape[0]):
        refs[-2][at] = place[at]


def run_load(place, arrays, after):
    count = len(arrays)
    smem = pl.BlockSpec(memory_space=pltpu.SMEM)
    *loaded, place = pl.pallas_call(
        functools.partial(load_kernel, count),
        in_specs=[smem] + [pl.BlockSpec(memory_space=pltpu.HBM)] * (count + len(after)),
        out_specs=[pl.BlockSpec(memory_space=pltpu.VMEM)] * count + [smem],
        out_shape=[jax.ShapeDtypeStruct(array.shape, array.dtype) for array in (*arrays, place)],
        scratch_shapes=[pltpu.SemaphoreType.DMA((count,))],
        compiler_params=pltpu.CompilerParams(vmem_limit_bytes=LITTLE),
        cost_estimate=pl.CostEstimate(flops=10**11, bytes_accessed=0, transcendentals=0),
        name="load",
    )(place, *arrays, *after)
    return loaded, place


def hidden_kernel(chips, block, place, *refs):
    direct = refs[:chips]
    got, own, fetched = refs[chips], refs[chips + 1 : chips + 3], refs[chips + 3 : chips + 7]
    hidden_ref, act, sems = refs[chips + 7 :]
    side = place[2]
    channels = 2 * chips * LANES
    pairs = []
    for back in range(chips):
        for other in range(2):
            line = line_of(place, back, other) * LANES
            for start, source in (
                (side * channels + line, direct[back].at[other]),
                ((1 - side) * channels + line, got.at[back, other]),
            ):
                lanes = pl.ds(pl.multiple_of(start, LANES), LANES)
                pairs.append((source, act.at[:, lanes]))
    copy_all(pairs, sems)

    core, group = place[1], place[3]
    depth = fetched[0].shape[1]

    def own_side(at, columns):
        return dot(act[...], own[at][:, columns])

    def far_side(at, columns):
        total = None
        for piece, far_group, far_core in zip(fetched, (0, 1, 0, 1), (0, 0, 1, 1)):
            quarter = 2 * (1 - group if far_group else group) + (1 - core if far_core else core)
            rows = pl.ds(pl.multiple_of(quarter * depth, depth), depth)
            term = dot(act[:, rows], piece[at, :, columns])
            total = term if total is None else total + term
        return total

    for whose, product in ((side, own_side), (1 - side, far_side)):

        @pl.loop(0, channels // block)
        def _(j):
            columns = pl.ds(pl.multiple_of(j * block, block), block)
            target = pl.ds(pl.multiple_of(whose * channels + j * block, block), block)
            gated = product(0, columns) * jax.nn.sigmoid(product(1, columns))
            hidden_ref[:, target] = gated.astype(jnp.bfloat16)


def run_hidden(place, direct, got, *weights):
    chips = len(direct)
    rows = got.shape[2]
    width, channels = weights[0].shape
    in_vmem = pl.BlockSpec(memory_space=pltpu.VMEM)
    return pl.pallas_call(
        functools.partial(hidden_kernel, chips, min(512, channels)),
        in_specs=[pl.BlockSpec(memory_space=pltpu.SMEM)]
        + [pl.BlockSpec(memory_space=pltpu.HBM)] * (chips + 1)
        + [in_vmem] * len(weights),
        out_specs=in_vmem,
        scratch_shapes=[
            pltpu.VMEM((rows, width), jnp.bfloat16),
            pltpu.SemaphoreType.DMA((4 * chips,)),
        ],
        out_shape=jax.ShapeDtypeStruct((rows, width), jnp.bfloat16),
        compiler_params=pltpu.CompilerParams(vmem_limit_bytes=LITTLE),
        name="hidden",
    )(place, *direct, got, *weights)


def send_kernel(place, hidden, mine, twin, out_ref):
    depth = mine.shape[0]
    core = place[1]
    total = None
    for half, weight in ((core, mine), (1 - core, twin)):
        rows = pl.ds(pl.multiple_of(half * depth, depth), depth)
        term = dot(hidden[:, rows], weight[...])
        total = term if total is None else total + term
    out_ref[...] = total.astype(jnp.bfloat16)


def run_send(place, hidden, halves):
    rows = hidden.shape[0]
    channels = halves[0].shape[1]
    in_vmem = pl.BlockSpec(memory_space=pltpu.VMEM)
    return pl.pallas_call(
        send_kernel,
        in_specs=[pl.BlockSpec(memory_space=pltpu.SMEM)] + [in_vmem] * 3,
        out_specs=in_vmem,
        out_shape=jax.ShapeDtypeStruct((rows, channels), jnp.bfloat16),
        compiler_params=pltpu.CompilerParams(vmem_limit_bytes=LITTLE),
        name="send",
    )(place, hidden, *halves)


def finish_kernel(side, *refs):
    parts, weight, tokens, out_ref = refs[:SPLIT], refs[SPLIT], refs[SPLIT + 1], refs[SPLIT + 2]
    rows = parts[0].shape[0]
    for q in range(SPLIT):
        at = pl.ds(q * rows, rows)
        made = dot(parts[q][...], weight[...])
        out_ref[at, :] = (made + tokens[at, :].astype(jnp.float32)).astype(jnp.bfloat16)


def run_finish(side, parts, weight, tokens):
    rows, width = parts[0].shape
    channels = weight.shape[1]
    block = min(512, channels)
    return pl.pallas_call(
        finish_kernel,
        grid_spec=pltpu.PrefetchScalarGridSpec(
            num_scalar_prefetch=1,
            grid=(channels // block,),
            in_specs=[pl.BlockSpec((rows, width), lambda j, side: (0, 0))] * SPLIT
            + [
                pl.BlockSpec((width, block), lambda j, side: (0, j)),
                pl.BlockSpec((SPLIT * rows, block), lambda j, side: (side[0], j)),
            ],
            out_specs=pl.BlockSpec((SPLIT * rows, block), lambda j, side: (side[0], j)),
        ),
        out_shape=jax.ShapeDtypeStruct(tokens.shape, jnp.bfloat16),
        compiler_params=pltpu.CompilerParams(vmem_limit_bytes=GRANT),
        cost_estimate=work(SPLIT * rows, width, channels),
        name="finish",
    )(side, *parts, weight, tokens)


def add_kernel(q, side, got, tokens, kept, out_ref, before, after, loads, stores):
    rows = got.shape[0]
    part = rows // PARTS
    start = (SPLIT * (1 - side[0]) + q) * rows

    def here(p):
        return pl.ds(pl.multiple_of(start + p * part, part), part)

    def piece(p):
        return pl.ds(p * part, part)

    def load(p):
        return pltpu.make_async_copy(tokens.at[here(p)], before.at[piece(p)], loads.at[p])

    def store(p):
        return pltpu.make_async_copy(after.at[piece(p)], out_ref.at[here(p)], stores.at[p])

    for p in range(PARTS):
        load(p).start()
    for p in range(PARTS):
        load(p).wait()
        added = got[piece(p), :].astype(jnp.float32) + before[piece(p), :].astype(jnp.float32)
        after[piece(p), :] = added.astype(jnp.bfloat16)
        store(p).start()
    for p in range(PARTS):
        store(p).wait()


def add_far(side, q, got, tokens, result):
    anywhere = pl.BlockSpec(memory_space=pl.ANY)
    return pl.pallas_call(
        functools.partial(add_kernel, q),
        in_specs=[
            pl.BlockSpec(memory_space=pltpu.SMEM),
            pl.BlockSpec(memory_space=pltpu.VMEM),
            anywhere,
            anywhere,
        ],
        out_specs=anywhere,
        out_shape=jax.ShapeDtypeStruct(tokens.shape, jnp.bfloat16),
        input_output_aliases={3: 0},
        scratch_shapes=[
            pltpu.VMEM(got.shape, got.dtype),
            pltpu.VMEM(got.shape, got.dtype),
            pltpu.SemaphoreType.DMA((PARTS,)),
            pltpu.SemaphoreType.DMA((PARTS,)),
        ],
        compiler_params=pltpu.CompilerParams(vmem_limit_bytes=LITTLE),
        name="add_far",
    )(side, got, tokens, result)


def swap(array, axis):
    return lax.ppermute(array, axis, [(0, 1), (1, 0)])


def ahead(array, offset):
    chips = lax.axis_size("seq")
    return lax.ppermute(array, "seq", [(j, (j + offset) % chips) for j in range(chips)])


def anchor_kernel(*refs):
    refs[-1][...] = jnp.zeros(refs[-1].shape, refs[-1].dtype)


def anchor(after):
    return pl.pallas_call(
        anchor_kernel,
        in_specs=[pl.BlockSpec(memory_space=pltpu.HBM)] * len(after),
        out_specs=pl.BlockSpec(memory_space=pltpu.VMEM),
        out_shape=jax.ShapeDtypeStruct((8, LANES), jnp.float32),
        compiler_params=pltpu.CompilerParams(vmem_limit_bytes=LITTLE),
        cost_estimate=pl.CostEstimate(flops=10**11, bytes_accessed=0, transcendentals=0),
        name="anchor",
    )(*after)


def others_kernel(place, *refs):
    lanes = pl.ds(pl.multiple_of((1 - place[1]) * LANES, LANES), LANES)
    for at, block in enumerate(refs[:-1]):
        refs[-1][at] = block[:, lanes]


def run_others(place, blocks):
    in_vmem = pl.BlockSpec(memory_space=pltpu.VMEM)
    rows = blocks[0].shape[0]
    return pl.pallas_call(
        others_kernel,
        in_specs=[pl.BlockSpec(memory_space=pltpu.SMEM)] + [in_vmem] * len(blocks),
        out_specs=in_vmem,
        out_shape=jax.ShapeDtypeStruct((len(blocks), rows, LANES), blocks[0].dtype),
        compiler_params=pltpu.CompilerParams(vmem_limit_bytes=LITTLE),
        cost_estimate=pl.CostEstimate(flops=HOP, bytes_accessed=0, transcendentals=0),
        name="others",
    )(place, *blocks)


def by_tokens(tokens, low_angle, high_taps, level_mix, w_value, w_gate, out_weight):
    rows, channels = tokens.shape
    chips = lax.axis_size("seq")
    narrow = channels // (2 * chips)
    chip, core = lax.axis_index("seq"), lax.axis_index("sub")
    side, group = lax.axis_index("chan"), lax.axis_index("groups")
    live = min(LEVELS, (rows * 2 * chips - 1).bit_length())
    order = sorted(range(1, chips), key=lambda s: abs(2 * s - chips))
    place = jnp.stack([chip, core, side, group, chips]).astype(jnp.int32)

    pair = run_pair(w_value, w_gate)
    tokens, pair = lax.optimization_barrier((tokens, pair))
    def columns(back, first, count):
        start = ((chip - back) % chips * 2 + first) * narrow
        return lax.dynamic_slice_in_dim(tokens, start, count * narrow, 1)

    blocks = [columns(-s, 0, 2) for s in range(1, chips)]
    mine, other = columns(0, core, 1), columns(0, 1 - core, 1)
    blocks, out_piece = lax.optimization_barrier((blocks, out_weight))
    direct = [None] * chips
    for s in order:
        direct[s] = ahead(blocks[s - 1], s)
    handed = [swap(other, "sub"), swap(run_others(place, direct[1:]), "sub")]

    depth = w_value.shape[0] // 4
    half = lax.dynamic_slice_in_dim(out_piece, core * 2 * depth, 2 * depth, 0)
    pair_first = swap(pair, "chan")
    direct[2], pair_first, half = lax.optimization_barrier((direct[2], pair_first, half))
    pair_second = swap(pair_first, "groups")
    half_first = swap(half, "chan")
    pair_third = swap(pair_first, "sub")

    *kept, given_far, given_near = run_filter(
        place, low_angle, high_taps, level_mix, mine, direct[1:], handed, live
    )

    far, near = run_join([*kept, swap(given_far, "sub"), swap(given_near, "sub")])
    far, pair_third = lax.optimization_barrier((far, pair_third))
    far_got = [far[0]] + [None] * (chips - 1)
    for s in order:
        far_got[s] = ahead(far[s], s)

    def exchange(backs):
        return (
            swap(jnp.stack([far_got[back][0] for back in backs]), "chan"),
            cross(jnp.stack([far_got[back][1] for back in backs])),
        )

    both = anchor([pair_second, half_first])
    far_got, pair_second, half_first, both = lax.optimization_barrier(
        (far_got, pair_second, half_first, both)
    )
    far_got = list(far_got)
    near_got = [[part[0]] + [None] * (chips - 1) for part in near]
    for s in order:
        near[0][s], far_got[s] = lax.optimization_barrier((near[0][s], far_got[s]))
        near_got[0][s] = ahead(near[0][s], s)
    rows = near[0][0].shape[1]

    def exchange(q, before):
        part = slice(q * rows, (q + 1) * rows)
        mine, before = lax.optimization_barrier(
            (jnp.stack([block[:, part] for block in far_got]), before)
        )
        return swap(mine, "chan")

    got = [exchange(q, half_first) for q in range(SPLIT)]
    pair_fourth = swap(pair_second, "sub")
    loaded, place = run_load(
        place, [w_value, w_gate, pair_first, pair_second, pair_third], far_got[1:]
    )
    near_got[0], got[0], place, pair_fourth, half_first = lax.optimization_barrier(
        (near_got[0], got[0], place, pair_fourth, half_first)
    )
    half_second = swap(half_first, "sub")
    loaded.append(pair_fourth)
    which = place[2:3]
    hidden, returned = [], []
    for q in range(SPLIT):
        if q + 1 < SPLIT:
            for s in order:
                near[q + 1][s], near_got[q][s] = lax.optimization_barrier(
                    (near[q + 1][s], near_got[q][s])
                )
                near_got[q + 1][s] = ahead(near[q + 1][s], s)
        made = run_hidden(place, near_got[q], got[q], *loaded)
        sent = run_send(place, made, [half_first, half_second])
        if q + 1 < SPLIT:
            near_got[q + 1], got[q + 1], sent = lax.optimization_barrier(
                (near_got[q + 1], got[q + 1], sent)
            )
        hidden.append(made)
        returned.append(swap(sent, "chan"))
    hidden, returned[0] = lax.optimization_barrier((hidden, returned[0]))
    result = run_finish(which, hidden, out_weight, tokens)
    for q in range(SPLIT):
        result = add_far(which, q, returned[q], tokens, result)
    return result


def solution(mesh):
    def shards(tokens, *rest):
        ways = mesh.shape["seq"] * mesh.shape["sub"]
        pairs = all(mesh.shape[name] == 2 for name in ("groups", "chan", "sub"))
        rows, channels = tokens.shape
        fits = channels == ways * LANES and rows % 64 == 0
        fits = fits and rows * ways == 8 * WIDE * RUN and rest[3].shape[0] % 512 == 0
        return (by_tokens if pairs and fits else general)(tokens, *rest)

    return jax.shard_map(
        shards,
        mesh=mesh,
        in_specs=(
            P(("groups", "seq", "sub"), "chan"),
            P("chan"),
            P(None, "chan"),
            P(None, "chan"),
            P(None, "chan"),
            P(None, "chan"),
            P(None, "chan"),
        ),
        out_specs=P(("groups", "seq", "sub"), "chan"),
        check_vma=False,
    )
```
